32 devices in a mesh: groups: 1, ffn: 32 (over z, y, x, core).
Axes of the slice: x: 2, y: 2, z: 4, core: 2. Of those that a mesh axis runs over, the one named last changes fastest.
Arguments:
- tokens: bfloat16 [256, 4096], P(('groups', 'ffn')), may hold values from -500 to 500
- norm_gain: float32 [4096], replicated, may hold values from 0.1 to 1.9
- routes: int32 [256, 8], P(('groups', 'ffn')), may hold values from 0 to 15, all different within a row; in each aligned block of 8 rows (0 to 7, 8 to 15, ...) at most 8 rows name the same one
- gate_scores: float32 [256, 8], P(('groups', 'ffn')), may hold values from 0.05 to 1
- w_gate: bfloat16 [4096, 12288], P(None, 'ffn'), may hold values from -0.09375 to 0.09375
- w_up: bfloat16 [4096, 12288], P(None, 'ffn'), may hold values from -0.09375 to 0.09375
- w_down: bfloat16 [12288, 4096], P('ffn'), may hold values from -0.21875 to 0.21875
- query: bfloat16 [8, 8192], P('groups'), may hold values from -17 to 17
- k_cache: bfloat16 [8, 4096, 512], P('groups', 'ffn'), may hold values from -4 to 4
- v_cache: bfloat16 [8, 4096, 512], P('groups', 'ffn'), may hold values from -4 to 4
- cache_len: int32 [8], P('groups'), may hold values from 256 to 4096, as said below
Outputs:
- combined: bfloat16 [256, 4096], P(('groups', 'ffn'))
- attention: bfloat16 [8, 8192], P('groups', 'ffn')
The draws below stay inside these ranges and needn't reach their ends.
Inputs may be any that keep to these rules, and one draw needn't show every extreme that they name: `routes`: within the 8 rows of one device no expert is named by more than 8 rows, a bound that some block reaches; a row names 8 different experts. A row uses its first cache_len positions; some row has exactly 4096.
All inputs are finite; a program needn't handle non-finite values.
Results may differ from the reference program's by a relative error of at most 0.012.
Values may be sent and summed in bfloat16 or wider, within the bound.
No kernel may reach another device: no remote copies, remote signals or barrier semaphores. Data moves between devices by JAX's collectives and lax.ppermute only.
A program may use at most 128 MiB of HBM per device.

```python
import math
import jax
import jax.numpy as jnp
import numpy as np
from jax import lax

D = 4096
HEADS = 64
KV_HEADS = 4
HEAD_DIM = 128
FF_WIN = 768
TOPK = 8
ROWS_DEV = 8
SEG = 128
ROWS_B = 8
EXPERTS = 16
CAP = 8
ROWS_A = 256
LEN = 4096
N_FFN = 32


def draw_tokens(key, part):
    key = jax.random.fold_in(key, 11)
    first_key, second_key, third_key = jax.random.split(key, 3)
    base_draw = jnp.clip(jax.random.normal(first_key, (ROWS_A, D), jnp.float32), -5.0, 5.0)
    row_scale = jnp.exp(jax.random.uniform(second_key, (ROWS_A, 1), jnp.float32, 0.0, math.log(10.0)))
    col_scale = jnp.exp(jax.random.uniform(third_key, (1, D), jnp.float32, 0.0, math.log(10.0)))
    return (base_draw * row_scale * col_scale).astype(jnp.bfloat16)


def draw_query(key, part):
    key = jax.random.fold_in(key, 21)
    third_key = jax.random.fold_in(key, 2)
    result = jnp.clip(2.5 * jax.random.normal(third_key, (ROWS_B, HEADS, HEAD_DIM), jnp.float32), -10.0, 10.0)
    return result.reshape(ROWS_B, HEADS * HEAD_DIM).astype(jnp.bfloat16)


def draw_k_cache(key, part):
    key = jax.random.fold_in(key, 31)
    result = jnp.clip(jax.random.normal(key, (ROWS_B, LEN, KV_HEADS * HEAD_DIM), jnp.float32), -4.0, 4.0)
    return result.astype(jnp.bfloat16)


def draw_cache_len(key, part):
    key = jax.random.fold_in(key, 41)
    first_key, second_key = jax.random.split(key, 2)
    lengths = jax.random.randint(first_key, (ROWS_B,), LEN // 16, LEN + 1, jnp.int32)
    longest = jax.random.randint(second_key, (), 0, ROWS_B, jnp.int32)
    return jnp.where(jnp.arange(ROWS_B, dtype=jnp.int32) == longest, LEN, lengths).astype(jnp.int32)


def level_of(stream_key, extent, cuts, least, top_value):
    gain, own = 1.0, jax.random.fold_in(stream_key, 6)
    for dim, blocks in cuts:
        steps = jnp.exp(jax.random.uniform(jax.random.fold_in(own, dim), (blocks,), jnp.float32, least / len(cuts), top_value / len(cuts)))
        gain = gain * jnp.repeat(steps, extent[dim] // blocks).reshape([-1 if axis == dim else 1 for axis in range(len(extent))])
    return gain


def assign_block(rng, own, number, rows, count, top, limit, slope):
    order = jax.random.permutation(rng, count)
    crowded, common = portions_of(count, rows * top, limit, slope, True), portions_of(count, rows * top, limit, slope, False)
    places = jnp.arange(count)

    def named(sizes, turn):
        used = int((sizes > 0).sum())
        fixed = max(1, used // 4)
        moved = fixed + (places - fixed + turn * (used - fixed)) % max(1, count - fixed)
        return jnp.zeros((count,), jnp.int32).at[order[jnp.where(places < fixed, places, moved)]].set(jnp.asarray(sizes, jnp.int32))

    sizes = jnp.where(number % 4 == 0, named(crowded, number // 4), named(common, number - number // 4 - 1))
    mixed = jax.random.permutation(jax.random.fold_in(own, 3), count)
    giver, taker = mixed[0:count // 2 * 2:2], mixed[1:count // 2 * 2:2]
    room = jnp.minimum(sizes[giver] - 1, limit - sizes[taker]) // 2
    room = jnp.where((giver == order[0]) | (taker == order[0]) | (sizes[taker] == 0), 0, jnp.maximum(room, 0))
    moved = jax.random.randint(jax.random.fold_in(own, 4), (count // 2,), 0, 1 << 20) % (room + 1)
    sizes = sizes.at[giver].add(-moved).at[taker].add(moved)
    items = jnp.searchsorted(jnp.cumsum(sizes), jnp.arange(rows * top), side="right").astype(jnp.int32)
    table = items.reshape(top, rows).T
    table = table[jax.random.permutation(jax.random.fold_in(own, 1), rows)]
    turn = jax.random.randint(jax.random.fold_in(own, 2), (rows, 1), 0, top)
    return jnp.take_along_axis(table, (jnp.arange(top)[None, :] + turn) % top, axis=1)


def portions_of(count, total, limit, lean, full):
    weights = [(1 << 20) // math.isqrt(rank ** lean) + 1 for rank in range(1, count + 1)]
    largest = limit if full else min(limit, max(-(-total // count), total * weights[0] // sum(weights)))
    least = 1 if total - largest >= count - 1 else 0
    counts, spare = [largest] + [least] * (count - 1), total - largest - least * (count - 1)
    while spare > 0:
        free = [i for i in range(1, count) if counts[i] < largest] or [i for i in range(1, count) if counts[i] < limit]
        mass, budget = sum([weights[i] for i in free]), spare
        for i in free:
            addition = min(limit - counts[i], max(1, budget * weights[i] // mass), spare)
            counts[i] = counts[i] + addition
            spare = spare - addition
    return np.array(counts)


def normal_values(own_key, dims, spread, limit, cuts=(), held_as=jnp.bfloat16):
    entries = jax.random.normal(own_key, dims, jnp.float32) * spread
    if len(cuts) > 0:
        entries = level_of(own_key, dims, cuts, -0.22, 0.18) * entries
    return jnp.clip(entries, min=-limit, max=limit).astype(held_as)


def setup_inputs(seed: int = 0, part: int = 0) -> dict:
    keys = jax.random.split(jax.random.key(seed), 12)
    own_keys = jax.random.split(jax.random.fold_in(keys[11], part), 12)
    tokens = draw_tokens(jax.random.fold_in(jax.random.fold_in(keys[11], part), 71), part)
    norm_gain = jnp.clip(1.0 + 0.18 * jax.random.normal(keys[1], (D,), jnp.float32), 0.1, 1.9)
    routes_keys = jax.random.split(jax.random.fold_in(own_keys[2], 1), ROWS_A // ROWS_DEV)
    routes_turns = jax.random.permutation(jax.random.fold_in(own_keys[2], 3), ROWS_A // ROWS_DEV)
    routes = jax.vmap(lambda own, number: assign_block(jax.random.fold_in(own_keys[2], 2), own, number, ROWS_DEV, EXPERTS, TOPK, CAP, 2))(routes_keys, routes_turns).reshape((ROWS_A, TOPK))
    gate_scores = jnp.clip(jnp.exp(math.log(1.0) - 2.9957323 * jax.random.uniform(own_keys[3], (ROWS_A, TOPK), jnp.float32) ** level_of(own_keys[3], (ROWS_A, TOPK), ((0, 32),), -0.2, 0.2)), 0.05, 1.0)
    w_gate = normal_values(keys[4], (D, EXPERTS * FF_WIN), D ** -0.5, 0.09375, ((1, 32),))
    w_up = normal_values(keys[5], (D, EXPERTS * FF_WIN), D ** -0.5, 0.09375, ((1, 32),))
    w_down = normal_values(keys[6], (EXPERTS * FF_WIN, D), FF_WIN ** -0.5, 0.21875, ((0, 32),))
    query = draw_query(jax.random.fold_in(jax.random.fold_in(keys[11], part), 71), part)
    k_cache = draw_k_cache(jax.random.fold_in(jax.random.fold_in(keys[11], part), 71), part)
    v_cache = normal_values(own_keys[9], (ROWS_B, LEN, KV_HEADS * HEAD_DIM), 1.0, 4.0, ((1, 32),))
    cache_len = draw_cache_len(jax.random.fold_in(jax.random.fold_in(keys[11], part), 71), part)
    return {"tokens": tokens, "norm_gain": norm_gain, "routes": routes, "gate_scores": gate_scores, "w_gate": w_gate, "w_up": w_up, "w_down": w_down, "query": query, "k_cache": k_cache, "v_cache": v_cache, "cache_len": cache_len}


def rms_normed(tokens, norm_gain):
    features = tokens.astype(jnp.float32)
    mean_square = lax.optimization_barrier(jnp.mean(features * features, axis=-1, keepdims=True))
    return (features * lax.rsqrt(mean_square + 1e-06) * norm_gain.astype(jnp.float32)).astype(jnp.bfloat16)

def slot_ranks(blocked, expert_count):
    one_hot = (blocked[..., None] == jnp.arange(expert_count, dtype=jnp.int32)).astype(jnp.int32)
    before = jnp.cumsum(one_hot, axis=-2) - one_hot
    return lax.optimization_barrier(jnp.sum(before * one_hot, axis=-1)).astype(jnp.int32)

def reference(tokens, norm_gain, routes, gate_scores, w_gate, w_up, w_down, query, k_cache, v_cache, cache_len):
    normed = rms_normed(tokens, norm_gain)
    gate_share = gate_scores / lax.optimization_barrier(jnp.sum(gate_scores, axis=-1, keepdims=True))
    blocked = routes.reshape(N_FFN, ROWS_DEV * TOPK).astype(jnp.int32)
    slot_rank = slot_ranks(blocked, EXPERTS)
    source = jnp.arange(N_FFN, dtype=jnp.int32)[:, None]
    position = ((blocked * N_FFN + source) * CAP + slot_rank).reshape(-1).astype(jnp.int32)
    row_index = jnp.arange(ROWS_A * TOPK, dtype=jnp.int32) // TOPK
    buffer = jnp.zeros((EXPERTS * N_FFN * CAP, D), jnp.bfloat16).at[position].set(normed[row_index])
    buffer = buffer.reshape(EXPERTS, N_FFN * CAP, D)

    def expert_output(expert_item):
        expert_index, slot_rows = expert_item
        first_col = expert_index * FF_WIN
        gate_cols = lax.dynamic_slice_in_dim(w_gate, first_col, FF_WIN, 1)
        up_cols = lax.dynamic_slice_in_dim(w_up, first_col, FF_WIN, 1)
        down_rows = lax.dynamic_slice_in_dim(w_down, first_col, FF_WIN, 0)
        gate_part = jnp.dot(slot_rows, gate_cols, preferred_element_type=jnp.float32)
        up_part = jnp.dot(slot_rows, up_cols, preferred_element_type=jnp.float32)
        hidden = (jax.nn.silu(gate_part) * up_part).astype(jnp.bfloat16)
        return jnp.dot(hidden, down_rows, preferred_element_type=jnp.float32).astype(jnp.bfloat16)
    expert_out = lax.map(expert_output, (jnp.arange(EXPERTS, dtype=jnp.int32), buffer))
    picked = expert_out.reshape(-1, D)[position].reshape(ROWS_A, TOPK, D)
    combined = lax.optimization_barrier(jnp.sum(picked.astype(jnp.float32) * gate_share[:, :, None], axis=1)).astype(jnp.bfloat16)
    per_group = HEADS // KV_HEADS
    queries = query.astype(jnp.float32).reshape(ROWS_B, KV_HEADS, per_group, HEAD_DIM)
    cache_keys = k_cache.astype(jnp.float32).reshape(ROWS_B, N_FFN, SEG, KV_HEADS, HEAD_DIM)
    cache_values = v_cache.astype(jnp.float32).reshape(ROWS_B, N_FFN, SEG, KV_HEADS, HEAD_DIM)
    scores = jnp.einsum('rgqd,rbsgd->rgqbs', queries, cache_keys) * HEAD_DIM ** (-0.5)
    positions = jnp.arange(LEN, dtype=jnp.int32).reshape(N_FFN, SEG)
    usable = (positions[None, :, :] < cache_len[:, None, None])[:, None, None, :, :]
    block_max = lax.optimization_barrier(jnp.max(jnp.where(usable, scores, -1e+30), axis=-1))
    weights = jnp.where(usable, jnp.exp(scores - block_max[..., None]), 0.0).astype(jnp.bfloat16)
    weights_wide = weights.astype(jnp.float32)
    block_sum = lax.optimization_barrier(jnp.sum(weights_wide, axis=-1))
    block_acc = jnp.einsum('rgqbs,rbsgd->rgqbd', weights_wide, cache_values)
    top_score = lax.optimization_barrier(jnp.max(block_max, axis=-1))
    factor = jnp.exp(block_max - top_score[..., None])
    weight_total = lax.optimization_barrier(jnp.sum(block_sum * factor, axis=-1))
    weighted = lax.optimization_barrier(jnp.sum(block_acc * factor[..., None], axis=-2))
    attention = (weighted / weight_total[..., None]).reshape(ROWS_B, HEADS * HEAD_DIM).astype(jnp.bfloat16)
    return (combined, attention)
```

```python
import functools

import jax
import jax.numpy as jnp
from jax import lax
from jax.experimental import pallas as pl
from jax.experimental.pallas import tpu as pltpu
from jax.sharding import PartitionSpec as P

HEADS = 64
KV_HEADS = 4
HEAD_DIM = 128
LANES = 128
VMEM = pl.BlockSpec(memory_space=pltpu.VMEM)
SMEM = pl.BlockSpec(memory_space=pltpu.SMEM)


def levels_of(devices):
    levels, stride = [], 2
    while stride < devices:
        radix = 4 if devices // stride >= 4 else 2
        levels.append((stride, radix))
        stride *= radix
    return levels


def exchange(value, distance):
    size = lax.axis_size("ffn")
    return lax.ppermute(value, "ffn", [(i, i ^ distance) for i in range(size)])


def call(body, out_shape, *args, in_specs=None, scratch=(), flops=0, nbytes=0):
    return pl.pallas_call(
        body,
        out_shape=out_shape,
        in_specs=in_specs or [VMEM] * len(args),
        out_specs=jax.tree.map(lambda _: VMEM, out_shape),
        scratch_shapes=list(scratch),
        compiler_params=pltpu.CompilerParams(vmem_limit_bytes=24 * 2**20),
        cost_estimate=pl.CostEstimate(flops=flops, bytes_accessed=nbytes, transcendentals=0),
    )(*args)


def payload_kernel(experts, tokens_ref, gain_ref, routes_ref, scores_ref, out_ref):
    features = tokens_ref[...].astype(jnp.float32)
    width = features.shape[1]
    mean_square = jnp.mean(features * features, axis=-1, keepdims=True)
    normed = features * lax.rsqrt(mean_square + 1e-06) * gain_ref[...]
    scores = scores_ref[...]
    share = scores / jnp.sum(scores, axis=-1, keepdims=True)
    extra = out_ref.shape[1] - width
    lane = lax.broadcasted_iota(jnp.int32, (features.shape[0], extra), 1)
    routes = routes_ref[...]
    gates = jnp.zeros(lane.shape, jnp.float32)
    for choice in range(routes.shape[1]):
        gates += jnp.where(
            routes[:, choice : choice + 1] == lane % experts, share[:, choice : choice + 1], 0.0
        )
    high = gates.astype(jnp.bfloat16).astype(jnp.float32)
    coded = jnp.where(lane < experts, high, jnp.where(lane < 2 * experts, gates - high, 0.0))
    out_ref[:, :width] = normed.astype(jnp.bfloat16)
    out_ref[:, width:] = coded.astype(jnp.bfloat16)


def expert_kernel(experts, expert_ref, same_ref, other_ref, gate_ref, up_ref, down_ref, own_ref, far_ref):
    width = gate_ref.shape[0]
    rows = same_ref.shape[0]
    stacked = jnp.concatenate([same_ref[:, :width], other_ref[:, :width]], axis=0)
    coded = jnp.concatenate([same_ref[:, width:], other_ref[:, width:]], axis=0).astype(jnp.float32)
    lane = lax.broadcasted_iota(jnp.int32, coded.shape, 1)
    mine = (lane < 2 * experts) & (lane % experts == expert_ref[0])
    share = jnp.sum(jnp.where(mine, coded, 0.0), axis=-1, keepdims=True)
    gate_part = jnp.dot(stacked, gate_ref[...], preferred_element_type=jnp.float32)
    up_part = jnp.dot(stacked, up_ref[...], preferred_element_type=jnp.float32)
    hidden = (gate_part / (1.0 + jnp.exp(-gate_part)) * up_part).astype(jnp.bfloat16)
    step = 1024
    for first in range(0, width, step):
        cols = slice(first, first + step)
        part = jnp.dot(hidden, down_ref[:, cols], preferred_element_type=jnp.float32)
        part = (part * share).astype(jnp.bfloat16)
        own_ref[:, cols] = part[:rows]
        far_ref[:, cols] = part[rows:]


def sum_kernel(count, *refs):
    total = refs[0][...].astype(jnp.float32)
    for ref in refs[1:count]:
        total += ref[...].astype(jnp.float32)
    outs = refs[count:]
    rows = total.shape[0] // len(outs)
    for place, out_ref in enumerate(outs):
        out_ref[...] = total[place * rows : (place + 1) * rows].astype(out_ref.dtype)


def summed(parts, pieces):
    rows, width = parts[0].shape
    shape = jax.ShapeDtypeStruct((rows // pieces, width), jnp.bfloat16)
    return call(
        functools.partial(sum_kernel, len(parts)),
        [shape] * pieces,
        *parts,
        flops=rows * width * len(parts),
        nbytes=2 * rows * width * (len(parts) + 1),
    )


def attend(query, k_cache, v_cache, cache_len):
    devices = lax.axis_size("ffn")
    rows, seg_len, kv_width = k_cache.shape
    info = jnp.concatenate([(lax.axis_index("ffn") * seg_len)[None], cache_len]).astype(jnp.int32)
    queries = query.reshape(rows, KV_HEADS, HEADS // KV_HEADS, HEAD_DIM)
    keys = k_cache.reshape(rows, seg_len, KV_HEADS, HEAD_DIM)
    values = v_cache.reshape(rows, seg_len, KV_HEADS, HEAD_DIM)
    scores = jnp.einsum(
        "rgqd,rsgd->rgqs", queries, keys, preferred_element_type=jnp.float32
    ) * HEAD_DIM ** (-0.5)
    positions = info[0] + jnp.arange(seg_len, dtype=jnp.int32)
    usable = (positions[None, :] < cache_len[:, None])[:, None, None, :]
    peak = jnp.max(jnp.where(usable, scores, -1e30), axis=-1)
    weights = jnp.where(usable, jnp.exp(scores - peak[..., None]), 0.0).astype(jnp.bfloat16)
    total = jnp.sum(weights.astype(jnp.float32), axis=-1)
    acc = jnp.einsum("rgqs,rsgd->rgqd", weights, values, preferred_element_type=jnp.float32)
    own = query.shape[1] // devices
    if own % HEAD_DIM:
        peak = jnp.repeat(peak.reshape(rows, HEADS), HEAD_DIM, axis=1).reshape(rows, devices, own)
        total = jnp.repeat(total.reshape(rows, HEADS), HEAD_DIM, axis=1).reshape(rows, devices, own)
        packed = jnp.concatenate([acc.reshape(rows, devices, own), peak[..., :1], total[..., :1]], axis=-1)
        heads = 1
    else:
        heads = own // HEAD_DIM
        packed = jnp.concatenate(
            [
                acc.reshape(rows, devices, own),
                peak.reshape(rows, devices, heads),
                total.reshape(rows, devices, heads),
            ],
            axis=-1,
        )
    packed = packed.transpose(1, 0, 2)
    arrived = lax.all_to_all(packed, "ffn", split_axis=0, concat_axis=0, tiled=True)
    acc = arrived[:, :, :own].reshape(devices, rows, heads, own // heads)
    peak = arrived[:, :, own : own + heads]
    total = arrived[:, :, own + heads :]
    top = jnp.max(peak, axis=0)
    factor = jnp.exp(peak - top[None])
    weight_total = jnp.sum(total * factor, axis=0)
    weighted = jnp.sum(acc * factor[..., None], axis=0)
    return (weighted / weight_total[..., None]).reshape(rows, own).astype(jnp.bfloat16)


def per_device(
    tokens, norm_gain, routes, gate_scores, w_gate, w_up, w_down, query, k_cache, v_cache, cache_len
):
    rows_dev, width = tokens.shape
    devices = lax.axis_size("ffn")
    experts = devices // 2
    levels = levels_of(devices)
    extra = -(-2 * experts // LANES) * LANES
    expert = (lax.axis_index("ffn") // 2).astype(jnp.int32)[None]

    block = call(
        functools.partial(payload_kernel, experts),
        jax.ShapeDtypeStruct((rows_dev, width + extra), jnp.bfloat16),
        tokens,
        norm_gain[None],
        routes,
        gate_scores,
    )
    for stride, radix in reversed(levels[1:]):
        arrived = [exchange(block, stride * k) for k in reversed(range(1, radix))]
        block = jnp.concatenate([block] + arrived[::-1], axis=0)
    stride, radix = levels[0]
    order = [3, 1, 2][-(radix - 1) :] if radix == 4 else [1]
    chunks = {k: exchange(block, stride * k) for k in order}
    chunks[0] = block

    rows = block.shape[0]
    hidden = w_gate.shape[1]
    partial = {}
    for k in [0] + order[1:] + order[:1]:
        other = exchange(chunks[k], 1)
        shape = jax.ShapeDtypeStruct((rows, width), jnp.bfloat16)
        own, far = call(
            functools.partial(expert_kernel, experts),
            [shape, shape],
            expert,
            chunks[k],
            other,
            w_gate,
            w_up,
            w_down,
            in_specs=[SMEM] + [VMEM] * 5,
            flops=2 * rows * width * hidden * 6,
            nbytes=2 * (3 * width * hidden + 4 * rows * width),
        )
        (partial[k],) = summed([own, exchange(far, 1)], 1)
    parts = [partial[0]] + [exchange(partial[k], stride * k) for k in range(1, radix)]
    for stride, radix in levels[1:]:
        pieces = summed(parts, radix)
        parts = [pieces[0]] + [exchange(pieces[k], stride * k) for k in range(1, radix)]
    (combined,) = summed(parts, 1)

    attention = attend(query, k_cache, v_cache, cache_len)
    return (combined, attention)


def solution(mesh):
    in_specs = (
        P(("groups", "ffn"), None),
        P(),
        P(("groups", "ffn"), None),
        P(("groups", "ffn"), None),
        P(None, "ffn"),
        P(None, "ffn"),
        P("ffn", None),
        P("groups", None),
        P("groups", "ffn", None),
        P("groups", "ffn", None),
        P("groups"),
    )
    out_specs = (P(("groups", "ffn"), None), P("groups", "ffn"))
    return jax.shard_map(
        per_device, mesh=mesh, in_specs=in_specs, out_specs=out_specs, check_vma=False
    )
```

```python
import functools

import jax
import jax.numpy as jnp
from jax import lax
from jax.experimental import pallas as pl
from jax.experimental.pallas import tpu as pltpu
from jax.sharding import PartitionSpec as P

HEADS = 64
KV_HEADS = 4
HEAD_DIM = 128
LANES = 128
VMEM = pl.BlockSpec(memory_space=pltpu.VMEM)
SMEM = pl.BlockSpec(memory_space=pltpu.SMEM)
HBM = pl.BlockSpec(memory_space=pltpu.HBM)


def levels_of(devices):
    levels, stride = [], 2
    while stride < devices:
        radix = 4 if devices // stride >= 4 else 2
        levels.append((stride, radix))
        stride *= radix
    return levels


def offsets_of(levels):
    offsets = [0]
    for stride, radix in reversed(levels):
        offsets = [stride * k ^ low for k in range(radix) for low in offsets]
    return offsets


def exchange(value, distance):
    size = lax.axis_size("ffn")
    return lax.ppermute(value, "ffn", [(i, i ^ distance) for i in range(size)])


def after(value, *others):
    return lax.optimization_barrier((value, *others))[0]


def call(body, out_shape, args, in_specs=None, scratch=(), flops=0, nbytes=0, mib=16):
    return pl.pallas_call(
        body,
        out_shape=out_shape,
        in_specs=in_specs or [VMEM] * len(args),
        out_specs=jax.tree.map(lambda _: VMEM, out_shape),
        scratch_shapes=list(scratch),
        compiler_params=pltpu.CompilerParams(vmem_limit_bytes=mib * 2**20),
        cost_estimate=pl.CostEstimate(flops=flops, bytes_accessed=nbytes, transcendentals=0),
    )(*args)


def in_hbm(*arrays):
    return [pltpu.with_memory_space_constraint(array, pltpu.HBM) for array in arrays]


def fetched(count):
    return pltpu.SemaphoreType.DMA((count,))


def fetch(sources, targets, sems):
    copies = [pltpu.make_async_copy(s, t, sems.at[i]) for i, (s, t) in enumerate(zip(sources, targets))]
    for copy in copies:
        copy.start()
    return copies


def payload_kernel(
    experts, tokens_hbm, gain_hbm, routes_hbm, scores_hbm, out_ref, tokens_ref, gain_ref, routes_ref, scores_ref, sems
):
    copies = fetch(
        [tokens_hbm, gain_hbm, routes_hbm, scores_hbm], [tokens_ref, gain_ref, routes_ref, scores_ref], sems
    )
    for copy in copies:
        copy.wait()
    features = tokens_ref[...].astype(jnp.float32)
    width = features.shape[1]
    mean_square = jnp.mean(features * features, axis=-1, keepdims=True)
    normed = features * lax.rsqrt(mean_square + 1e-06) * gain_ref[...]
    scores = scores_ref[...]
    share = scores / jnp.sum(scores, axis=-1, keepdims=True)
    extra = out_ref.shape[1] - width
    lane = lax.broadcasted_iota(jnp.int32, (features.shape[0], extra), 1)
    routes = routes_ref[...]
    gates = jnp.zeros(lane.shape, jnp.float32)
    for choice in range(routes.shape[1]):
        gates += jnp.where(
            routes[:, choice : choice + 1] == lane % experts, share[:, choice : choice + 1], 0.0
        )
    high = gates.astype(jnp.bfloat16).astype(jnp.float32)
    coded = jnp.where(lane < experts, high, jnp.where(lane < 2 * experts, gates - high, 0.0))
    out_ref[:, :width] = normed.astype(jnp.bfloat16)
    out_ref[:, width:] = coded.astype(jnp.bfloat16)


def coded_log(value):
    high = value.astype(jnp.bfloat16).astype(jnp.float32)
    middle = (value - high).astype(jnp.bfloat16).astype(jnp.float32)
    return [high, middle, value - high - middle]


def attention_kernel(
    own, offsets, info_ref, query_hbm, key_hbm, value_hbm, near_ref, far_ref, query_ref, key_ref, value_ref, dest_ref, sems
):
    copies = fetch([query_hbm, key_hbm, value_hbm], [query_ref, key_ref, value_ref], sems)
    rows, seg_len, _ = key_ref.shape
    per_group = HEADS // KV_HEADS
    shape = (per_group * rows, rows * seg_len)
    row_of = lax.broadcasted_iota(jnp.int32, shape, 0) % rows
    key_at = lax.broadcasted_iota(jnp.int32, shape, 1)
    limit = jnp.full((1, rows * seg_len), 0, jnp.int32)
    lane_row = lax.broadcasted_iota(jnp.int32, limit.shape, 1) // seg_len
    for row in range(rows):
        limit = jnp.where(lane_row == row, info_ref[2 + row] + row * seg_len - info_ref[1], limit)
    usable = (row_of == key_at // seg_len) & (key_at < limit)
    per_dest = max(1, own // HEAD_DIM)
    extra = near_ref.shape[1]
    lane = lax.broadcasted_iota(jnp.int32, (rows, extra), 1)
    for copy in copies:
        copy.wait()
    for group in range(KV_HEADS):
        cols = slice(group * HEAD_DIM, (group + 1) * HEAD_DIM)
        keys = key_ref[:, :, cols].reshape(rows * seg_len, HEAD_DIM)
        values = value_ref[:, :, cols].reshape(rows * seg_len, HEAD_DIM)
        scores = lax.dot_general(
            query_ref[group * per_group * rows : (group + 1) * per_group * rows],
            keys,
            (((1,), (1,)), ((), ())),
            preferred_element_type=jnp.float32,
        ) * HEAD_DIM ** (-0.5)
        peak = jnp.max(jnp.where(usable, scores, -1e30), axis=-1, keepdims=True)
        weights = jnp.where(usable, jnp.exp(scores - peak), 0.0).astype(jnp.bfloat16)
        total = jnp.sum(weights.astype(jnp.float32), axis=-1, keepdims=True)
        acc = jnp.dot(weights, values, preferred_element_type=jnp.float32)
        some = total > 0.0
        safe = jnp.where(some, total, 1.0)
        mean = acc / safe
        logs = jnp.where(some, peak + jnp.log(safe), -1e30)
        if own >= HEAD_DIM:
            for first in range(0, per_group, per_dest):
                dest = (group * per_group + first) // per_dest
                stats = jnp.zeros(lane.shape, jnp.float32)
                for slot in range(per_dest):
                    at = slice((first + slot) * rows, (first + slot + 1) * rows)
                    dest_ref[dest, :, slot * HEAD_DIM : (slot + 1) * HEAD_DIM] = mean[at]
                    for place, part in enumerate(coded_log(logs[at])):
                        stats = jnp.where(lane == own + 3 * slot + place, part, stats)
                dest_ref[dest, :, own:] = stats[:, own:]
        else:
            for head in range(per_group):
                at = slice(head * rows, (head + 1) * rows)
                for half in range(HEAD_DIM // own):
                    dest = (group * per_group + head) * (HEAD_DIM // own) + half
                    block = jnp.zeros(lane.shape, jnp.float32)
                    moved = mean[at] if half == 0 else pltpu.roll(mean[at], HEAD_DIM - half * own, 1)
                    block = jnp.where(lane < own, moved, block)
                    for place, part in enumerate(coded_log(logs[at])):
                        block = jnp.where(lane == own + place, part, block)
                    dest_ref[dest] = block
    for out_ref, core in ((near_ref, 0), (far_ref, 1)):
        for place in range(0, len(offsets), 2):
            pair = [dest_ref[info_ref[0] ^ (offset ^ core)] for offset in offsets[place : place + 2]]
            out_ref[place * rows : (place + 2) * rows] = jnp.concatenate(pair, axis=0).astype(jnp.bfloat16)


def attend(query, k_cache, v_cache, cache_len, levels):
    devices = lax.axis_size("ffn")
    rows, seg_len, _ = k_cache.shape
    own = query.shape[1] // devices
    extra = -(-(own + 3 * max(1, own // HEAD_DIM)) // LANES) * LANES
    me = lax.axis_index("ffn").astype(jnp.int32)
    info = jnp.concatenate([me[None], (me * seg_len)[None], cache_len])
    stacked = query.reshape(rows, HEADS, HEAD_DIM).transpose(1, 0, 2).reshape(HEADS * rows, HEAD_DIM)
    offsets = offsets_of(levels)
    out = jax.ShapeDtypeStruct((len(offsets) * rows, extra), jnp.bfloat16)
    return call(
        functools.partial(attention_kernel, own, offsets),
        [out, out],
        [info, *in_hbm(stacked, k_cache, v_cache)],
        in_specs=[SMEM, HBM, HBM, HBM],
        scratch=[
            pltpu.VMEM(stacked.shape, stacked.dtype),
            pltpu.VMEM(k_cache.shape, k_cache.dtype),
            pltpu.VMEM(v_cache.shape, v_cache.dtype),
            pltpu.VMEM((devices, rows, extra), jnp.float32),
            fetched(3),
        ],
        flops=4 * query.size * seg_len * rows,
        nbytes=2 * (k_cache.size + v_cache.size + query.size),
    )


def expert_kernel(experts, chunks, expert_ref, *refs):
    count = len(chunks)
    same_refs, other_refs, refs = refs[:count], refs[count : 2 * count], refs[2 * count :]
    near_ref, far_ref, gate_hbm, up_hbm, down_hbm, own_out, far_out, gate_ref, up_ref, down_ref, sems = refs
    width, hidden_size = gate_ref.shape
    rows = same_refs[0].shape[0]
    cuts = sems.shape[0] // 3
    depth = width // cuts
    sources, targets = [], []
    for cut in range(cuts):
        at = pl.ds(cut * depth, depth)
        sources += [gate_hbm.at[at], up_hbm.at[at]]
        targets += [gate_ref.at[at], up_ref.at[at]]
    for cut in range(cuts):
        at = pl.ds(cut * depth, depth)
        sources.append(down_hbm.at[:, at])
        targets.append(down_ref.at[:, at])
    copies = fetch(sources, targets, sems)
    coded = jnp.concatenate([r[:, width:] for r in same_refs + other_refs], axis=0).astype(jnp.float32)
    lane = lax.broadcasted_iota(jnp.int32, coded.shape, 1)
    mine = (lane < 2 * experts) & (lane % experts == expert_ref[0])
    share = jnp.sum(jnp.where(mine, coded, 0.0), axis=-1, keepdims=True)
    for place, chunk in enumerate(chunks):
        at, here = slice(place * rows, (place + 1) * rows), slice(chunk * rows, (chunk + 1) * rows)
        own_out[at, width:] = near_ref[here]
        far_out[at, width:] = far_ref[here]
    gate_part = jnp.zeros((coded.shape[0], hidden_size), jnp.float32)
    up_part = gate_part
    for cut in range(cuts):
        at = slice(cut * depth, (cut + 1) * depth)
        stacked = jnp.concatenate([r[:, at] for r in same_refs + other_refs], axis=0)
        copies[2 * cut].wait()
        gate_part += jnp.dot(stacked, gate_ref[at], preferred_element_type=jnp.float32)
        copies[2 * cut + 1].wait()
        up_part += jnp.dot(stacked, up_ref[at], preferred_element_type=jnp.float32)
    hidden = (gate_part / (1.0 + jnp.exp(-gate_part)) * up_part).astype(jnp.bfloat16)
    for cut in range(cuts):
        at = slice(cut * depth, (cut + 1) * depth)
        copies[2 * cuts + cut].wait()
        part = jnp.dot(hidden, down_ref[:, at], preferred_element_type=jnp.float32)
        part = (part * share).astype(jnp.bfloat16)
        own_out[:, at] = part[: count * rows]
        far_out[:, at] = part[count * rows :]


def apply_expert(expert, same, other, chunks, sums, weights):
    rows = same[0].shape[0]
    width, hidden = weights[0].shape
    devices = lax.axis_size("ffn")
    shape = jax.ShapeDtypeStruct((len(chunks) * rows, width + sums[0].shape[1]), jnp.bfloat16)
    return call(
        functools.partial(expert_kernel, devices // 2, chunks),
        [shape, shape],
        [expert, *same, *other, *sums, *weights],
        in_specs=[SMEM] + [VMEM] * (2 * len(chunks) + 2) + [HBM] * 3,
        scratch=[pltpu.VMEM(w.shape, w.dtype) for w in weights] + [fetched(12)],
        flops=4 * len(chunks) * rows * width * hidden * 3,
        nbytes=2 * (3 * width * hidden + 4 * len(chunks) * rows * width),
        mib=32,
    )


def merged(own, parts):
    heads, piece = max(1, own // HEAD_DIM), min(own, HEAD_DIM)
    lane = lax.broadcasted_iota(jnp.int32, parts[0].shape, 1)
    result = jnp.zeros(parts[0].shape, jnp.float32)
    for head in range(heads):
        stat = (lane >= own + 3 * head) & (lane < own + 3 * head + 3)
        logs = [jnp.sum(jnp.where(stat, p, 0.0), axis=-1, keepdims=True) for p in parts]
        top = functools.reduce(jnp.maximum, logs)
        scales = [jnp.exp(log - top) for log in logs]
        total = sum(scales)
        mean = sum(p * s for p, s in zip(parts, scales)) / total
        result = jnp.where((lane >= head * piece) & (lane < (head + 1) * piece), mean, result)
        for place, part in enumerate(coded_log(top + jnp.log(total))):
            result = jnp.where(lane == own + 3 * head + place, part, result)
    return result


def sum_kernel(count, width, own, last, *refs):
    refs, outs = refs[:count], refs[count:]
    rows = outs[0].shape[0]
    pieces = 1 if last else len(outs)
    for place in range(pieces):
        at = slice(place * rows, (place + 1) * rows)
        total = sum(ref[at, :width].astype(jnp.float32) for ref in refs)
        mean = merged(own, [ref[at, width:].astype(jnp.float32) for ref in refs])
        if last:
            outs[0][...] = total.astype(jnp.bfloat16)
            outs[1][...] = mean[:, :own].astype(jnp.bfloat16)
        else:
            outs[place][:, :width] = total.astype(jnp.bfloat16)
            outs[place][:, width:] = mean.astype(jnp.bfloat16)


def summed(parts, pieces, width, own, last=False):
    rows, whole = parts[0].shape
    if last:
        shapes = [jax.ShapeDtypeStruct((rows, n), jnp.bfloat16) for n in (width, own)]
    else:
        shapes = [jax.ShapeDtypeStruct((rows // pieces, whole), jnp.bfloat16)] * pieces
    return call(
        functools.partial(sum_kernel, len(parts), width, own, last),
        shapes,
        parts,
        flops=rows * whole * len(parts),
        nbytes=2 * rows * whole * (len(parts) + 1),
    )


def per_device(
    tokens, norm_gain, routes, gate_scores, w_gate, w_up, w_down, query, k_cache, v_cache, cache_len
):
    rows_dev, width = tokens.shape
    devices = lax.axis_size("ffn")
    experts = devices // 2
    levels = levels_of(devices)
    own = query.shape[1] // devices
    extra = -(-2 * experts // LANES) * LANES
    expert = (lax.axis_index("ffn") // 2).astype(jnp.int32)[None]
    weights = in_hbm(w_gate, w_up, w_down)

    gain = norm_gain[None]
    block = call(
        functools.partial(payload_kernel, experts),
        jax.ShapeDtypeStruct((rows_dev, width + extra), jnp.bfloat16),
        in_hbm(tokens, gain, routes, gate_scores),
        in_specs=[HBM] * 4,
        scratch=[pltpu.VMEM(a.shape, a.dtype) for a in (tokens, gain, routes, gate_scores)] + [fetched(4)],
    )
    for stride, radix in reversed(levels[1:]):
        arrived = [exchange(block, stride * k) for k in reversed(range(1, radix))]
        block = jnp.concatenate([block] + arrived[::-1], axis=0)
    sums = attend(query, k_cache, v_cache, cache_len, levels)

    stride, radix = levels[0]
    chunks = {0: block}
    for k in range(1, min(radix, 3)):
        chunks[k] = exchange(block, stride * k)
    near, far = apply_expert(expert, [block], [exchange(block, 1)], [0], sums, weights)
    for k in range(3, radix):
        chunks[k] = exchange(after(block, near), stride * k)
    (total,) = summed([near, exchange(far, 1)], 1, width, own)
    parts = [total]
    done = near
    for group in ([1, 2], [3]) if radix == 4 else ([1],):
        same = [after(chunks[k], done) for k in group]
        near, far = apply_expert(expert, same, [exchange(s, 1) for s in same], group, sums, weights)
        pieces = summed([near, exchange(far, 1)], len(group), width, own)
        parts += [exchange(piece, stride * k) for piece, k in zip(pieces, group)]
        done = near
    for stride, radix in levels[1:]:
        pieces = summed(parts, radix, width, own)
        parts = [pieces[0]] + [exchange(pieces[k], stride * k) for k in range(1, radix)]
    return tuple(summed(parts, 1, width, own, last=True))


def solution(mesh):
    in_specs = (
        P(("groups", "ffn"), None),
        P(),
        P(("groups", "ffn"), None),
        P(("groups", "ffn"), None),
        P(None, "ffn"),
        P(None, "ffn"),
        P("ffn", None),
        P("groups", None),
        P("groups", "ffn", None),
        P("groups", "ffn", None),
        P("groups"),
    )
    out_specs = (P(("groups", "ffn"), None), P("groups", "ffn"))
    return jax.shard_map(
        per_device, mesh=mesh, in_specs=in_specs, out_specs=out_specs, check_vma=False
    )
```

```python
import functools

import jax
import jax.numpy as jnp
from jax import lax
from jax.experimental import pallas as pl
from jax.experimental.pallas import tpu as pltpu
from jax.sharding import PartitionSpec as P

HEADS = 64
KV_HEADS = 4
HEAD_DIM = 128
LANES = 128
VMEM = pl.BlockSpec(memory_space=pltpu.VMEM)
SMEM = pl.BlockSpec(memory_space=pltpu.SMEM)
HBM = pl.BlockSpec(memory_space=pltpu.HBM)


def levels_of(devices):
    levels, stride = [], 2
    while stride < devices:
        radix = 4 if devices // stride >= 4 else 2
        levels.append((stride, radix))
        stride *= radix
    return levels


def offsets_of(levels):
    offsets = [0]
    for stride, radix in reversed(levels):
        offsets = [stride * k ^ low for k in range(radix) for low in offsets]
    return offsets


def exchange(value, distance):
    size = lax.axis_size("ffn")
    return lax.ppermute(value, "ffn", [(i, i ^ distance) for i in range(size)])


def after(value, *others):
    return lax.optimization_barrier((value, *others))[0]


def call(body, out_shape, args, in_specs=None, scratch=(), flops=1, nbytes=1, mib=16):
    return pl.pallas_call(
        body,
        out_shape=out_shape,
        in_specs=in_specs or [VMEM] * len(args),
        out_specs=jax.tree.map(lambda _: VMEM, out_shape),
        scratch_shapes=list(scratch),
        compiler_params=pltpu.CompilerParams(vmem_limit_bytes=mib * 2**20),
        cost_estimate=pl.CostEstimate(flops=flops, bytes_accessed=nbytes, transcendentals=0),
    )(*args)


def in_hbm(*arrays):
    return [pltpu.with_memory_space_constraint(array, pltpu.HBM) for array in arrays]


def fetched(count):
    return pltpu.SemaphoreType.DMA((count,))


def fetch(sources, targets, sems):
    copies = [pltpu.make_async_copy(s, t, sems.at[i]) for i, (s, t) in enumerate(zip(sources, targets))]
    for copy in copies:
        copy.start()
    return copies


def payload_kernel(
    experts, tokens_hbm, gain_hbm, routes_hbm, scores_hbm, out_ref, tokens_ref, gain_ref, routes_ref, scores_ref, sems
):
    copies = fetch(
        [tokens_hbm, gain_hbm, routes_hbm, scores_hbm], [tokens_ref, gain_ref, routes_ref, scores_ref], sems
    )
    for copy in copies:
        copy.wait()
    features = tokens_ref[...].astype(jnp.float32)
    width = features.shape[1]
    mean_square = jnp.mean(features * features, axis=-1, keepdims=True)
    normed = features * lax.rsqrt(mean_square + 1e-06) * gain_ref[...]
    scores = scores_ref[...]
    share = scores / jnp.sum(scores, axis=-1, keepdims=True)
    extra = out_ref.shape[1] - width
    lane = lax.broadcasted_iota(jnp.int32, (features.shape[0], extra), 1)
    routes = routes_ref[...]
    gates = jnp.zeros(lane.shape, jnp.float32)
    for choice in range(routes.shape[1]):
        gates += jnp.where(
            routes[:, choice : choice + 1] == lane % experts, share[:, choice : choice + 1], 0.0
        )
    high = gates.astype(jnp.bfloat16).astype(jnp.float32)
    coded = jnp.where(lane < experts, high, jnp.where(lane < 2 * experts, gates - high, 0.0))
    out_ref[:, :width] = normed.astype(jnp.bfloat16)
    out_ref[:, width:] = coded.astype(jnp.bfloat16)


def coded_log(value):
    high = value.astype(jnp.bfloat16).astype(jnp.float32)
    middle = (value - high).astype(jnp.bfloat16).astype(jnp.float32)
    return [high, middle, value - high - middle]


def attention_kernel(
    own, offsets, length_ref, *refs
):
    query_hbm, key_hbm, value_hbm, gate_hbm, up_hbm, near_ref, far_ref, gate_out, up_out = refs[:9]
    query_ref, key_ref, value_ref, dest_ref, sems = refs[9:]
    sources = [query_hbm, key_hbm, value_hbm, gate_hbm, up_hbm]
    copies = fetch(sources, [query_ref, key_ref, value_ref, gate_out, up_out], sems)
    me = lax.axis_index("ffn")
    rows, seg_len, _ = key_ref.shape
    per_group = HEADS // KV_HEADS
    shape = (per_group * rows, rows * seg_len)
    row_of = lax.broadcasted_iota(jnp.int32, shape, 0) % rows
    key_at = lax.broadcasted_iota(jnp.int32, shape, 1)
    limit = jnp.full((1, rows * seg_len), 0, jnp.int32)
    lane_row = lax.broadcasted_iota(jnp.int32, limit.shape, 1) // seg_len
    for row in range(rows):
        limit = jnp.where(lane_row == row, length_ref[row] + row * seg_len - me * seg_len, limit)
    usable = (row_of == key_at // seg_len) & (key_at < limit)
    per_dest = max(1, own // HEAD_DIM)
    extra = near_ref.shape[1]
    lane = lax.broadcasted_iota(jnp.int32, (rows, extra), 1)
    for copy in copies[:3]:
        copy.wait()
    for group in range(KV_HEADS):
        cols = slice(group * HEAD_DIM, (group + 1) * HEAD_DIM)
        keys = key_ref[:, :, cols].reshape(rows * seg_len, HEAD_DIM)
        values = value_ref[:, :, cols].reshape(rows * seg_len, HEAD_DIM)
        scores = lax.dot_general(
            query_ref[group * per_group * rows : (group + 1) * per_group * rows],
            keys,
            (((1,), (1,)), ((), ())),
            preferred_element_type=jnp.float32,
        ) * HEAD_DIM ** (-0.5)
        peak = jnp.max(jnp.where(usable, scores, -1e30), axis=-1, keepdims=True)
        weights = jnp.where(usable, jnp.exp(scores - peak), 0.0).astype(jnp.bfloat16)
        total = jnp.sum(weights.astype(jnp.float32), axis=-1, keepdims=True)
        acc = jnp.dot(weights, values, preferred_element_type=jnp.float32)
        some = total > 0.0
        safe = jnp.where(some, total, 1.0)
        mean = acc / safe
        logs = jnp.where(some, peak + jnp.log(safe), -1e30)
        if own >= HEAD_DIM:
            for first in range(0, per_group, per_dest):
                dest = (group * per_group + first) // per_dest
                stats = jnp.zeros(lane.shape, jnp.float32)
                for slot in range(per_dest):
                    at = slice((first + slot) * rows, (first + slot + 1) * rows)
                    dest_ref[dest, :, slot * HEAD_DIM : (slot + 1) * HEAD_DIM] = mean[at]
                    for place, part in enumerate(coded_log(logs[at])):
                        stats = jnp.where(lane == own + 3 * slot + place, part, stats)
                dest_ref[dest, :, own:] = stats[:, own:]
        else:
            for head in range(per_group):
                at = slice(head * rows, (head + 1) * rows)
                for half in range(HEAD_DIM // own):
                    dest = (group * per_group + head) * (HEAD_DIM // own) + half
                    block = jnp.zeros(lane.shape, jnp.float32)
                    moved = mean[at] if half == 0 else pltpu.roll(mean[at], HEAD_DIM - half * own, 1)
                    block = jnp.where(lane < own, moved, block)
                    for place, part in enumerate(coded_log(logs[at])):
                        block = jnp.where(lane == own + place, part, block)
                    dest_ref[dest] = block
    for out_ref, core in ((near_ref, 0), (far_ref, 1)):
        for place in range(0, len(offsets), 2):
            pair = [dest_ref[me ^ (offset ^ core)] for offset in offsets[place : place + 2]]
            out_ref[place * rows : (place + 2) * rows] = jnp.concatenate(pair, axis=0).astype(jnp.bfloat16)
    for copy in copies[3:]:
        copy.wait()


def attend(query, k_cache, v_cache, cache_len, levels, weights):
    devices = lax.axis_size("ffn")
    rows, seg_len, _ = k_cache.shape
    own = query.shape[1] // devices
    extra = -(-(own + 3 * max(1, own // HEAD_DIM)) // LANES) * LANES
    stacked = query.reshape(rows, HEADS, HEAD_DIM).transpose(1, 0, 2).reshape(HEADS * rows, HEAD_DIM)
    offsets = offsets_of(levels)
    out = jax.ShapeDtypeStruct((len(offsets) * rows, extra), jnp.bfloat16)
    return call(
        functools.partial(attention_kernel, own, offsets),
        [out, out] + [pltpu.VMEM(w.shape, w.dtype) for w in weights],
        [cache_len, *in_hbm(stacked, k_cache, v_cache, *weights)],
        in_specs=[SMEM] + [HBM] * 5,
        scratch=[
            pltpu.VMEM(stacked.shape, stacked.dtype),
            pltpu.VMEM(k_cache.shape, k_cache.dtype),
            pltpu.VMEM(v_cache.shape, v_cache.dtype),
            pltpu.VMEM((devices, rows, extra), jnp.float32),
            fetched(5),
        ],
        flops=10**9,
        nbytes=2 * sum(w.size for w in weights),
    )


def expert_kernel(experts, count, *refs):
    same_refs, other_refs, refs = refs[:count], refs[count : 2 * count], refs[2 * count :]
    near_ref, far_ref, gate_ref, up_ref, down_hbm, own_out, far_out, down_ref, sems = refs
    width = gate_ref.shape[0]
    rows = same_refs[0].shape[0]
    step = width // sems.shape[0]
    cuts = [pl.ds(first, step) for first in range(0, width, step)]
    copies = fetch([down_hbm.at[:, at] for at in cuts], [down_ref.at[:, at] for at in cuts], sems)
    coded = jnp.concatenate([r[:, width:] for r in same_refs + other_refs], axis=0).astype(jnp.float32)
    lane = lax.broadcasted_iota(jnp.int32, coded.shape, 1)
    mine = (lane < 2 * experts) & (lane % experts == lax.axis_index("ffn") // 2)
    share = jnp.sum(jnp.where(mine, coded, 0.0), axis=-1, keepdims=True)
    own_out[:, width:] = near_ref[...]
    far_out[:, width:] = far_ref[...]
    stacked = jnp.concatenate([r[:, :width] for r in same_refs + other_refs], axis=0)
    gate_part = jnp.dot(stacked, gate_ref[...], preferred_element_type=jnp.float32)
    up_part = jnp.dot(stacked, up_ref[...], preferred_element_type=jnp.float32)
    hidden = (gate_part / (1.0 + jnp.exp(-gate_part)) * up_part).astype(jnp.bfloat16)
    for copy, at in zip(copies, cuts):
        copy.wait()
        part = jnp.dot(hidden, down_ref[:, at], preferred_element_type=jnp.float32)
        part = (part * share).astype(jnp.bfloat16)
        own_out[:, at] = part[: count * rows]
        far_out[:, at] = part[count * rows :]


def apply_expert(same, sums, weights):
    rows = same[0].shape[0]
    width, hidden = weights[0].shape
    devices = lax.axis_size("ffn")
    shape = jax.ShapeDtypeStruct((len(same) * rows, width + sums[0].shape[1]), jnp.bfloat16)
    args = [*same, *[exchange(s, 1) for s in same], *sums, *weights[:2], *in_hbm(weights[2])]
    return call(
        functools.partial(expert_kernel, devices // 2, len(same)),
        [shape, shape],
        args,
        in_specs=[VMEM] * (2 * len(same) + 4) + [HBM],
        scratch=[pltpu.VMEM(weights[2].shape, weights[2].dtype), fetched(4)],
        flops=4 * len(same) * rows * width * hidden * 3,
        nbytes=2 * 3 * width * hidden,
        mib=8 + sum(2 * a.size for a in args) // 2**20,
    )


def merged(own, parts):
    heads, piece = max(1, own // HEAD_DIM), min(own, HEAD_DIM)
    lane = lax.broadcasted_iota(jnp.int32, parts[0].shape, 1)
    result = jnp.zeros(parts[0].shape, jnp.float32)
    for head in range(heads):
        stat = (lane >= own + 3 * head) & (lane < own + 3 * head + 3)
        logs = [jnp.sum(jnp.where(stat, p, 0.0), axis=-1, keepdims=True) for p in parts]
        top = functools.reduce(jnp.maximum, logs)
        scales = [jnp.exp(log - top) for log in logs]
        total = sum(scales)
        mean = sum(p * s for p, s in zip(parts, scales)) / total
        result = jnp.where((lane >= head * piece) & (lane < (head + 1) * piece), mean, result)
        for place, part in enumerate(coded_log(top + jnp.log(total))):
            result = jnp.where(lane == own + 3 * head + place, part, result)
    return result


def sum_kernel(count, width, own, last, *refs):
    refs, outs = refs[:count], refs[count:]
    first = 0
    for out_ref in outs[:1] if last else outs:
        rows = out_ref.shape[0]
        at = slice(first, first + rows)
        first += rows
        total = sum(ref[at, :width].astype(jnp.float32) for ref in refs)
        mean = merged(own, [ref[at, width:].astype(jnp.float32) for ref in refs])
        if last:
            outs[0][...] = total.astype(jnp.bfloat16)
            outs[1][...] = mean[:, :own].astype(jnp.bfloat16)
        else:
            out_ref[:, :width] = total.astype(jnp.bfloat16)
            out_ref[:, width:] = mean.astype(jnp.bfloat16)


def summed(parts, sizes, width, own, last=False):
    rows, whole = parts[0].shape
    if last:
        shapes = [jax.ShapeDtypeStruct((rows, n), jnp.bfloat16) for n in (width, own)]
    else:
        shapes = [jax.ShapeDtypeStruct((n, whole), jnp.bfloat16) for n in sizes]
    return call(functools.partial(sum_kernel, len(parts), width, own, last), shapes, parts)


def stack_kernel(*refs):
    stacked = jnp.concatenate([ref[...].astype(jnp.float32) for ref in refs[:-1]], axis=0)
    refs[-1][...] = stacked.astype(jnp.bfloat16)


def stack(parts):
    rows, width = parts[0].shape
    return call(stack_kernel, jax.ShapeDtypeStruct((len(parts) * rows, width), jnp.bfloat16), parts)


def gather(block, levels, *ready):
    for stride, radix in reversed(levels):
        arrived = {k: exchange(block, stride * k) for k in reversed(range(1, radix))}
        block = stack([block] + [after(arrived[k], *ready) for k in range(1, radix)])
    return block


def scatter(pieces, levels, width, own):
    stride, radix = levels[0]
    parts = [pieces[0]] + [exchange(pieces[k], stride * k) for k in range(1, radix)]
    if len(levels) == 1:
        return parts
    rows = parts[0].shape[0] // levels[1][1]
    return scatter(summed(parts, [rows] * levels[1][1], width, own), levels[1:], width, own)


def per_device(
    tokens, norm_gain, routes, gate_scores, w_gate, w_up, w_down, query, k_cache, v_cache, cache_len
):
    rows_dev, width = tokens.shape
    devices = lax.axis_size("ffn")
    experts = devices // 2
    levels = levels_of(devices)
    own = query.shape[1] // devices
    extra = -(-2 * experts // LANES) * LANES
    block = call(
        functools.partial(payload_kernel, experts),
        jax.ShapeDtypeStruct((rows_dev, width + extra), jnp.bfloat16),
        in_hbm(tokens, norm_gain[None], routes, gate_scores),
        in_specs=[HBM] * 4,
        scratch=[pltpu.VMEM(a.shape, a.dtype) for a in (tokens, norm_gain[None], routes, gate_scores)]
        + [fetched(4)],
    )
    *sums, w_gate, w_up = attend(query, k_cache, v_cache, cache_len, levels, (w_gate, w_up))
    (stride, radix), *outer = levels
    corner = 3 * stride
    chunks, ready = {}, [sums[0]]
    if radix == 4:
        across = exchange(block, corner)
        ready.append(across)
        chunks[3] = gather(across, outer)
    chunks[0] = gather(block, outer, *ready)
    for k in range(1, min(radix, 3)):
        chunks[k] = exchange(chunks[0], stride * k)
    rows = chunks[0].shape[0]
    cut = [rows // outer[0][1]] * outer[0][1]
    near, far = apply_expert([chunks[k] for k in range(radix)], sums, (w_gate, w_up, w_down))
    sizes = [rows] * min(radix, 3) + (cut if radix == 4 else [])
    pieces = summed([near, exchange(far, 1)], sizes, width, own)
    parts = [pieces[0]] + [exchange(pieces[k], stride * k) for k in range(1, min(radix, 3))]
    if radix == 4:
        corner_parts = scatter(pieces[3:], outer, width, own)
    last = scatter(summed(parts, cut, width, own), outer, width, own)
    if radix == 4:
        (corner_sum,) = summed(corner_parts, [rows_dev], width, own)
        last.append(exchange(corner_sum, corner))
    return tuple(summed(last, [], width, own, last=True))


def solution(mesh):
    in_specs = (
        P(("groups", "ffn"), None),
        P(),
        P(("groups", "ffn"), None),
        P(("groups", "ffn"), None),
        P(None, "ffn"),
        P(None, "ffn"),
        P("ffn", None),
        P("groups", None),
        P("groups", "ffn", None),
        P("groups", "ffn", None),
        P("groups"),
    )
    out_specs = (P(("groups", "ffn"), None), P("groups", "ffn"))
    return jax.shard_map(
        per_device, mesh=mesh, in_specs=in_specs, out_specs=out_specs, check_vma=False
    )
```

```python
import functools

import jax
import jax.numpy as jnp
from jax import lax
from jax.experimental import pallas as pl
from jax.experimental.pallas import tpu as pltpu
from jax.sharding import PartitionSpec as P

HEADS = 64
KV_HEADS = 4
HEAD_DIM = 128
LANES = 128
VMEM = pl.BlockSpec(memory_space=pltpu.VMEM)
SMEM = pl.BlockSpec(memory_space=pltpu.SMEM)
HBM = pl.BlockSpec(memory_space=pltpu.HBM)


def levels_of(devices):
    levels, stride = [], 2
    while stride < devices:
        radix = 4 if devices // stride >= 4 else 2
        levels.append((stride, radix))
        stride *= radix
    return levels


def offsets_of(levels):
    offsets = [0]
    for stride, radix in reversed(levels):
        offsets = [stride * k ^ low for k in range(radix) for low in offsets]
    return offsets


def exchange(value, distance):
    size = lax.axis_size("ffn")
    return lax.ppermute(value, "ffn", [(i, i ^ distance) for i in range(size)])


def after(value, *others):
    return lax.optimization_barrier((value, *others))[0]


def call(body, out_shape, args, in_specs=None, scratch=(), flops=1, nbytes=1, mib=16):
    return pl.pallas_call(
        body,
        out_shape=out_shape,
        in_specs=in_specs or [VMEM] * len(args),
        out_specs=jax.tree.map(lambda _: VMEM, out_shape),
        scratch_shapes=list(scratch),
        compiler_params=pltpu.CompilerParams(vmem_limit_bytes=mib * 2**20),
        cost_estimate=pl.CostEstimate(flops=flops, bytes_accessed=nbytes, transcendentals=0),
    )(*args)


def in_hbm(*arrays):
    return [pltpu.with_memory_space_constraint(array, pltpu.HBM) for array in arrays]


def fetched(count):
    return pltpu.SemaphoreType.DMA((count,))


def fetch(sources, targets, sems):
    copies = [pltpu.make_async_copy(s, t, sems.at[i]) for i, (s, t) in enumerate(zip(sources, targets))]
    for copy in copies:
        copy.start()
    return copies


def payload_kernel(
    experts, tokens_hbm, gain_hbm, routes_hbm, scores_hbm, out_ref, tokens_ref, gain_ref, routes_ref, scores_ref, sems
):
    copies = fetch(
        [tokens_hbm, gain_hbm, routes_hbm, scores_hbm], [tokens_ref, gain_ref, routes_ref, scores_ref], sems
    )
    for copy in copies:
        copy.wait()
    features = tokens_ref[...].astype(jnp.float32)
    width = features.shape[1]
    mean_square = jnp.mean(features * features, axis=-1, keepdims=True)
    normed = features * lax.rsqrt(mean_square + 1e-06) * gain_ref[...]
    scores = scores_ref[...]
    share = scores / jnp.sum(scores, axis=-1, keepdims=True)
    extra = out_ref.shape[1] - width
    lane = lax.broadcasted_iota(jnp.int32, (features.shape[0], extra), 1)
    routes = routes_ref[...]
    gates = jnp.zeros(lane.shape, jnp.float32)
    for choice in range(routes.shape[1]):
        gates += jnp.where(
            routes[:, choice : choice + 1] == lane % experts, share[:, choice : choice + 1], 0.0
        )
    high = gates.astype(jnp.bfloat16).astype(jnp.float32)
    coded = jnp.where(lane < experts, high, jnp.where(lane < 2 * experts, gates - high, 0.0))
    out_ref[:, :width] = normed.astype(jnp.bfloat16)
    out_ref[:, width:] = coded.astype(jnp.bfloat16)


def coded_log(value):
    high = value.astype(jnp.bfloat16).astype(jnp.float32)
    middle = (value - high).astype(jnp.bfloat16).astype(jnp.float32)
    return [high, middle, value - high - middle]


def attention_kernel(
    own, offsets, length_ref, *refs
):
    query_hbm, key_hbm, value_hbm, gate_hbm, up_hbm, near_ref, far_ref, gate_out, up_out = refs[:9]
    query_ref, key_ref, value_ref, dest_ref, sems = refs[9:]
    sources = [query_hbm, key_hbm, value_hbm, gate_hbm, up_hbm]
    copies = fetch(sources, [query_ref, key_ref, value_ref, gate_out, up_out], sems)
    me = lax.axis_index("ffn")
    rows, seg_len, _ = key_ref.shape
    per_group = HEADS // KV_HEADS
    shape = (per_group * rows, rows * seg_len)
    row_of = lax.broadcasted_iota(jnp.int32, shape, 0) % rows
    key_at = lax.broadcasted_iota(jnp.int32, shape, 1)
    limit = jnp.full((1, rows * seg_len), 0, jnp.int32)
    lane_row = lax.broadcasted_iota(jnp.int32, limit.shape, 1) // seg_len
    for row in range(rows):
        limit = jnp.where(lane_row == row, length_ref[row] + row * seg_len - me * seg_len, limit)
    usable = (row_of == key_at // seg_len) & (key_at < limit)
    per_dest = max(1, own // HEAD_DIM)
    extra = near_ref.shape[1]
    lane = lax.broadcasted_iota(jnp.int32, (rows, extra), 1)
    for copy in copies[:3]:
        copy.wait()
    for group in range(KV_HEADS):
        cols = slice(group * HEAD_DIM, (group + 1) * HEAD_DIM)
        keys = key_ref[:, :, cols].reshape(rows * seg_len, HEAD_DIM)
        values = value_ref[:, :, cols].reshape(rows * seg_len, HEAD_DIM)
        scores = lax.dot_general(
            query_ref[group * per_group * rows : (group + 1) * per_group * rows],
            keys,
            (((1,), (1,)), ((), ())),
            preferred_element_type=jnp.float32,
        ) * HEAD_DIM ** (-0.5)
        peak = jnp.max(jnp.where(usable, scores, -1e30), axis=-1, keepdims=True)
        weights = jnp.where(usable, jnp.exp(scores - peak), 0.0).astype(jnp.bfloat16)
        total = jnp.sum(weights.astype(jnp.float32), axis=-1, keepdims=True)
        acc = jnp.dot(weights, values, preferred_element_type=jnp.float32)
        some = total > 0.0
        safe = jnp.where(some, total, 1.0)
        mean = acc / safe
        logs = jnp.where(some, peak + jnp.log(safe), -1e30)
        if own >= HEAD_DIM:
            for first in range(0, per_group, per_dest):
                dest = (group * per_group + first) // per_dest
                stats = jnp.zeros(lane.shape, jnp.float32)
                for slot in range(per_dest):
                    at = slice((first + slot) * rows, (first + slot + 1) * rows)
                    dest_ref[dest, :, slot * HEAD_DIM : (slot + 1) * HEAD_DIM] = mean[at]
                    for place, part in enumerate(coded_log(logs[at])):
                        stats = jnp.where(lane == own + 3 * slot + place, part, stats)
                dest_ref[dest, :, own:] = stats[:, own:]
        else:
            for head in range(per_group):
                at = slice(head * rows, (head + 1) * rows)
                for half in range(HEAD_DIM // own):
                    dest = (group * per_group + head) * (HEAD_DIM // own) + half
                    block = jnp.zeros(lane.shape, jnp.float32)
                    moved = mean[at] if half == 0 else pltpu.roll(mean[at], HEAD_DIM - half * own, 1)
                    block = jnp.where(lane < own, moved, block)
                    for place, part in enumerate(coded_log(logs[at])):
                        block = jnp.where(lane == own + place, part, block)
                    dest_ref[dest] = block
    for out_ref, core in ((near_ref, 0), (far_ref, 1)):
        for place in range(0, len(offsets), 2):
            pair = [dest_ref[me ^ (offset ^ core)] for offset in offsets[place : place + 2]]
            out_ref[place * rows : (place + 2) * rows] = jnp.concatenate(pair, axis=0).astype(jnp.bfloat16)
    for copy in copies[3:]:
        copy.wait()


def attend(query, k_cache, v_cache, cache_len, levels, weights):
    devices = lax.axis_size("ffn")
    rows, seg_len, _ = k_cache.shape
    own = query.shape[1] // devices
    extra = -(-(own + 3 * max(1, own // HEAD_DIM)) // LANES) * LANES
    stacked = query.reshape(rows, HEADS, HEAD_DIM).transpose(1, 0, 2).reshape(HEADS * rows, HEAD_DIM)
    offsets = offsets_of(levels)
    out = jax.ShapeDtypeStruct((len(offsets) * rows, extra), jnp.bfloat16)
    return call(
        functools.partial(attention_kernel, own, offsets),
        [out, out] + [pltpu.VMEM(w.shape, w.dtype) for w in weights],
        [cache_len, *in_hbm(stacked, k_cache, v_cache, *weights)],
        in_specs=[SMEM] + [HBM] * 5,
        scratch=[
            pltpu.VMEM(stacked.shape, stacked.dtype),
            pltpu.VMEM(k_cache.shape, k_cache.dtype),
            pltpu.VMEM(v_cache.shape, v_cache.dtype),
            pltpu.VMEM((devices, rows, extra), jnp.float32),
            fetched(5),
        ],
        flops=4 * 10**9,
        nbytes=2 * sum(w.size for w in weights),
    )


def expert_kernel(experts, chunks, load, *refs):
    count = len(chunks)
    same_refs, other_refs, refs = refs[:count], refs[count : 2 * count], refs[2 * count :]
    near_ref, far_ref, gate_ref, up_ref, down_ref, own_out, far_out = refs[:7]
    width = gate_ref.shape[0]
    rows = same_refs[0].shape[0]
    step = 1024
    cuts = [pl.ds(first, step) for first in range(0, width, step)]
    copies = [None] * len(cuts)
    if load:
        down_hbm, down_ref, sems = down_ref, refs[7], refs[8]
        copies = fetch([down_hbm.at[:, at] for at in cuts], [down_ref.at[:, at] for at in cuts], sems)
    coded = jnp.concatenate([r[:, width:] for r in same_refs + other_refs], axis=0).astype(jnp.float32)
    lane = lax.broadcasted_iota(jnp.int32, coded.shape, 1)
    mine = (lane < 2 * experts) & (lane % experts == lax.axis_index("ffn") // 2)
    share = jnp.sum(jnp.where(mine, coded, 0.0), axis=-1, keepdims=True)
    for place, chunk in enumerate(chunks):
        at, here = slice(place * rows, (place + 1) * rows), slice(chunk * rows, (chunk + 1) * rows)
        own_out[at, width:] = near_ref[here]
        far_out[at, width:] = far_ref[here]
    stacked = jnp.concatenate([r[:, :width] for r in same_refs + other_refs], axis=0)
    gate_part = jnp.dot(stacked, gate_ref[...], preferred_element_type=jnp.float32)
    up_part = jnp.dot(stacked, up_ref[...], preferred_element_type=jnp.float32)
    hidden = (gate_part / (1.0 + jnp.exp(-gate_part)) * up_part).astype(jnp.bfloat16)
    for copy, at in zip(copies, cuts):
        if load:
            copy.wait()
        part = jnp.dot(hidden, down_ref[:, at], preferred_element_type=jnp.float32)
        part = (part * share).astype(jnp.bfloat16)
        own_out[:, at] = part[: count * rows]
        far_out[:, at] = part[count * rows :]


def apply_expert(same, chunks, sums, weights, load=False):
    rows = same[0].shape[0]
    width, hidden = weights[0].shape
    devices = lax.axis_size("ffn")
    outs = [jax.ShapeDtypeStruct((len(same) * rows, width + sums[0].shape[1]), jnp.bfloat16)] * 2
    args = [*same, *[exchange(s, 1) for s in same], *sums, *weights]
    in_specs, scratch = [VMEM] * len(args), []
    if load:
        args[-1:], in_specs[-1] = in_hbm(args[-1]), HBM
        outs.append(pltpu.VMEM(weights[2].shape, weights[2].dtype))
        scratch.append(fetched(width // 1024))
    return call(
        functools.partial(expert_kernel, devices // 2, chunks, load),
        outs,
        args,
        in_specs=in_specs,
        scratch=scratch,
        flops=4 * 10**9,
        nbytes=2 * 3 * width * hidden,
        mib=8 + sum(2 * a.size for a in args) // 2**20,
    )


def merged(own, parts):
    heads, piece = max(1, own // HEAD_DIM), min(own, HEAD_DIM)
    lane = lax.broadcasted_iota(jnp.int32, parts[0].shape, 1)
    result = jnp.zeros(parts[0].shape, jnp.float32)
    for head in range(heads):
        stat = (lane >= own + 3 * head) & (lane < own + 3 * head + 3)
        logs = [jnp.sum(jnp.where(stat, p, 0.0), axis=-1, keepdims=True) for p in parts]
        top = functools.reduce(jnp.maximum, logs)
        scales = [jnp.exp(log - top) for log in logs]
        total = sum(scales)
        mean = sum(p * s for p, s in zip(parts, scales)) / total
        result = jnp.where((lane >= head * piece) & (lane < (head + 1) * piece), mean, result)
        for place, part in enumerate(coded_log(top + jnp.log(total))):
            result = jnp.where(lane == own + 3 * head + place, part, result)
    return result


def sum_kernel(count, width, own, last, *refs):
    refs, outs = refs[:count], refs[count:]
    first = 0
    for out_ref in outs[:1] if last else outs:
        rows = out_ref.shape[0]
        at = slice(first, first + rows)
        first += rows
        total = sum(ref[at, :width].astype(jnp.float32) for ref in refs)
        mean = merged(own, [ref[at, width:].astype(jnp.float32) for ref in refs])
        if last:
            outs[0][...] = total.astype(jnp.bfloat16)
            outs[1][...] = mean[:, :own].astype(jnp.bfloat16)
        else:
            out_ref[:, :width] = total.astype(jnp.bfloat16)
            out_ref[:, width:] = mean.astype(jnp.bfloat16)


def summed(parts, sizes, width, own, last=False):
    rows, whole = parts[0].shape
    if last:
        shapes = [jax.ShapeDtypeStruct((rows, n), jnp.bfloat16) for n in (width, own)]
    else:
        shapes = [jax.ShapeDtypeStruct((n, whole), jnp.bfloat16) for n in sizes]
    return call(functools.partial(sum_kernel, len(parts), width, own, last), shapes, parts)


def stack_kernel(*refs):
    stacked = jnp.concatenate([ref[...].astype(jnp.float32) for ref in refs[:-1]], axis=0)
    refs[-1][...] = stacked.astype(jnp.bfloat16)


def stack(parts):
    rows, width = parts[0].shape
    return call(stack_kernel, jax.ShapeDtypeStruct((len(parts) * rows, width), jnp.bfloat16), parts)


def start_order(radix):
    return [2, 3, 1] if radix == 4 else [1]


def gather(block, levels, *ready):
    for stride, radix in reversed(levels):
        arrived = {k: exchange(block, stride * k) for k in start_order(radix)}
        block = stack([block] + [after(arrived[k], *ready) for k in range(1, radix)])
    return block


def scatter(pieces, levels, width, own):
    stride, radix = levels[0]
    parts = [pieces[0]] + [exchange(pieces[k], stride * k) for k in start_order(radix)]
    if len(levels) == 1:
        return parts
    rows = parts[0].shape[0] // levels[1][1]
    return scatter(summed(parts, [rows] * levels[1][1], width, own), levels[1:], width, own)


def per_device(
    tokens, norm_gain, routes, gate_scores, w_gate, w_up, w_down, query, k_cache, v_cache, cache_len
):
    rows_dev, width = tokens.shape
    devices = lax.axis_size("ffn")
    experts = devices // 2
    levels = levels_of(devices)
    own = query.shape[1] // devices
    extra = -(-2 * experts // LANES) * LANES
    block = call(
        functools.partial(payload_kernel, experts),
        jax.ShapeDtypeStruct((rows_dev, width + extra), jnp.bfloat16),
        in_hbm(tokens, norm_gain[None], routes, gate_scores),
        in_specs=[HBM] * 4,
        scratch=[pltpu.VMEM(a.shape, a.dtype) for a in (tokens, norm_gain[None], routes, gate_scores)]
        + [fetched(4)],
    )
    *sums, w_gate, w_up = attend(query, k_cache, v_cache, cache_len, levels, (w_gate, w_up))
    (stride, radix), *outer = levels
    corner = 3 * stride
    weights = (w_gate, w_up, w_down)
    rows = rows_dev * (devices // (2 * radix))
    cut = [rows // outer[0][1]] * outer[0][1]
    across = [exchange(block, corner)] if radix == 4 else []
    base = gather(block, outer, sums[0], *across)
    sides = [1, 2] if radix == 4 else [1]
    chunks = [exchange(base, stride * k) for k in sides]

    near, far, w_down = apply_expert([base], [0], sums, weights, load=True)
    weights = (w_gate, w_up, w_down)
    ready = [near]
    if across:
        last_chunk = gather(across[0], outer, near)
        ready.append(last_chunk)
    chunks = [after(chunk, *ready) for chunk in chunks]
    own_near, own_far = near, far
    near, far = apply_expert(chunks, sides, sums, weights)
    own_far = after(own_far, near)
    if across:
        corner_near, corner_far = apply_expert([last_chunk], [3], sums, weights)
    (total,) = summed([own_near, exchange(own_far, 1)], [rows], width, own)
    pieces = summed([near, exchange(far, 1)], [rows] * len(sides), width, own)
    parts = [total] + [exchange(piece, stride * k) for piece, k in zip(pieces, sides)]
    if across:
        corner_pieces = summed([corner_near, exchange(corner_far, 1)], cut, width, own)
        corner_parts = scatter(corner_pieces, outer, width, own)
    pieces = summed(parts, cut, width, own)
    last = scatter(pieces, outer, width, own)
    if across:
        corner_parts = [after(part, pieces[0]) for part in corner_parts]
        (corner_sum,) = summed(corner_parts, [rows_dev], width, own)
        last.append(exchange(corner_sum, corner))
    return tuple(summed(last, [], width, own, last=True))


def solution(mesh):
    in_specs = (
        P(("groups", "ffn"), None),
        P(),
        P(("groups", "ffn"), None),
        P(("groups", "ffn"), None),
        P(None, "ffn"),
        P(None, "ffn"),
        P("ffn", None),
        P("groups", None),
        P("groups", "ffn", None),
        P("groups", "ffn", None),
        P("groups"),
    )
    out_specs = (P(("groups", "ffn"), None), P("groups", "ffn"))
    return jax.shard_map(
        per_device, mesh=mesh, in_specs=in_specs, out_specs=out_specs, check_vma=False
    )
```

```python
import functools

import jax
import jax.numpy as jnp
from jax import lax
from jax.experimental import pallas as pl
from jax.experimental.pallas import tpu as pltpu
from jax.sharding import PartitionSpec as P

HEADS = 64
KV_HEADS = 4
HEAD_DIM = 128
LANES = 128
VMEM = pl.BlockSpec(memory_space=pltpu.VMEM)
SMEM = pl.BlockSpec(memory_space=pltpu.SMEM)
HBM = pl.BlockSpec(memory_space=pltpu.HBM)


def levels_of(devices):
    levels, stride = [], 2
    while stride < devices:
        radix = 4 if devices // stride >= 4 else 2
        levels.append((stride, radix))
        stride *= radix
    return levels


def offsets_of(levels):
    offsets = [0]
    for stride, radix in reversed(levels):
        offsets = [stride * k ^ low for k in range(radix) for low in offsets]
    return offsets


def exchange(value, distance):
    size = lax.axis_size("ffn")
    return lax.ppermute(value, "ffn", [(i, i ^ distance) for i in range(size)])


def after(value, *others):
    return lax.optimization_barrier((value, *others))[0]


def call(body, out_shape, args, in_specs=None, scratch=(), flops=1, nbytes=1, mib=16):
    return pl.pallas_call(
        body,
        out_shape=out_shape,
        in_specs=in_specs or [VMEM] * len(args),
        out_specs=jax.tree.map(lambda _: VMEM, out_shape),
        scratch_shapes=list(scratch),
        compiler_params=pltpu.CompilerParams(vmem_limit_bytes=mib * 2**20),
        cost_estimate=pl.CostEstimate(flops=flops, bytes_accessed=nbytes, transcendentals=0),
    )(*args)


def in_hbm(*arrays):
    return [pltpu.with_memory_space_constraint(array, pltpu.HBM) for array in arrays]


def fetched(count):
    return pltpu.SemaphoreType.DMA((count,))


def fetch(sources, targets, sems):
    copies = [pltpu.make_async_copy(s, t, sems.at[i]) for i, (s, t) in enumerate(zip(sources, targets))]
    for copy in copies:
        copy.start()
    return copies


def payload_kernel(
    experts, tokens_hbm, gain_hbm, routes_hbm, scores_hbm, out_ref, tokens_ref, gain_ref, routes_ref, scores_ref, sems
):
    copies = fetch(
        [tokens_hbm, gain_hbm, routes_hbm, scores_hbm], [tokens_ref, gain_ref, routes_ref, scores_ref], sems
    )
    for copy in copies:
        copy.wait()
    features = tokens_ref[...].astype(jnp.float32)
    width = features.shape[1]
    mean_square = jnp.mean(features * features, axis=-1, keepdims=True)
    normed = features * lax.rsqrt(mean_square + 1e-06) * gain_ref[...]
    scores = scores_ref[...]
    share = scores / jnp.sum(scores, axis=-1, keepdims=True)
    extra = out_ref.shape[1] - width
    lane = lax.broadcasted_iota(jnp.int32, (features.shape[0], extra), 1)
    routes = routes_ref[...]
    gates = jnp.zeros(lane.shape, jnp.float32)
    for choice in range(routes.shape[1]):
        gates += jnp.where(
            routes[:, choice : choice + 1] == lane % experts, share[:, choice : choice + 1], 0.0
        )
    high = gates.astype(jnp.bfloat16).astype(jnp.float32)
    coded = jnp.where(lane < experts, high, jnp.where(lane < 2 * experts, gates - high, 0.0))
    out_ref[:, :width] = normed.astype(jnp.bfloat16)
    out_ref[:, width:] = coded.astype(jnp.bfloat16)


def coded_log(value):
    high = value.astype(jnp.bfloat16).astype(jnp.float32)
    middle = (value - high).astype(jnp.bfloat16).astype(jnp.float32)
    return [high, middle, value - high - middle]


def keep_kernel(count, *refs):
    copies = fetch(refs[:count], refs[count : 2 * count], refs[2 * count])
    for copy in copies:
        copy.wait()


def keep(*arrays):
    return call(
        functools.partial(keep_kernel, len(arrays)),
        [pltpu.VMEM(a.shape, a.dtype) for a in arrays],
        in_hbm(*arrays),
        in_specs=[HBM] * len(arrays),
        scratch=[fetched(len(arrays))],
        flops=4 * 10**9,
    )


def attention_kernel(
    own, offsets, length_hbm, query_hbm, key_hbm, value_hbm, near_ref, far_ref, *scratch
):
    length_ref, query_ref, key_ref, value_ref, dest_ref, sems = scratch
    sources = [length_hbm, query_hbm, key_hbm, value_hbm]
    copies = fetch(sources, [length_ref, query_ref, key_ref, value_ref], sems)
    copies[0].wait()
    me = lax.axis_index("ffn")
    rows, seg_len, _ = key_ref.shape
    per_group = HEADS // KV_HEADS
    shape = (per_group * rows, rows * seg_len)
    row_of = lax.broadcasted_iota(jnp.int32, shape, 0) % rows
    key_at = lax.broadcasted_iota(jnp.int32, shape, 1)
    limit = jnp.full((1, rows * seg_len), 0, jnp.int32)
    lane_row = lax.broadcasted_iota(jnp.int32, limit.shape, 1) // seg_len
    for row in range(rows):
        limit = jnp.where(lane_row == row, length_ref[row] + row * seg_len - me * seg_len, limit)
    usable = (row_of == key_at // seg_len) & (key_at < limit)
    per_dest = max(1, own // HEAD_DIM)
    extra = near_ref.shape[1]
    lane = lax.broadcasted_iota(jnp.int32, (rows, extra), 1)
    for copy in copies[1:]:
        copy.wait()
    for group in range(KV_HEADS):
        cols = slice(group * HEAD_DIM, (group + 1) * HEAD_DIM)
        keys = key_ref[:, :, cols].reshape(rows * seg_len, HEAD_DIM)
        values = value_ref[:, :, cols].reshape(rows * seg_len, HEAD_DIM)
        scores = lax.dot_general(
            query_ref[group * per_group * rows : (group + 1) * per_group * rows],
            keys,
            (((1,), (1,)), ((), ())),
            preferred_element_type=jnp.float32,
        ) * HEAD_DIM ** (-0.5)
        peak = jnp.max(jnp.where(usable, scores, -1e30), axis=-1, keepdims=True)
        weights = jnp.where(usable, jnp.exp(scores - peak), 0.0).astype(jnp.bfloat16)
        total = jnp.sum(weights.astype(jnp.float32), axis=-1, keepdims=True)
        acc = jnp.dot(weights, values, preferred_element_type=jnp.float32)
        some = total > 0.0
        safe = jnp.where(some, total, 1.0)
        mean = acc / safe
        logs = jnp.where(some, peak + jnp.log(safe), -1e30)
        if own >= HEAD_DIM:
            for first in range(0, per_group, per_dest):
                dest = (group * per_group + first) // per_dest
                stats = jnp.zeros(lane.shape, jnp.float32)
                for slot in range(per_dest):
                    at = slice((first + slot) * rows, (first + slot + 1) * rows)
                    dest_ref[dest, :, slot * HEAD_DIM : (slot + 1) * HEAD_DIM] = mean[at]
                    for place, part in enumerate(coded_log(logs[at])):
                        stats = jnp.where(lane == own + 3 * slot + place, part, stats)
                dest_ref[dest, :, own:] = stats[:, own:]
        else:
            for head in range(per_group):
                at = slice(head * rows, (head + 1) * rows)
                for half in range(HEAD_DIM // own):
                    dest = (group * per_group + head) * (HEAD_DIM // own) + half
                    block = jnp.zeros(lane.shape, jnp.float32)
                    moved = mean[at] if half == 0 else pltpu.roll(mean[at], HEAD_DIM - half * own, 1)
                    block = jnp.where(lane < own, moved, block)
                    for place, part in enumerate(coded_log(logs[at])):
                        block = jnp.where(lane == own + place, part, block)
                    dest_ref[dest] = block
    for out_ref, core in ((near_ref, 0), (far_ref, 1)):
        for place in range(0, len(offsets), 2):
            pair = [dest_ref[me ^ (offset ^ core)] for offset in offsets[place : place + 2]]
            out_ref[place * rows : (place + 2) * rows] = jnp.concatenate(pair, axis=0).astype(jnp.bfloat16)


def attend(query, k_cache, v_cache, cache_len, levels):
    devices = lax.axis_size("ffn")
    rows, seg_len, _ = k_cache.shape
    own = query.shape[1] // devices
    extra = -(-(own + 3 * max(1, own // HEAD_DIM)) // LANES) * LANES
    stacked = query.reshape(rows, HEADS, HEAD_DIM).transpose(1, 0, 2).reshape(HEADS * rows, HEAD_DIM)
    offsets = offsets_of(levels)
    out = jax.ShapeDtypeStruct((len(offsets) * rows, extra), jnp.bfloat16)
    return call(
        functools.partial(attention_kernel, own, offsets),
        [out, out],
        in_hbm(cache_len, stacked, k_cache, v_cache),
        in_specs=[HBM] * 4,
        scratch=[
            pltpu.SMEM(cache_len.shape, cache_len.dtype),
            pltpu.VMEM(stacked.shape, stacked.dtype),
            pltpu.VMEM(k_cache.shape, k_cache.dtype),
            pltpu.VMEM(v_cache.shape, v_cache.dtype),
            pltpu.VMEM((devices, rows, extra), jnp.float32),
            fetched(4),
        ],
        flops=4 * 10**9,
    )


def expert_kernel(experts, chunks, *refs):
    count = len(chunks)
    same_refs, other_refs, refs = refs[:count], refs[count : 2 * count], refs[2 * count :]
    near_ref, far_ref, gate_ref, up_ref, down_ref, own_out, far_out = refs
    width = gate_ref.shape[0]
    rows = same_refs[0].shape[0]
    coded = jnp.concatenate([r[:, width:] for r in same_refs + other_refs], axis=0).astype(jnp.float32)
    lane = lax.broadcasted_iota(jnp.int32, coded.shape, 1)
    mine = (lane < 2 * experts) & (lane % experts == lax.axis_index("ffn") // 2)
    share = jnp.sum(jnp.where(mine, coded, 0.0), axis=-1, keepdims=True)
    for place, chunk in enumerate(chunks):
        at, here = slice(place * rows, (place + 1) * rows), slice(chunk * rows, (chunk + 1) * rows)
        own_out[at, width:] = near_ref[here]
        far_out[at, width:] = far_ref[here]
    stacked = jnp.concatenate([r[:, :width] for r in same_refs + other_refs], axis=0)
    gate_part = jnp.dot(stacked, gate_ref[...], preferred_element_type=jnp.float32)
    up_part = jnp.dot(stacked, up_ref[...], preferred_element_type=jnp.float32)
    hidden = (gate_part / (1.0 + jnp.exp(-gate_part)) * up_part).astype(jnp.bfloat16)
    step = 1024
    for first in range(0, width, step):
        at = slice(first, first + step)
        part = jnp.dot(hidden, down_ref[:, at], preferred_element_type=jnp.float32)
        part = (part * share).astype(jnp.bfloat16)
        own_out[:, at] = part[: count * rows]
        far_out[:, at] = part[count * rows :]


def apply_expert(same, other, chunks, sums, weights):
    rows = same[0].shape[0]
    width, hidden = weights[0].shape
    devices = lax.axis_size("ffn")
    shape = jax.ShapeDtypeStruct((len(same) * rows, width + sums[0].shape[1]), jnp.bfloat16)
    args = [*same, *other, *sums, *weights]
    return call(
        functools.partial(expert_kernel, devices // 2, chunks),
        [shape, shape],
        args,
        flops=4 * 10**9,
        nbytes=2 * 3 * width * hidden,
        mib=8 + sum(2 * a.size for a in args) // 2**20,
    )


def merged(own, parts):
    heads, piece = max(1, own // HEAD_DIM), min(own, HEAD_DIM)
    lane = lax.broadcasted_iota(jnp.int32, parts[0].shape, 1)
    result = jnp.zeros(parts[0].shape, jnp.float32)
    for head in range(heads):
        stat = (lane >= own + 3 * head) & (lane < own + 3 * head + 3)
        logs = [jnp.sum(jnp.where(stat, p, 0.0), axis=-1, keepdims=True) for p in parts]
        top = functools.reduce(jnp.maximum, logs)
        scales = [jnp.exp(log - top) for log in logs]
        total = sum(scales)
        mean = sum(p * s for p, s in zip(parts, scales)) / total
        result = jnp.where((lane >= head * piece) & (lane < (head + 1) * piece), mean, result)
        for place, part in enumerate(coded_log(top + jnp.log(total))):
            result = jnp.where(lane == own + 3 * head + place, part, result)
    return result


def sum_kernel(count, width, own, last, *refs):
    refs, outs = refs[:count], refs[count:]
    first = 0
    for out_ref in outs[:1] if last else outs:
        rows = out_ref.shape[0]
        at = slice(first, first + rows)
        first += rows
        total = sum(ref[at, :width].astype(jnp.float32) for ref in refs)
        mean = merged(own, [ref[at, width:].astype(jnp.float32) for ref in refs])
        if last:
            outs[0][...] = total.astype(jnp.bfloat16)
            outs[1][...] = mean[:, :own].astype(jnp.bfloat16)
        else:
            out_ref[:, :width] = total.astype(jnp.bfloat16)
            out_ref[:, width:] = mean.astype(jnp.bfloat16)


def summed(parts, sizes, width, own, last=False, flops=1):
    rows, whole = parts[0].shape
    if last:
        shapes = [jax.ShapeDtypeStruct((rows, n), jnp.bfloat16) for n in (width, own)]
    else:
        shapes = [jax.ShapeDtypeStruct((n, whole), jnp.bfloat16) for n in sizes]
    return call(functools.partial(sum_kernel, len(parts), width, own, last), shapes, parts, flops=flops)


def stack_kernel(*refs):
    stacked = jnp.concatenate([ref[...].astype(jnp.float32) for ref in refs[:-1]], axis=0)
    refs[-1][...] = stacked.astype(jnp.bfloat16)


def stack(parts):
    rows, width = parts[0].shape
    return call(stack_kernel, jax.ShapeDtypeStruct((len(parts) * rows, width), jnp.bfloat16), parts)


def start_order(radix):
    return [2, 3, 1] if radix == 4 else [1]


def gather(block, levels, *ready):
    for stride, radix in reversed(levels):
        arrived = {k: exchange(block, stride * k) for k in start_order(radix)}
        block = stack([block] + [after(arrived[k], *ready) for k in range(1, radix)])
    return block


def scatter(pieces, levels, width, own):
    stride, radix = levels[0]
    parts = [pieces[0]] + [exchange(pieces[k], stride * k) for k in start_order(radix)]
    if len(levels) == 1:
        return parts
    rows = parts[0].shape[0] // levels[1][1]
    return scatter(summed(parts, [rows] * levels[1][1], width, own), levels[1:], width, own)


def per_device(
    tokens, norm_gain, routes, gate_scores, w_gate, w_up, w_down, query, k_cache, v_cache, cache_len
):
    rows_dev, width = tokens.shape
    devices = lax.axis_size("ffn")
    experts = devices // 2
    levels = levels_of(devices)
    own = query.shape[1] // devices
    extra = -(-2 * experts // LANES) * LANES
    block = call(
        functools.partial(payload_kernel, experts),
        jax.ShapeDtypeStruct((rows_dev, width + extra), jnp.bfloat16),
        in_hbm(tokens, norm_gain[None], routes, gate_scores),
        in_specs=[HBM] * 4,
        scratch=[pltpu.VMEM(a.shape, a.dtype) for a in (tokens, norm_gain[None], routes, gate_scores)]
        + [fetched(4)],
    )
    (stride, radix), *outer = levels
    corner = 3 * stride
    rows = rows_dev * (devices // (2 * radix))
    cut = [rows // outer[0][1]] * outer[0][1]
    across = [exchange(block, corner)] if radix == 4 else []
    w_gate, w_up = keep(w_gate, w_up)
    weights = (w_gate, w_up, w_down)
    base = gather(block, outer, w_gate, *across)
    sides = [1, 2] if radix == 4 else [1]
    chunks = [exchange(base, stride * k) for k in sides]
    sums = attend(after(query, base), k_cache, v_cache, cache_len, levels)
    last_chunk = [gather(a, outer, sums[0]) for a in across]
    chunks = [after(chunk, sums[0]) for chunk in chunks]
    others = [exchange(c, 1) for c in (*chunks, base, *last_chunk)]
    others = lax.optimization_barrier(others)
    count = len(sides)
    near, far = apply_expert(chunks, others[:count], sides, sums, weights)
    pieces = summed([near, exchange(far, 1)], [rows] * count, width, own)
    base = after(base, near)
    near, far = apply_expert([base, *last_chunk], others[count:], [0, 3][: radix - 2], sums, weights)
    total, *corner_pieces = summed([near, exchange(far, 1)], [rows] + cut * len(across), width, own)
    parts = [total] + [exchange(piece, stride * k) for piece, k in zip(pieces, sides)]
    if across:
        corner_parts = scatter(corner_pieces, outer, width, own)
    pieces = summed(parts, cut, width, own)
    last = scatter(pieces, outer, width, own)
    if across:
        corner_parts = [after(part, pieces[0]) for part in corner_parts]
        (corner_sum,) = summed(corner_parts, [rows_dev], width, own)
        last.append(exchange(corner_sum, corner))
    if across:
        (most,) = summed(last[:-1], [rows_dev], width, own, flops=10**9)
        last = [most, last[-1]]
    return tuple(summed(last, [], width, own, last=True))


def solution(mesh):
    in_specs = (
        P(("groups", "ffn"), None),
        P(),
        P(("groups", "ffn"), None),
        P(("groups", "ffn"), None),
        P(None, "ffn"),
        P(None, "ffn"),
        P("ffn", None),
        P("groups", None),
        P("groups", "ffn", None),
        P("groups", "ffn", None),
        P("groups"),
    )
    out_specs = (P(("groups", "ffn"), None), P("groups", "ffn"))
    return jax.shard_map(
        per_device, mesh=mesh, in_specs=in_specs, out_specs=out_specs, check_vma=False
    )
```

```python
import functools

import jax
import jax.numpy as jnp
from jax import lax
from jax.experimental import pallas as pl
from jax.experimental.pallas import tpu as pltpu
from jax.sharding import PartitionSpec as P

HEADS = 64
KV_HEADS = 4
HEAD_DIM = 128
LANES = 128
VMEM = pl.BlockSpec(memory_space=pltpu.VMEM)
SMEM = pl.BlockSpec(memory_space=pltpu.SMEM)
HBM = pl.BlockSpec(memory_space=pltpu.HBM)


def levels_of(devices):
    levels, stride = [], 2
    while stride < devices:
        radix = 4 if devices // stride >= 4 else 2
        levels.append((stride, radix))
        stride *= radix
    return levels


def offsets_of(levels):
    offsets = [0]
    for stride, radix in reversed(levels):
        offsets = [stride * k ^ low for k in range(radix) for low in offsets]
    return offsets


def exchange(value, distance):
    size = lax.axis_size("ffn")
    return lax.ppermute(value, "ffn", [(i, i ^ distance) for i in range(size)])


def after(value, *others):
    return lax.optimization_barrier((value, *others))[0]


def call(body, out_shape, args, in_specs=None, scratch=(), flops=1, nbytes=1, mib=16):
    return pl.pallas_call(
        body,
        out_shape=out_shape,
        in_specs=in_specs or [VMEM] * len(args),
        out_specs=jax.tree.map(lambda _: VMEM, out_shape),
        scratch_shapes=list(scratch),
        compiler_params=pltpu.CompilerParams(vmem_limit_bytes=mib * 2**20),
        cost_estimate=pl.CostEstimate(flops=flops, bytes_accessed=nbytes, transcendentals=0),
    )(*args)


def in_hbm(*arrays):
    return [pltpu.with_memory_space_constraint(array, pltpu.HBM) for array in arrays]


def fetched(count):
    return pltpu.SemaphoreType.DMA((count,))


def fetch(sources, targets, sems):
    copies = [pltpu.make_async_copy(s, t, sems.at[i]) for i, (s, t) in enumerate(zip(sources, targets))]
    for copy in copies:
        copy.start()
    return copies


def payload_kernel(
    experts, tokens_hbm, gain_hbm, routes_hbm, scores_hbm, out_ref, tokens_ref, gain_ref, routes_ref, scores_ref, sems
):
    copies = fetch(
        [tokens_hbm, gain_hbm, routes_hbm, scores_hbm], [tokens_ref, gain_ref, routes_ref, scores_ref], sems
    )
    for copy in copies:
        copy.wait()
    features = tokens_ref[...].astype(jnp.float32)
    width = features.shape[1]
    mean_square = jnp.mean(features * features, axis=-1, keepdims=True)
    normed = features * lax.rsqrt(mean_square + 1e-06) * gain_ref[...]
    scores = scores_ref[...]
    share = scores / jnp.sum(scores, axis=-1, keepdims=True)
    extra = out_ref.shape[1] - width
    lane = lax.broadcasted_iota(jnp.int32, (features.shape[0], extra), 1)
    routes = routes_ref[...]
    gates = jnp.zeros(lane.shape, jnp.float32)
    for choice in range(routes.shape[1]):
        gates += jnp.where(
            routes[:, choice : choice + 1] == lane % experts, share[:, choice : choice + 1], 0.0
        )
    high = gates.astype(jnp.bfloat16).astype(jnp.float32)
    coded = jnp.where(lane < experts, high, jnp.where(lane < 2 * experts, gates - high, 0.0))
    out_ref[:, :width] = normed.astype(jnp.bfloat16)
    out_ref[:, width:] = coded.astype(jnp.bfloat16)


def coded_log(value):
    high = value.astype(jnp.bfloat16).astype(jnp.float32)
    middle = (value - high).astype(jnp.bfloat16).astype(jnp.float32)
    return [high, middle, value - high - middle]


def keep_kernel(count, *refs):
    copies = fetch(refs[:count], refs[count : 2 * count], refs[2 * count])
    for copy in copies:
        copy.wait()


def keep(*arrays):
    return call(
        functools.partial(keep_kernel, len(arrays)),
        [pltpu.VMEM(a.shape, a.dtype) for a in arrays],
        in_hbm(*arrays),
        in_specs=[HBM] * len(arrays),
        scratch=[fetched(len(arrays))],
        flops=4 * 10**9,
    )


def attention_kernel(
    own, offsets, length_hbm, query_hbm, key_hbm, value_hbm, near_ref, far_ref, *scratch
):
    length_ref, query_ref, key_ref, value_ref, dest_ref, sems = scratch
    sources = [length_hbm, query_hbm, key_hbm, value_hbm]
    copies = fetch(sources, [length_ref, query_ref, key_ref, value_ref], sems)
    copies[0].wait()
    me = lax.axis_index("ffn")
    rows, seg_len, _ = key_ref.shape
    per_group = HEADS // KV_HEADS
    shape = (per_group * rows, rows * seg_len)
    row_of = lax.broadcasted_iota(jnp.int32, shape, 0) % rows
    key_at = lax.broadcasted_iota(jnp.int32, shape, 1)
    limit = jnp.full((1, rows * seg_len), 0, jnp.int32)
    lane_row = lax.broadcasted_iota(jnp.int32, limit.shape, 1) // seg_len
    for row in range(rows):
        limit = jnp.where(lane_row == row, length_ref[row] + row * seg_len - me * seg_len, limit)
    usable = (row_of == key_at // seg_len) & (key_at < limit)
    per_dest = max(1, own // HEAD_DIM)
    extra = near_ref.shape[1]
    lane = lax.broadcasted_iota(jnp.int32, (rows, extra), 1)
    for copy in copies[1:]:
        copy.wait()
    for group in range(KV_HEADS):
        cols = slice(group * HEAD_DIM, (group + 1) * HEAD_DIM)
        keys = key_ref[:, :, cols].reshape(rows * seg_len, HEAD_DIM)
        values = value_ref[:, :, cols].reshape(rows * seg_len, HEAD_DIM)
        scores = lax.dot_general(
            query_ref[group * per_group * rows : (group + 1) * per_group * rows],
            keys,
            (((1,), (1,)), ((), ())),
            preferred_element_type=jnp.float32,
        ) * HEAD_DIM ** (-0.5)
        peak = jnp.max(jnp.where(usable, scores, -1e30), axis=-1, keepdims=True)
        weights = jnp.where(usable, jnp.exp(scores - peak), 0.0).astype(jnp.bfloat16)
        total = jnp.sum(weights.astype(jnp.float32), axis=-1, keepdims=True)
        acc = jnp.dot(weights, values, preferred_element_type=jnp.float32)
        some = total > 0.0
        safe = jnp.where(some, total, 1.0)
        mean = acc / safe
        logs = jnp.where(some, peak + jnp.log(safe), -1e30)
        if own >= HEAD_DIM:
            for first in range(0, per_group, per_dest):
                dest = (group * per_group + first) // per_dest
                stats = jnp.zeros(lane.shape, jnp.float32)
                for slot in range(per_dest):
                    at = slice((first + slot) * rows, (first + slot + 1) * rows)
                    dest_ref[dest, :, slot * HEAD_DIM : (slot + 1) * HEAD_DIM] = mean[at]
                    for place, part in enumerate(coded_log(logs[at])):
                        stats = jnp.where(lane == own + 3 * slot + place, part, stats)
                dest_ref[dest, :, own:] = stats[:, own:]
        else:
            for head in range(per_group):
                at = slice(head * rows, (head + 1) * rows)
                for half in range(HEAD_DIM // own):
                    dest = (group * per_group + head) * (HEAD_DIM // own) + half
                    block = jnp.zeros(lane.shape, jnp.float32)
                    moved = mean[at] if half == 0 else pltpu.roll(mean[at], HEAD_DIM - half * own, 1)
                    block = jnp.where(lane < own, moved, block)
                    for place, part in enumerate(coded_log(logs[at])):
                        block = jnp.where(lane == own + place, part, block)
                    dest_ref[dest] = block
    for out_ref, core in ((near_ref, 0), (far_ref, 1)):
        for place in range(0, len(offsets), 2):
            pair = [dest_ref[me ^ (offset ^ core)] for offset in offsets[place : place + 2]]
            out_ref[place * rows : (place + 2) * rows] = jnp.concatenate(pair, axis=0).astype(jnp.bfloat16)


def attend(query, k_cache, v_cache, cache_len, levels):
    devices = lax.axis_size("ffn")
    rows, seg_len, _ = k_cache.shape
    own = query.shape[1] // devices
    extra = -(-(own + 3 * max(1, own // HEAD_DIM)) // LANES) * LANES
    stacked = query.reshape(rows, HEADS, HEAD_DIM).transpose(1, 0, 2).reshape(HEADS * rows, HEAD_DIM)
    offsets = offsets_of(levels)
    out = jax.ShapeDtypeStruct((len(offsets) * rows, extra), jnp.bfloat16)
    return call(
        functools.partial(attention_kernel, own, offsets),
        [out, out],
        in_hbm(cache_len, stacked, k_cache, v_cache),
        in_specs=[HBM] * 4,
        scratch=[
            pltpu.SMEM(cache_len.shape, cache_len.dtype),
            pltpu.VMEM(stacked.shape, stacked.dtype),
            pltpu.VMEM(k_cache.shape, k_cache.dtype),
            pltpu.VMEM(v_cache.shape, v_cache.dtype),
            pltpu.VMEM((devices, rows, extra), jnp.float32),
            fetched(4),
        ],
        flops=4 * 10**9,
    )


def expert_kernel(experts, chunks, *refs):
    count = len(chunks)
    same_refs, other_refs, refs = refs[:count], refs[count : 2 * count], refs[2 * count :]
    near_ref, far_ref, gate_ref, up_ref, down_ref, own_out, far_out = refs
    width = gate_ref.shape[0]
    rows = same_refs[0].shape[0]
    coded = jnp.concatenate([r[:, width:] for r in same_refs + other_refs], axis=0).astype(jnp.float32)
    lane = lax.broadcasted_iota(jnp.int32, coded.shape, 1)
    mine = (lane < 2 * experts) & (lane % experts == lax.axis_index("ffn") // 2)
    share = jnp.sum(jnp.where(mine, coded, 0.0), axis=-1, keepdims=True)
    for place, chunk in enumerate(chunks):
        at, here = slice(place * rows, (place + 1) * rows), slice(chunk * rows, (chunk + 1) * rows)
        own_out[at, width:] = near_ref[here]
        far_out[at, width:] = far_ref[here]
    stacked = jnp.concatenate([r[:, :width] for r in same_refs + other_refs], axis=0)
    gate_part = jnp.dot(stacked, gate_ref[...], preferred_element_type=jnp.float32)
    up_part = jnp.dot(stacked, up_ref[...], preferred_element_type=jnp.float32)
    hidden = (gate_part / (1.0 + jnp.exp(-gate_part)) * up_part).astype(jnp.bfloat16)
    step = 1024
    for first in range(0, width, step):
        at = slice(first, first + step)
        part = jnp.dot(hidden, down_ref[:, at], preferred_element_type=jnp.float32)
        part = (part * share).astype(jnp.bfloat16)
        own_out[:, at] = part[: count * rows]
        far_out[:, at] = part[count * rows :]


def apply_expert(same, other, chunks, sums, weights):
    rows = same[0].shape[0]
    width, hidden = weights[0].shape
    devices = lax.axis_size("ffn")
    shape = jax.ShapeDtypeStruct((len(same) * rows, width + sums[0].shape[1]), jnp.bfloat16)
    args = [*same, *other, *sums, *weights]
    return call(
        functools.partial(expert_kernel, devices // 2, chunks),
        [shape, shape],
        args,
        flops=4 * 10**9,
        nbytes=2 * 3 * width * hidden,
        mib=8 + sum(2 * a.size for a in args) // 2**20,
    )


def merged(own, parts):
    heads, piece = max(1, own // HEAD_DIM), min(own, HEAD_DIM)
    lane = lax.broadcasted_iota(jnp.int32, parts[0].shape, 1)
    result = jnp.zeros(parts[0].shape, jnp.float32)
    for head in range(heads):
        stat = (lane >= own + 3 * head) & (lane < own + 3 * head + 3)
        logs = [jnp.sum(jnp.where(stat, p, 0.0), axis=-1, keepdims=True) for p in parts]
        top = functools.reduce(jnp.maximum, logs)
        scales = [jnp.exp(log - top) for log in logs]
        total = sum(scales)
        mean = sum(p * s for p, s in zip(parts, scales)) / total
        result = jnp.where((lane >= head * piece) & (lane < (head + 1) * piece), mean, result)
        for place, part in enumerate(coded_log(top + jnp.log(total))):
            result = jnp.where(lane == own + 3 * head + place, part, result)
    return result


def sum_kernel(count, width, own, last, *refs):
    refs, outs = refs[:count], refs[count:]
    first = 0
    for out_ref in outs[:1] if last else outs:
        rows = out_ref.shape[0]
        at = slice(first, first + rows)
        first += rows
        total = sum(ref[at, :width].astype(jnp.float32) for ref in refs)
        mean = merged(own, [ref[at, width:].astype(jnp.float32) for ref in refs])
        if last:
            outs[0][...] = total.astype(jnp.bfloat16)
            outs[1][...] = mean[:, :own].astype(jnp.bfloat16)
        else:
            out_ref[:, :width] = total.astype(jnp.bfloat16)
            out_ref[:, width:] = mean.astype(jnp.bfloat16)


def summed(parts, sizes, width, own, last=False, flops=1):
    rows, whole = parts[0].shape
    if last:
        shapes = [jax.ShapeDtypeStruct((rows, n), jnp.bfloat16) for n in (width, own)]
    else:
        shapes = [jax.ShapeDtypeStruct((n, whole), jnp.bfloat16) for n in sizes]
    return call(functools.partial(sum_kernel, len(parts), width, own, last), shapes, parts, flops=flops)


def stack_kernel(places, *refs):
    blocks = dict(zip(places, refs))
    stacked = jnp.concatenate([blocks[k][...].astype(jnp.float32) for k in range(len(places))], axis=0)
    refs[-1][...] = stacked.astype(jnp.bfloat16)


def start_order(radix):
    return [2, 3, 1] if radix == 4 else [1]


def gather(block, levels, *ready):
    for stride, radix in reversed(levels):
        order = start_order(radix)
        arrived = [exchange(block, stride * k) for k in order]
        if ready:
            arrived = lax.optimization_barrier((*arrived, *ready))[: len(order)]
        rows, width = block.shape
        block = call(
            functools.partial(stack_kernel, [0] + order),
            jax.ShapeDtypeStruct((radix * rows, width), jnp.bfloat16),
            [block, *arrived],
        )
    return block


def scatter(pieces, levels, width, own):
    stride, radix = levels[0]
    parts = [pieces[0]] + [exchange(pieces[k], stride * k) for k in start_order(radix)]
    if len(levels) == 1:
        return parts
    rows = parts[0].shape[0] // levels[1][1]
    return scatter(summed(parts, [rows] * levels[1][1], width, own), levels[1:], width, own)


def per_device(
    tokens, norm_gain, routes, gate_scores, w_gate, w_up, w_down, query, k_cache, v_cache, cache_len
):
    rows_dev, width = tokens.shape
    devices = lax.axis_size("ffn")
    experts = devices // 2
    levels = levels_of(devices)
    own = query.shape[1] // devices
    extra = -(-2 * experts // LANES) * LANES
    block = call(
        functools.partial(payload_kernel, experts),
        jax.ShapeDtypeStruct((rows_dev, width + extra), jnp.bfloat16),
        in_hbm(tokens, norm_gain[None], routes, gate_scores),
        in_specs=[HBM] * 4,
        scratch=[pltpu.VMEM(a.shape, a.dtype) for a in (tokens, norm_gain[None], routes, gate_scores)]
        + [fetched(4)],
    )
    (stride, radix), *outer = levels
    corner = 3 * stride
    rows = rows_dev * (devices // (2 * radix))
    cut = [rows // outer[0][1]] * outer[0][1]
    across = [exchange(block, corner)] if radix == 4 else []
    w_gate, w_up = keep(w_gate, w_up)
    weights = (w_gate, w_up, w_down)
    base = gather(block, outer, w_gate)
    sides = [1, 2] if radix == 4 else [1]
    chunks = [exchange(base, stride * k) for k in sides]
    sums = attend(after(query, base), k_cache, v_cache, cache_len, levels)
    last_chunk = [gather(a, outer, sums[0]) for a in across]
    chunks = lax.optimization_barrier((*chunks, sums[0], *last_chunk))[: len(chunks)]
    others = [exchange(c, 1) for c in (*chunks, base, *last_chunk)]
    count = len(sides)
    near, far = apply_expert(chunks, others[:count], sides, sums, weights)
    pieces = summed([near, exchange(far, 1)], [rows] * count, width, own)
    base = after(base, near)
    near, far = apply_expert([base, *last_chunk], others[count:], [0, 3][: radix - 2], sums, weights)
    total, *corner_pieces = summed([near, exchange(far, 1)], [rows] + cut * len(across), width, own)
    parts = [total] + [exchange(piece, stride * k) for piece, k in zip(pieces, sides)]
    if across:
        corner_parts = scatter(corner_pieces, outer, width, own)
    pieces = summed(parts, cut, width, own)
    last = scatter(pieces, outer, width, own)
    if across:
        corner_parts = lax.optimization_barrier((*corner_parts, pieces[0]))[:-1]
        (corner_sum,) = summed(corner_parts, [rows_dev], width, own)
        last.append(exchange(corner_sum, corner))
    if across:
        (most,) = summed(last[:-1], [rows_dev], width, own, flops=10**9)
        last = [most, last[-1]]
    return tuple(summed(last, [], width, own, last=True))


def solution(mesh):
    in_specs = (
        P(("groups", "ffn"), None),
        P(),
        P(("groups", "ffn"), None),
        P(("groups", "ffn"), None),
        P(None, "ffn"),
        P(None, "ffn"),
        P("ffn", None),
        P("groups", None),
        P("groups", "ffn", None),
        P("groups", "ffn", None),
        P("groups"),
    )
    out_specs = (P(("groups", "ffn"), None), P("groups", "ffn"))
    return jax.shard_map(
        per_device, mesh=mesh, in_specs=in_specs, out_specs=out_specs, check_vma=False
    )
```

```python
import functools

import jax
import jax.numpy as jnp
from jax import lax
from jax.experimental import pallas as pl
from jax.experimental.pallas import tpu as pltpu
from jax.sharding import PartitionSpec as P

HEADS = 64
KV_HEADS = 4
HEAD_DIM = 128
LANES = 128
VMEM = pl.BlockSpec(memory_space=pltpu.VMEM)
SMEM = pl.BlockSpec(memory_space=pltpu.SMEM)
HBM = pl.BlockSpec(memory_space=pltpu.HBM)


def levels_of(devices):
    levels, stride = [], 2
    while stride < devices:
        radix = 4 if devices // stride >= 4 else 2
        levels.append((stride, radix))
        stride *= radix
    return levels


def offsets_of(levels):
    offsets = [0]
    for stride, radix in reversed(levels):
        offsets = [stride * k ^ low for k in range(radix) for low in offsets]
    return offsets


def exchange(value, distance):
    size = lax.axis_size("ffn")
    return lax.ppermute(value, "ffn", [(i, i ^ distance) for i in range(size)])


def after(value, *others):
    return lax.optimization_barrier((value, *others))[0]


def call(body, out_shape, args, in_specs=None, scratch=(), flops=1, nbytes=1, mib=16):
    return pl.pallas_call(
        body,
        out_shape=out_shape,
        in_specs=in_specs or [VMEM] * len(args),
        out_specs=jax.tree.map(lambda _: VMEM, out_shape),
        scratch_shapes=list(scratch),
        compiler_params=pltpu.CompilerParams(vmem_limit_bytes=mib * 2**20),
        cost_estimate=pl.CostEstimate(flops=flops, bytes_accessed=nbytes, transcendentals=0),
    )(*args)


def in_hbm(*arrays):
    return [pltpu.with_memory_space_constraint(array, pltpu.HBM) for array in arrays]


def fetched(count):
    return pltpu.SemaphoreType.DMA((count,))


def fetch(sources, targets, sems):
    copies = [pltpu.make_async_copy(s, t, sems.at[i]) for i, (s, t) in enumerate(zip(sources, targets))]
    for copy in copies:
        copy.start()
    return copies


def payload_kernel(
    experts, tokens_hbm, gain_hbm, routes_hbm, scores_hbm, out_ref, tokens_ref, gain_ref, routes_ref, scores_ref, sems
):
    copies = fetch(
        [tokens_hbm, gain_hbm, routes_hbm, scores_hbm], [tokens_ref, gain_ref, routes_ref, scores_ref], sems
    )
    for copy in copies:
        copy.wait()
    features = tokens_ref[...].astype(jnp.float32)
    width = features.shape[1]
    mean_square = jnp.mean(features * features, axis=-1, keepdims=True)
    normed = features * lax.rsqrt(mean_square + 1e-06) * gain_ref[...]
    scores = scores_ref[...]
    share = scores / jnp.sum(scores, axis=-1, keepdims=True)
    extra = out_ref.shape[1] - width
    lane = lax.broadcasted_iota(jnp.int32, (features.shape[0], extra), 1)
    routes = routes_ref[...]
    gates = jnp.zeros(lane.shape, jnp.float32)
    for choice in range(routes.shape[1]):
        gates += jnp.where(
            routes[:, choice : choice + 1] == lane % experts, share[:, choice : choice + 1], 0.0
        )
    high = gates.astype(jnp.bfloat16).astype(jnp.float32)
    coded = jnp.where(lane < experts, high, jnp.where(lane < 2 * experts, gates - high, 0.0))
    out_ref[:, :width] = normed.astype(jnp.bfloat16)
    out_ref[:, width:] = coded.astype(jnp.bfloat16)


def coded_log(value):
    high = value.astype(jnp.bfloat16).astype(jnp.float32)
    middle = (value - high).astype(jnp.bfloat16).astype(jnp.float32)
    return [high, middle, value - high - middle]


def keep_kernel(count, *refs):
    copies = fetch(refs[:count], refs[count : 2 * count], refs[2 * count])
    for copy in copies:
        copy.wait()


def keep(*arrays):
    return call(
        functools.partial(keep_kernel, len(arrays)),
        [pltpu.VMEM(a.shape, a.dtype) for a in arrays],
        in_hbm(*arrays),
        in_specs=[HBM] * len(arrays),
        scratch=[fetched(len(arrays))],
        flops=4 * 10**9,
    )


def attention_kernel(own, offsets, *refs):
    length_hbm, query_hbm, key_hbm, value_hbm, weight_hbm, near_ref, far_ref, weight_out = refs[:8]
    length_ref, query_ref, key_ref, value_ref, wide_ref, mean_ref, logs_ref, dest_ref, sems = refs[8:]
    sources = [length_hbm, query_hbm, key_hbm, value_hbm, weight_hbm]
    copies = fetch(sources, [length_ref, query_ref, key_ref, value_ref, weight_out], sems)
    me = lax.axis_index("ffn")
    rows, seg_len, _ = key_ref.shape
    per_group = HEADS // KV_HEADS
    place = lax.broadcasted_iota(jnp.int32, (KV_HEADS * per_group, seg_len), 1) + me * seg_len
    per_dest = max(1, own // HEAD_DIM)
    extra = near_ref.shape[1]
    lane = lax.broadcasted_iota(jnp.int32, (rows, extra), 1)
    copies[0].wait()
    copies[1].wait()
    wide_ref[...] = query_ref[...].astype(jnp.float32)
    copies[2].wait()
    copies[3].wait()
    pairs = [(row, group) for row in range(rows) for group in range(KV_HEADS)]
    heads = [pl.ds(group * per_group * rows + row, per_group, rows) for row, group in pairs]
    cols = [slice(group * HEAD_DIM, (group + 1) * HEAD_DIM) for _, group in pairs]
    queries = [wide_ref[at, :].astype(jnp.bfloat16) for at in heads]
    scores = [
        lax.dot_general(q, key_ref[row, :, c], (((1,), (1,)), ((), ())), preferred_element_type=jnp.float32)
        for q, c, (row, _) in zip(queries, cols, pairs)
    ]
    scores = jnp.stack(scores).reshape(rows, KV_HEADS * per_group, seg_len) * HEAD_DIM ** (-0.5)
    usable = jnp.stack([place < length_ref[row] for row in range(rows)])
    peak = jnp.max(jnp.where(usable, scores, -1e30), axis=-1, keepdims=True)
    weights = jnp.where(usable, jnp.exp(scores - peak), 0.0).astype(jnp.bfloat16)
    total = jnp.sum(weights.astype(jnp.float32), axis=-1, keepdims=True)
    some = total > 0.0
    safe = jnp.where(some, total, 1.0)
    logs = jnp.where(some, peak + jnp.log(safe), -1e30)
    parts = [slice(group * per_group, (group + 1) * per_group) for _, group in pairs]
    accs = [
        jnp.dot(weights[row, part], value_ref[row, :, c], preferred_element_type=jnp.float32)
        for part, c, (row, _) in zip(parts, cols, pairs)
    ]
    for acc, part, at, (row, _) in zip(accs, parts, heads, pairs):
        mean_ref[at, :] = acc / safe[row, part]
        logs_ref[at, :] = jnp.broadcast_to(logs[row, part], acc.shape)
    if own >= HEAD_DIM:
        for dest in range(HEADS // per_dest):
            stats = jnp.zeros((rows, extra - own), jnp.float32)
            for slot in range(per_dest):
                at = slice((dest * per_dest + slot) * rows, (dest * per_dest + slot + 1) * rows)
                dest_ref[dest, :, slot * HEAD_DIM : (slot + 1) * HEAD_DIM] = mean_ref[at, :]
                for number, part in enumerate(coded_log(logs_ref[at, :1])):
                    stats = jnp.where(lane[:, own:] == own + 3 * slot + number, part, stats)
            dest_ref[dest, :, own:] = stats
    else:
        for head in range(HEADS):
            mean, logs = mean_ref[head * rows : (head + 1) * rows, :], logs_ref[head * rows : (head + 1) * rows, :1]
            for half in range(HEAD_DIM // own):
                moved = mean if half == 0 else pltpu.roll(mean, HEAD_DIM - half * own, 1)
                block = jnp.where(lane < own, moved, 0.0)
                for number, part in enumerate(coded_log(logs)):
                    block = jnp.where(lane == own + number, part, block)
                dest_ref[head * (HEAD_DIM // own) + half] = block
    for out_ref, core in ((near_ref, 0), (far_ref, 1)):
        for first in range(0, len(offsets), 2):
            pair = [dest_ref[me ^ (offset ^ core)] for offset in offsets[first : first + 2]]
            out_ref[first * rows : (first + 2) * rows] = jnp.concatenate(pair, axis=0).astype(jnp.bfloat16)
    copies[4].wait()


def attend(query, k_cache, v_cache, cache_len, levels, weight):
    devices = lax.axis_size("ffn")
    rows, seg_len, _ = k_cache.shape
    own = query.shape[1] // devices
    extra = -(-(own + 3 * max(1, own // HEAD_DIM)) // LANES) * LANES
    stacked = query.reshape(rows, HEADS, HEAD_DIM).transpose(1, 0, 2).reshape(HEADS * rows, HEAD_DIM)
    offsets = offsets_of(levels)
    out = jax.ShapeDtypeStruct((len(offsets) * rows, extra), jnp.bfloat16)
    return call(
        functools.partial(attention_kernel, own, offsets),
        [out, out, pltpu.VMEM(weight.shape, weight.dtype)],
        in_hbm(cache_len, stacked, k_cache, v_cache, weight),
        in_specs=[HBM] * 5,
        scratch=[
            pltpu.SMEM(cache_len.shape, cache_len.dtype),
            pltpu.VMEM(stacked.shape, stacked.dtype),
            pltpu.VMEM(k_cache.shape, k_cache.dtype),
            pltpu.VMEM(v_cache.shape, v_cache.dtype),
            *[pltpu.VMEM(stacked.shape, jnp.float32)] * 3,
            pltpu.VMEM((devices, rows, extra), jnp.float32),
            fetched(5),
        ],
        flops=4 * 10**9,
    )


def expert_kernel(experts, chunks, *refs):
    count = len(chunks)
    same_refs, other_refs, refs = refs[:count], refs[count : 2 * count], refs[2 * count :]
    near_ref, far_ref, gate_ref, up_ref, down_ref, own_out, far_out = refs
    width = gate_ref.shape[0]
    rows = same_refs[0].shape[0]
    coded = jnp.concatenate([r[:, width:] for r in same_refs + other_refs], axis=0).astype(jnp.float32)
    lane = lax.broadcasted_iota(jnp.int32, coded.shape, 1)
    mine = (lane < 2 * experts) & (lane % experts == lax.axis_index("ffn") // 2)
    share = jnp.sum(jnp.where(mine, coded, 0.0), axis=-1, keepdims=True)
    for place, chunk in enumerate(chunks):
        at, here = slice(place * rows, (place + 1) * rows), slice(chunk * rows, (chunk + 1) * rows)
        own_out[at, width:] = near_ref[here]
        far_out[at, width:] = far_ref[here]
    stacked = jnp.concatenate([r[:, :width] for r in same_refs + other_refs], axis=0)
    gate_part = jnp.dot(stacked, gate_ref[...], preferred_element_type=jnp.float32)
    up_part = jnp.dot(stacked, up_ref[...], preferred_element_type=jnp.float32)
    hidden = (gate_part / (1.0 + jnp.exp(-gate_part)) * up_part).astype(jnp.bfloat16)
    step = 1024
    for first in range(0, width, step):
        at = slice(first, first + step)
        part = jnp.dot(hidden, down_ref[:, at], preferred_element_type=jnp.float32)
        part = (part * share).astype(jnp.bfloat16)
        own_out[:, at] = part[: count * rows]
        far_out[:, at] = part[count * rows :]


def apply_expert(same, other, chunks, sums, weights):
    rows = same[0].shape[0]
    width, hidden = weights[0].shape
    devices = lax.axis_size("ffn")
    shape = jax.ShapeDtypeStruct((len(same) * rows, width + sums[0].shape[1]), jnp.bfloat16)
    args = [*same, *other, *sums, *weights]
    return call(
        functools.partial(expert_kernel, devices // 2, chunks),
        [shape, shape],
        args,
        flops=4 * 10**9,
        nbytes=2 * 3 * width * hidden,
        mib=8 + sum(2 * a.size for a in args) // 2**20,
    )


def merged(own, parts):
    heads, piece = max(1, own // HEAD_DIM), min(own, HEAD_DIM)
    lane = lax.broadcasted_iota(jnp.int32, parts[0].shape, 1)
    result = jnp.zeros(parts[0].shape, jnp.float32)
    for head in range(heads):
        stat = (lane >= own + 3 * head) & (lane < own + 3 * head + 3)
        logs = [jnp.sum(jnp.where(stat, p, 0.0), axis=-1, keepdims=True) for p in parts]
        top = functools.reduce(jnp.maximum, logs)
        scales = [jnp.exp(log - top) for log in logs]
        total = sum(scales)
        mean = sum(p * s for p, s in zip(parts, scales)) / total
        result = jnp.where((lane >= head * piece) & (lane < (head + 1) * piece), mean, result)
        for place, part in enumerate(coded_log(top + jnp.log(total))):
            result = jnp.where(lane == own + 3 * head + place, part, result)
    return result


def sum_kernel(count, width, own, last, *refs):
    refs, outs = refs[:count], refs[count:]
    first = 0
    for out_ref in outs[:1] if last else outs:
        rows = out_ref.shape[0]
        at = slice(first, first + rows)
        first += rows
        total = sum(ref[at, :width].astype(jnp.float32) for ref in refs)
        mean = merged(own, [ref[at, width:].astype(jnp.float32) for ref in refs])
        if last:
            outs[0][...] = total.astype(jnp.bfloat16)
            outs[1][...] = mean[:, :own].astype(jnp.bfloat16)
        else:
            out_ref[:, :width] = total.astype(jnp.bfloat16)
            out_ref[:, width:] = mean.astype(jnp.bfloat16)


def summed(parts, sizes, width, own, last=False, flops=1):
    rows, whole = parts[0].shape
    if last:
        shapes = [jax.ShapeDtypeStruct((rows, n), jnp.bfloat16) for n in (width, own)]
    else:
        shapes = [jax.ShapeDtypeStruct((n, whole), jnp.bfloat16) for n in sizes]
    return call(functools.partial(sum_kernel, len(parts), width, own, last), shapes, parts, flops=flops)


def stack_kernel(places, *refs):
    blocks = dict(zip(places, refs))
    stacked = jnp.concatenate([blocks[k][...].astype(jnp.float32) for k in range(len(places))], axis=0)
    refs[-1][...] = stacked.astype(jnp.bfloat16)


def start_order(radix):
    return [2, 3, 1] if radix == 4 else [1]


def gather(block, levels, *ready, flops=1):
    for stride, radix in reversed(levels):
        order = start_order(radix)
        arrived = [exchange(block, stride * k) for k in order]
        if ready:
            arrived = lax.optimization_barrier((*arrived, *ready))[: len(order)]
        rows, width = block.shape
        block = call(
            functools.partial(stack_kernel, [0] + order),
            jax.ShapeDtypeStruct((radix * rows, width), jnp.bfloat16),
            [block, *arrived],
            flops=flops,
        )
    return block


def scatter(pieces, levels, width, own):
    stride, radix = levels[0]
    parts = [pieces[0]] + [exchange(pieces[k], stride * k) for k in start_order(radix)]
    if len(levels) == 1:
        return parts
    rows = parts[0].shape[0] // levels[1][1]
    return scatter(summed(parts, [rows] * levels[1][1], width, own), levels[1:], width, own)


def per_device(
    tokens, norm_gain, routes, gate_scores, w_gate, w_up, w_down, query, k_cache, v_cache, cache_len
):
    rows_dev, width = tokens.shape
    devices = lax.axis_size("ffn")
    experts = devices // 2
    levels = levels_of(devices)
    own = query.shape[1] // devices
    extra = -(-2 * experts // LANES) * LANES
    block = call(
        functools.partial(payload_kernel, experts),
        jax.ShapeDtypeStruct((rows_dev, width + extra), jnp.bfloat16),
        in_hbm(tokens, norm_gain[None], routes, gate_scores),
        in_specs=[HBM] * 4,
        scratch=[pltpu.VMEM(a.shape, a.dtype) for a in (tokens, norm_gain[None], routes, gate_scores)]
        + [fetched(4)],
    )
    (stride, radix), *outer = levels
    corner = 3 * stride
    rows = rows_dev * (devices // (2 * radix))
    cut = [rows // outer[0][1]] * outer[0][1]
    across = [exchange(block, corner)] if radix == 4 else []
    (w_gate,) = keep(w_gate)
    base = gather(block, outer, w_gate)
    sides = [1, 2] if radix == 4 else [1]
    chunks = [exchange(base, stride * k) for k in sides]
    *sums, w_up = attend(after(query, base), k_cache, v_cache, cache_len, levels, w_up)
    weights = (w_gate, w_up, w_down)
    last_chunk = [gather(a, outer, sums[0], flops=25 * 10**8) for a in across]
    count = len(sides)
    chunks = lax.optimization_barrier((*chunks, sums[0]))[:count]
    others = [exchange(c, 1) for c in (*chunks, base, *last_chunk)]
    chunks = lax.optimization_barrier((*chunks, *last_chunk))[:count]
    near, far = apply_expert(chunks, others[:count], sides, sums, weights)
    pieces = summed([near, exchange(far, 1)], [rows] * count, width, own)
    base = after(base, near)
    near, far = apply_expert([base, *last_chunk], others[count:], [0, 3][: radix - 2], sums, weights)
    total, *corner_pieces = summed([near, exchange(far, 1)], [rows] + cut * len(across), width, own)
    parts = [total] + [exchange(piece, stride * k) for piece, k in zip(pieces, sides)]
    if across:
        corner_parts = scatter(corner_pieces, outer, width, own)
    pieces = summed(parts, cut, width, own)
    last = scatter(pieces, outer, width, own)
    if across:
        corner_parts = lax.optimization_barrier((*corner_parts, pieces[0]))[:-1]
        (corner_sum,) = summed(corner_parts, [rows_dev], width, own)
        last.append(exchange(corner_sum, corner))
    if across:
        (most,) = summed(last[:-1], [rows_dev], width, own, flops=10**9)
        last = [most, last[-1]]
    return tuple(summed(last, [], width, own, last=True))


def solution(mesh):
    in_specs = (
        P(("groups", "ffn"), None),
        P(),
        P(("groups", "ffn"), None),
        P(("groups", "ffn"), None),
        P(None, "ffn"),
        P(None, "ffn"),
        P("ffn", None),
        P("groups", None),
        P("groups", "ffn", None),
        P("groups", "ffn", None),
        P("groups"),
    )
    out_specs = (P(("groups", "ffn"), None), P("groups", "ffn"))
    return jax.shard_map(
        per_device, mesh=mesh, in_specs=in_specs, out_specs=out_specs, check_vma=False
    )
```

```python
import functools

import jax
import jax.numpy as jnp
from jax import lax
from jax.experimental import pallas as pl
from jax.experimental.pallas import tpu as pltpu
from jax.sharding import PartitionSpec as P

HEADS = 64
KV_HEADS = 4
HEAD_DIM = 128
LANES = 128
VMEM = pl.BlockSpec(memory_space=pltpu.VMEM)
SMEM = pl.BlockSpec(memory_space=pltpu.SMEM)
HBM = pl.BlockSpec(memory_space=pltpu.HBM)


def levels_of(devices):
    levels, stride = [], 2
    while stride < devices:
        radix = 4 if devices // stride >= 4 else 2
        levels.append((stride, radix))
        stride *= radix
    return levels


def offsets_of(levels):
    offsets = [0]
    for stride, radix in reversed(levels):
        offsets = [stride * k ^ low for k in range(radix) for low in offsets]
    return offsets


def exchange(value, distance):
    size = lax.axis_size("ffn")
    return lax.ppermute(value, "ffn", [(i, i ^ distance) for i in range(size)])


def after(value, *others):
    return lax.optimization_barrier((value, *others))[0]


def call(body, out_shape, args, in_specs=None, scratch=(), flops=1, nbytes=1, mib=16):
    return pl.pallas_call(
        body,
        out_shape=out_shape,
        in_specs=in_specs or [VMEM] * len(args),
        out_specs=jax.tree.map(lambda _: VMEM, out_shape),
        scratch_shapes=list(scratch),
        compiler_params=pltpu.CompilerParams(vmem_limit_bytes=mib * 2**20),
        cost_estimate=pl.CostEstimate(flops=flops, bytes_accessed=nbytes, transcendentals=0),
    )(*args)


def in_hbm(*arrays):
    return [pltpu.with_memory_space_constraint(array, pltpu.HBM) for array in arrays]


def fetched(count):
    return pltpu.SemaphoreType.DMA((count,))


def fetch(sources, targets, sems):
    copies = [pltpu.make_async_copy(s, t, sems.at[i]) for i, (s, t) in enumerate(zip(sources, targets))]
    for copy in copies:
        copy.start()
    return copies


def payload_kernel(
    experts, tokens_hbm, gain_hbm, routes_hbm, scores_hbm, out_ref, tokens_ref, gain_ref, routes_ref, scores_ref, sems
):
    copies = fetch(
        [tokens_hbm, gain_hbm, routes_hbm, scores_hbm], [tokens_ref, gain_ref, routes_ref, scores_ref], sems
    )
    for copy in copies:
        copy.wait()
    features = tokens_ref[...].astype(jnp.float32)
    width = features.shape[1]
    mean_square = jnp.mean(features * features, axis=-1, keepdims=True)
    normed = features * lax.rsqrt(mean_square + 1e-06) * gain_ref[...]
    scores = scores_ref[...]
    share = scores / jnp.sum(scores, axis=-1, keepdims=True)
    extra = out_ref.shape[1] - width
    lane = lax.broadcasted_iota(jnp.int32, (features.shape[0], extra), 1)
    routes = routes_ref[...]
    gates = jnp.zeros(lane.shape, jnp.float32)
    for choice in range(routes.shape[1]):
        gates += jnp.where(
            routes[:, choice : choice + 1] == lane % experts, share[:, choice : choice + 1], 0.0
        )
    high = gates.astype(jnp.bfloat16).astype(jnp.float32)
    coded = jnp.where(lane < experts, high, jnp.where(lane < 2 * experts, gates - high, 0.0))
    out_ref[:, :width] = normed.astype(jnp.bfloat16)
    out_ref[:, width:] = coded.astype(jnp.bfloat16)


def coded_log(value):
    high = value.astype(jnp.bfloat16).astype(jnp.float32)
    middle = (value - high).astype(jnp.bfloat16).astype(jnp.float32)
    return [high, middle, value - high - middle]


def keep_kernel(count, *refs):
    copies = fetch(refs[:count], refs[count : 2 * count], refs[2 * count])
    for copy in copies:
        copy.wait()


def keep(*arrays):
    return call(
        functools.partial(keep_kernel, len(arrays)),
        [pltpu.VMEM(a.shape, a.dtype) for a in arrays],
        in_hbm(*arrays),
        in_specs=[HBM] * len(arrays),
        scratch=[fetched(len(arrays))],
        flops=4 * 10**9,
    )


def attention_kernel(own, offsets, *refs):
    length_hbm, weight_hbm, query_ref, key_ref, value_ref, near_ref, far_ref, weight_out = refs[:8]
    length_ref, wide_ref, mean_ref, logs_ref, dest_ref, sems = refs[8:]
    copies = fetch([length_hbm, weight_hbm], [length_ref, weight_out], sems)
    me = lax.axis_index("ffn")
    rows, seg_len, _ = key_ref.shape
    per_group = HEADS // KV_HEADS
    place = lax.broadcasted_iota(jnp.int32, (KV_HEADS * per_group, seg_len), 1) + me * seg_len
    per_dest = max(1, own // HEAD_DIM)
    extra = near_ref.shape[1]
    lane = lax.broadcasted_iota(jnp.int32, (rows, extra), 1)
    wide_ref[...] = query_ref[...].astype(jnp.float32)
    pairs = [(row, group) for row in range(rows) for group in range(KV_HEADS)]
    heads = [pl.ds(group * per_group * rows + row, per_group, rows) for row, group in pairs]
    cols = [slice(group * HEAD_DIM, (group + 1) * HEAD_DIM) for _, group in pairs]
    queries = [wide_ref[at, :].astype(jnp.bfloat16) for at in heads]
    scores = [
        lax.dot_general(q, key_ref[row, :, c], (((1,), (1,)), ((), ())), preferred_element_type=jnp.float32)
        for q, c, (row, _) in zip(queries, cols, pairs)
    ]
    scores = jnp.stack(scores).reshape(rows, KV_HEADS * per_group, seg_len) * HEAD_DIM ** (-0.5)
    copies[0].wait()
    usable = jnp.stack([place < length_ref[row] for row in range(rows)])
    peak = jnp.max(jnp.where(usable, scores, -1e30), axis=-1, keepdims=True)
    weights = jnp.where(usable, jnp.exp(scores - peak), 0.0).astype(jnp.bfloat16)
    total = jnp.sum(weights.astype(jnp.float32), axis=-1, keepdims=True)
    some = total > 0.0
    safe = jnp.where(some, total, 1.0)
    logs = jnp.where(some, peak + jnp.log(safe), -1e30)
    parts = [slice(group * per_group, (group + 1) * per_group) for _, group in pairs]
    accs = [
        jnp.dot(weights[row, part], value_ref[row, :, c], preferred_element_type=jnp.float32)
        for part, c, (row, _) in zip(parts, cols, pairs)
    ]
    for acc, part, at, (row, _) in zip(accs, parts, heads, pairs):
        mean_ref[at, :] = acc / safe[row, part]
        logs_ref[at, :] = jnp.broadcast_to(logs[row, part], acc.shape)
    if own >= HEAD_DIM:
        for dest in range(HEADS // per_dest):
            stats = jnp.zeros((rows, extra - own), jnp.float32)
            for slot in range(per_dest):
                at = slice((dest * per_dest + slot) * rows, (dest * per_dest + slot + 1) * rows)
                dest_ref[dest, :, slot * HEAD_DIM : (slot + 1) * HEAD_DIM] = mean_ref[at, :]
                for number, part in enumerate(coded_log(logs_ref[at, :1])):
                    stats = jnp.where(lane[:, own:] == own + 3 * slot + number, part, stats)
            dest_ref[dest, :, own:] = stats
    else:
        for head in range(HEADS):
            mean, logs = mean_ref[head * rows : (head + 1) * rows, :], logs_ref[head * rows : (head + 1) * rows, :1]
            for half in range(HEAD_DIM // own):
                moved = mean if half == 0 else pltpu.roll(mean, HEAD_DIM - half * own, 1)
                block = jnp.where(lane < own, moved, 0.0)
                for number, part in enumerate(coded_log(logs)):
                    block = jnp.where(lane == own + number, part, block)
                dest_ref[head * (HEAD_DIM // own) + half] = block
    for out_ref, core in ((near_ref, 0), (far_ref, 1)):
        for first in range(0, len(offsets), 2):
            pair = [dest_ref[me ^ (offset ^ core)] for offset in offsets[first : first + 2]]
            out_ref[first * rows : (first + 2) * rows] = jnp.concatenate(pair, axis=0).astype(jnp.bfloat16)
    copies[1].wait()


def attend(stacked, k_cache, v_cache, cache_len, levels, weight):
    devices = lax.axis_size("ffn")
    rows, _, _ = k_cache.shape
    own = HEADS * HEAD_DIM // devices
    extra = -(-(own + 3 * max(1, own // HEAD_DIM)) // LANES) * LANES
    offsets = offsets_of(levels)
    out = jax.ShapeDtypeStruct((len(offsets) * rows, extra), jnp.bfloat16)
    return call(
        functools.partial(attention_kernel, own, offsets),
        [out, out, pltpu.VMEM(weight.shape, weight.dtype)],
        [*in_hbm(cache_len, weight), stacked, k_cache, v_cache],
        in_specs=[HBM] * 2 + [VMEM] * 3,
        scratch=[
            pltpu.SMEM(cache_len.shape, cache_len.dtype),
            *[pltpu.VMEM(stacked.shape, jnp.float32)] * 3,
            pltpu.VMEM((devices, rows, extra), jnp.float32),
            fetched(2),
        ],
        flops=4 * 10**9,
    )


def expert_kernel(experts, chunks, *refs):
    count = len(chunks)
    same_refs, other_refs, refs = refs[:count], refs[count : 2 * count], refs[2 * count :]
    near_ref, far_ref, gate_ref, up_ref, down_ref, own_out, far_out = refs
    width = gate_ref.shape[0]
    rows = same_refs[0].shape[0]
    coded = jnp.concatenate([r[:, width:] for r in same_refs + other_refs], axis=0).astype(jnp.float32)
    lane = lax.broadcasted_iota(jnp.int32, coded.shape, 1)
    mine = (lane < 2 * experts) & (lane % experts == lax.axis_index("ffn") // 2)
    share = jnp.sum(jnp.where(mine, coded, 0.0), axis=-1, keepdims=True)
    for place, chunk in enumerate(chunks):
        at, here = slice(place * rows, (place + 1) * rows), slice(chunk * rows, (chunk + 1) * rows)
        own_out[at, width:] = near_ref[here]
        far_out[at, width:] = far_ref[here]
    stacked = jnp.concatenate([r[:, :width] for r in same_refs + other_refs], axis=0)
    gate_part = jnp.dot(stacked, gate_ref[...], preferred_element_type=jnp.float32)
    up_part = jnp.dot(stacked, up_ref[...], preferred_element_type=jnp.float32)
    hidden = (gate_part / (1.0 + jnp.exp(-gate_part)) * up_part).astype(jnp.bfloat16)
    step = 1024
    for first in range(0, width, step):
        at = slice(first, first + step)
        part = jnp.dot(hidden, down_ref[:, at], preferred_element_type=jnp.float32)
        part = (part * share).astype(jnp.bfloat16)
        own_out[:, at] = part[: count * rows]
        far_out[:, at] = part[count * rows :]


def apply_expert(same, other, chunks, sums, weights):
    rows = same[0].shape[0]
    width, hidden = weights[0].shape
    devices = lax.axis_size("ffn")
    shape = jax.ShapeDtypeStruct((len(same) * rows, width + sums[0].shape[1]), jnp.bfloat16)
    args = [*same, *other, *sums, *weights]
    return call(
        functools.partial(expert_kernel, devices // 2, chunks),
        [shape, shape],
        args,
        flops=4 * 10**9,
        nbytes=2 * 3 * width * hidden,
        mib=8 + sum(2 * a.size for a in args) // 2**20,
    )


def merged(own, parts):
    heads, piece = max(1, own // HEAD_DIM), min(own, HEAD_DIM)
    lane = lax.broadcasted_iota(jnp.int32, parts[0].shape, 1)
    result = jnp.zeros(parts[0].shape, jnp.float32)
    for head in range(heads):
        stat = (lane >= own + 3 * head) & (lane < own + 3 * head + 3)
        logs = [jnp.sum(jnp.where(stat, p, 0.0), axis=-1, keepdims=True) for p in parts]
        top = functools.reduce(jnp.maximum, logs)
        scales = [jnp.exp(log - top) for log in logs]
        total = sum(scales)
        mean = sum(p * s for p, s in zip(parts, scales)) / total
        result = jnp.where((lane >= head * piece) & (lane < (head + 1) * piece), mean, result)
        for place, part in enumerate(coded_log(top + jnp.log(total))):
            result = jnp.where(lane == own + 3 * head + place, part, result)
    return result


def sum_kernel(count, width, own, last, *refs):
    refs, outs = refs[:count], refs[count:]
    rows = refs[0].shape[0]
    step = min(rows, 16)
    for first in range(0, rows, step):
        at = slice(first, first + step)
        total = sum(ref[at, :width].astype(jnp.float32) for ref in refs)
        mean = merged(own, [ref[at, width:].astype(jnp.float32) for ref in refs])
        if last:
            outs[0][at] = total.astype(jnp.bfloat16)
            outs[1][at] = mean[:, :own].astype(jnp.bfloat16)
            continue
        start = 0
        for out_ref in outs:
            low, high = max(first, start), min(first + step, start + out_ref.shape[0])
            if low < high:
                here, part = slice(low - start, high - start), slice(low - first, high - first)
                out_ref[here, :width] = total[part].astype(jnp.bfloat16)
                out_ref[here, width:] = mean[part].astype(jnp.bfloat16)
            start += out_ref.shape[0]


def summed(parts, sizes, width, own, last=False, flops=1):
    rows, whole = parts[0].shape
    if last:
        shapes = [jax.ShapeDtypeStruct((rows, n), jnp.bfloat16) for n in (width, own)]
    else:
        shapes = [jax.ShapeDtypeStruct((n, whole), jnp.bfloat16) for n in sizes]
    return call(functools.partial(sum_kernel, len(parts), width, own, last), shapes, parts, flops=flops)


def stack_kernel(places, *refs):
    blocks = dict(zip(places, refs))
    stacked = jnp.concatenate([blocks[k][...].astype(jnp.float32) for k in range(len(places))], axis=0)
    refs[-1][...] = stacked.astype(jnp.bfloat16)


def start_order(radix):
    return [2, 3, 1] if radix == 4 else [1]


def gather(block, levels, *ready, flops=1):
    for stride, radix in reversed(levels):
        order = start_order(radix)
        arrived = [exchange(block, stride * k) for k in order]
        if ready:
            arrived = lax.optimization_barrier((*arrived, *ready))[: len(order)]
        rows, width = block.shape
        block = call(
            functools.partial(stack_kernel, [0] + order),
            jax.ShapeDtypeStruct((radix * rows, width), jnp.bfloat16),
            [block, *arrived],
            flops=flops,
        )
    return block


def scatter(pieces, levels, width, own):
    stride, radix = levels[0]
    parts = [pieces[0]] + [exchange(pieces[k], stride * k) for k in start_order(radix)]
    if len(levels) == 1:
        return parts
    rows = parts[0].shape[0] // levels[1][1]
    return scatter(summed(parts, [rows] * levels[1][1], width, own), levels[1:], width, own)


def per_device(
    tokens, norm_gain, routes, gate_scores, w_gate, w_up, w_down, query, k_cache, v_cache, cache_len
):
    rows_dev, width = tokens.shape
    devices = lax.axis_size("ffn")
    experts = devices // 2
    levels = levels_of(devices)
    own = query.shape[1] // devices
    extra = -(-2 * experts // LANES) * LANES
    block = call(
        functools.partial(payload_kernel, experts),
        jax.ShapeDtypeStruct((rows_dev, width + extra), jnp.bfloat16),
        in_hbm(tokens, norm_gain[None], routes, gate_scores),
        in_specs=[HBM] * 4,
        scratch=[pltpu.VMEM(a.shape, a.dtype) for a in (tokens, norm_gain[None], routes, gate_scores)]
        + [fetched(4)],
    )
    (stride, radix), *outer = levels
    corner = 3 * stride
    rows = rows_dev * (devices // (2 * radix))
    cut = [rows // outer[0][1]] * outer[0][1]
    across = [exchange(block, corner)] if radix == 4 else []
    stacked = query.reshape(-1, HEADS, HEAD_DIM).transpose(1, 0, 2).reshape(-1, HEAD_DIM)
    w_gate, stacked, k_cache, v_cache = keep(w_gate, stacked, k_cache, v_cache)
    base = gather(block, outer, w_gate)
    sides = [1, 2] if radix == 4 else [1]
    chunks = [exchange(base, stride * k) for k in sides]
    *sums, w_up = attend(after(stacked, base), k_cache, v_cache, cache_len, levels, w_up)
    weights = (w_gate, w_up, w_down)
    last_chunk = [gather(a, outer, sums[0], flops=25 * 10**8) for a in across]
    count = len(sides)
    chunks = lax.optimization_barrier((*chunks, sums[0]))[:count]
    others = [exchange(c, 1) for c in (*chunks, base, *last_chunk)]
    chunks = lax.optimization_barrier((*chunks, *last_chunk))[:count]
    near, far = apply_expert(chunks, others[:count], sides, sums, weights)
    pieces = summed([near, exchange(far, 1)], [rows] * count, width, own)
    base = after(base, near)
    near, far = apply_expert([base, *last_chunk], others[count:], [0, 3][: radix - 2], sums, weights)
    total, *corner_pieces = summed([near, exchange(far, 1)], [rows] + cut * len(across), width, own)
    parts = [total] + [exchange(piece, stride * k) for piece, k in zip(pieces, sides)]
    if across:
        corner_parts = scatter(corner_pieces, outer, width, own)
    pieces = summed(parts, cut, width, own)
    last = scatter(pieces, outer, width, own)
    if across:
        corner_parts = lax.optimization_barrier((*corner_parts, pieces[0]))[:-1]
        (corner_sum,) = summed(corner_parts, [rows_dev], width, own)
        last.append(exchange(corner_sum, corner))
    if across:
        (most,) = summed(last[:-1], [rows_dev], width, own, flops=10**9)
        last = [most, last[-1]]
    return tuple(summed(last, [], width, own, last=True))


def solution(mesh):
    in_specs = (
        P(("groups", "ffn"), None),
        P(),
        P(("groups", "ffn"), None),
        P(("groups", "ffn"), None),
        P(None, "ffn"),
        P(None, "ffn"),
        P("ffn", None),
        P("groups", None),
        P("groups", "ffn", None),
        P("groups", "ffn", None),
        P("groups"),
    )
    out_specs = (P(("groups", "ffn"), None), P("groups", "ffn"))
    return jax.shard_map(
        per_device, mesh=mesh, in_specs=in_specs, out_specs=out_specs, check_vma=False
    )
```

```python
import functools

import jax
import jax.numpy as jnp
from jax import lax
from jax.experimental import pallas as pl
from jax.experimental.pallas import tpu as pltpu
from jax.sharding import PartitionSpec as P

HEADS = 64
KV_HEADS = 4
HEAD_DIM = 128
LANES = 128
STRIPS = 4
VMEM = pl.BlockSpec(memory_space=pltpu.VMEM)
SMEM = pl.BlockSpec(memory_space=pltpu.SMEM)
HBM = pl.BlockSpec(memory_space=pltpu.HBM)


def levels_of(devices):
    levels, stride = [], 2
    while stride < devices:
        radix = 4 if devices // stride >= 4 else 2
        levels.append((stride, radix))
        stride *= radix
    return levels


def offsets_of(levels):
    offsets = [0]
    for stride, radix in reversed(levels):
        offsets = [stride * k ^ low for k in range(radix) for low in offsets]
    return offsets


def exchange(value, distance):
    size = lax.axis_size("ffn")
    return lax.ppermute(value, "ffn", [(i, i ^ distance) for i in range(size)])


def after(value, *others):
    return lax.optimization_barrier((value, *others))[0]


def call(body, out_shape, args, in_specs=None, scratch=(), flops=1, nbytes=1, mib=16):
    return pl.pallas_call(
        body,
        out_shape=out_shape,
        in_specs=in_specs or [VMEM] * len(args),
        out_specs=jax.tree.map(lambda _: VMEM, out_shape),
        scratch_shapes=list(scratch),
        compiler_params=pltpu.CompilerParams(vmem_limit_bytes=mib * 2**20),
        cost_estimate=pl.CostEstimate(flops=flops, bytes_accessed=nbytes, transcendentals=0),
    )(*args)


def in_hbm(*arrays):
    return [pltpu.with_memory_space_constraint(array, pltpu.HBM) for array in arrays]


def fetched(count):
    return pltpu.SemaphoreType.DMA((count,))


def fetch(sources, targets, sems):
    copies = [pltpu.make_async_copy(s, t, sems.at[i]) for i, (s, t) in enumerate(zip(sources, targets))]
    for copy in copies:
        copy.start()
    return copies


def strips(ref, count):
    rows = ref.shape[0] // count
    return [ref.at[pl.ds(first * rows, rows)] for first in range(count)]


def payload_kernel(
    experts, tokens_hbm, gain_hbm, routes_hbm, scores_hbm, out_ref, tokens_ref, gain_ref, routes_ref, scores_ref, sems
):
    copies = fetch(
        [tokens_hbm, gain_hbm, routes_hbm, scores_hbm], [tokens_ref, gain_ref, routes_ref, scores_ref], sems
    )
    for copy in copies:
        copy.wait()
    features = tokens_ref[...].astype(jnp.float32)
    width = features.shape[1]
    mean_square = jnp.mean(features * features, axis=-1, keepdims=True)
    normed = features * lax.rsqrt(mean_square + 1e-06) * gain_ref[...]
    scores = scores_ref[...]
    share = scores / jnp.sum(scores, axis=-1, keepdims=True)
    extra = out_ref.shape[1] - width
    lane = lax.broadcasted_iota(jnp.int32, (features.shape[0], extra), 1)
    routes = routes_ref[...]
    gates = jnp.zeros(lane.shape, jnp.float32)
    for choice in range(routes.shape[1]):
        gates += jnp.where(
            routes[:, choice : choice + 1] == lane % experts, share[:, choice : choice + 1], 0.0
        )
    high = gates.astype(jnp.bfloat16).astype(jnp.float32)
    coded = jnp.where(lane < experts, high, jnp.where(lane < 2 * experts, gates - high, 0.0))
    out_ref[:, :width] = normed.astype(jnp.bfloat16)
    out_ref[:, width:] = coded.astype(jnp.bfloat16)


def coded_log(value):
    high = value.astype(jnp.bfloat16).astype(jnp.float32)
    middle = (value - high).astype(jnp.bfloat16).astype(jnp.float32)
    return [high, middle, value - high - middle]


def keep_kernel(cuts, *refs):
    count = len(cuts)
    sources = sum([strips(ref, cut) for ref, cut in zip(refs, cuts)], [])
    targets = sum([strips(ref, cut) for ref, cut in zip(refs[count:], cuts)], [])
    copies = fetch(sources, targets, refs[2 * count])
    for copy in copies:
        copy.wait()


def keep(*arrays):
    cuts = [STRIPS if a.size >= 2**20 else 1 for a in arrays]
    return call(
        functools.partial(keep_kernel, cuts),
        [pltpu.VMEM(a.shape, a.dtype) for a in arrays],
        in_hbm(*arrays),
        in_specs=[HBM] * len(arrays),
        scratch=[fetched(sum(cuts))],
        flops=4 * 10**9,
    )


def attention_kernel(own, offsets, *refs):
    length_hbm, weight_hbm, query_ref, key_ref, value_ref, near_ref, far_ref, weight_out = refs[:8]
    length_ref, wide_ref, mean_ref, logs_ref, dest_ref, sems = refs[8:]
    sources = [length_hbm, *strips(weight_hbm, STRIPS)]
    copies = fetch(sources, [length_ref, *strips(weight_out, STRIPS)], sems)
    me = lax.axis_index("ffn")
    rows, seg_len, _ = key_ref.shape
    per_group = HEADS // KV_HEADS
    place = lax.broadcasted_iota(jnp.int32, (KV_HEADS * per_group, seg_len), 1) + me * seg_len
    per_dest = max(1, own // HEAD_DIM)
    extra = near_ref.shape[1]
    lane = lax.broadcasted_iota(jnp.int32, (rows, extra), 1)
    wide_ref[...] = query_ref[...].astype(jnp.float32)
    pairs = [(row, group) for row in range(rows) for group in range(KV_HEADS)]
    heads = [pl.ds(group * per_group * rows + row, per_group, rows) for row, group in pairs]
    cols = [slice(group * HEAD_DIM, (group + 1) * HEAD_DIM) for _, group in pairs]
    queries = [wide_ref[at, :].astype(jnp.bfloat16) for at in heads]
    scores = [
        lax.dot_general(q, key_ref[row, :, c], (((1,), (1,)), ((), ())), preferred_element_type=jnp.float32)
        for q, c, (row, _) in zip(queries, cols, pairs)
    ]
    scores = jnp.stack(scores).reshape(rows, KV_HEADS * per_group, seg_len) * HEAD_DIM ** (-0.5)
    copies[0].wait()
    usable = jnp.stack([place < length_ref[row] for row in range(rows)])
    peak = jnp.max(jnp.where(usable, scores, -1e30), axis=-1, keepdims=True)
    weights = jnp.where(usable, jnp.exp(scores - peak), 0.0).astype(jnp.bfloat16)
    total = jnp.sum(weights.astype(jnp.float32), axis=-1, keepdims=True)
    some = total > 0.0
    safe = jnp.where(some, total, 1.0)
    logs = jnp.where(some, peak + jnp.log(safe), -1e30)
    parts = [slice(group * per_group, (group + 1) * per_group) for _, group in pairs]
    accs = [
        jnp.dot(weights[row, part], value_ref[row, :, c], preferred_element_type=jnp.float32)
        for part, c, (row, _) in zip(parts, cols, pairs)
    ]
    for acc, part, at, (row, _) in zip(accs, parts, heads, pairs):
        mean_ref[at, :] = acc / safe[row, part]
        logs_ref[at, :] = jnp.broadcast_to(logs[row, part], acc.shape)
    if own >= HEAD_DIM:
        for dest in range(HEADS // per_dest):
            stats = jnp.zeros((rows, extra - own), jnp.float32)
            for slot in range(per_dest):
                at = slice((dest * per_dest + slot) * rows, (dest * per_dest + slot + 1) * rows)
                dest_ref[dest, :, slot * HEAD_DIM : (slot + 1) * HEAD_DIM] = mean_ref[at, :]
                for number, part in enumerate(coded_log(logs_ref[at, :1])):
                    stats = jnp.where(lane[:, own:] == own + 3 * slot + number, part, stats)
            dest_ref[dest, :, own:] = stats
    else:
        for head in range(HEADS):
            mean, logs = mean_ref[head * rows : (head + 1) * rows, :], logs_ref[head * rows : (head + 1) * rows, :1]
            for half in range(HEAD_DIM // own):
                moved = mean if half == 0 else pltpu.roll(mean, HEAD_DIM - half * own, 1)
                block = jnp.where(lane < own, moved, 0.0)
                for number, part in enumerate(coded_log(logs)):
                    block = jnp.where(lane == own + number, part, block)
                dest_ref[head * (HEAD_DIM // own) + half] = block
    for out_ref, core in ((near_ref, 0), (far_ref, 1)):
        for first in range(0, len(offsets), 2):
            pair = [dest_ref[me ^ (offset ^ core)] for offset in offsets[first : first + 2]]
            out_ref[first * rows : (first + 2) * rows] = jnp.concatenate(pair, axis=0).astype(jnp.bfloat16)
    for copy in copies[1:]:
        copy.wait()


def attend(stacked, k_cache, v_cache, cache_len, levels, weight):
    devices = lax.axis_size("ffn")
    rows, _, _ = k_cache.shape
    own = HEADS * HEAD_DIM // devices
    extra = -(-(own + 3 * max(1, own // HEAD_DIM)) // LANES) * LANES
    offsets = offsets_of(levels)
    out = jax.ShapeDtypeStruct((len(offsets) * rows, extra), jnp.bfloat16)
    return call(
        functools.partial(attention_kernel, own, offsets),
        [out, out, pltpu.VMEM(weight.shape, weight.dtype)],
        [*in_hbm(cache_len, weight), stacked, k_cache, v_cache],
        in_specs=[HBM] * 2 + [VMEM] * 3,
        scratch=[
            pltpu.SMEM(cache_len.shape, cache_len.dtype),
            *[pltpu.VMEM(stacked.shape, jnp.float32)] * 3,
            pltpu.VMEM((devices, rows, extra), jnp.float32),
            fetched(1 + STRIPS),
        ],
        flops=4 * 10**9,
    )


def expert_kernel(experts, chunks, *refs):
    count = len(chunks)
    same_refs, other_refs, refs = refs[:count], refs[count : 2 * count], refs[2 * count :]
    near_ref, far_ref, gate_ref, up_ref, down_ref, own_out, far_out = refs
    width = gate_ref.shape[0]
    rows = same_refs[0].shape[0]
    coded = jnp.concatenate([r[:, width:] for r in same_refs + other_refs], axis=0).astype(jnp.float32)
    lane = lax.broadcasted_iota(jnp.int32, coded.shape, 1)
    mine = (lane < 2 * experts) & (lane % experts == lax.axis_index("ffn") // 2)
    share = jnp.sum(jnp.where(mine, coded, 0.0), axis=-1, keepdims=True)
    for place, chunk in enumerate(chunks):
        at, here = slice(place * rows, (place + 1) * rows), slice(chunk * rows, (chunk + 1) * rows)
        own_out[at, width:] = near_ref[here]
        far_out[at, width:] = far_ref[here]
    stacked = jnp.concatenate([r[:, :width] for r in same_refs + other_refs], axis=0)
    gate_part = jnp.dot(stacked, gate_ref[...], preferred_element_type=jnp.float32)
    up_part = jnp.dot(stacked, up_ref[...], preferred_element_type=jnp.float32)
    hidden = (gate_part / (1.0 + jnp.exp(-gate_part)) * up_part).astype(jnp.bfloat16)
    step = 1024
    for first in range(0, width, step):
        at = slice(first, first + step)
        part = jnp.dot(hidden, down_ref[:, at], preferred_element_type=jnp.float32)
        part = (part * share).astype(jnp.bfloat16)
        own_out[:, at] = part[: count * rows]
        far_out[:, at] = part[count * rows :]


def apply_expert(same, other, chunks, sums, weights):
    rows = same[0].shape[0]
    width, hidden = weights[0].shape
    devices = lax.axis_size("ffn")
    shape = jax.ShapeDtypeStruct((len(same) * rows, width + sums[0].shape[1]), jnp.bfloat16)
    args = [*same, *other, *sums, *weights]
    return call(
        functools.partial(expert_kernel, devices // 2, chunks),
        [shape, shape],
        args,
        flops=4 * 10**9,
        nbytes=2 * 3 * width * hidden,
        mib=8 + sum(2 * a.size for a in args) // 2**20,
    )


def merged(own, parts):
    heads, piece = max(1, own // HEAD_DIM), min(own, HEAD_DIM)
    lane = lax.broadcasted_iota(jnp.int32, parts[0].shape, 1)
    result = jnp.zeros(parts[0].shape, jnp.float32)
    for head in range(heads):
        stat = (lane >= own + 3 * head) & (lane < own + 3 * head + 3)
        logs = [jnp.sum(jnp.where(stat, p, 0.0), axis=-1, keepdims=True) for p in parts]
        top = functools.reduce(jnp.maximum, logs)
        scales = [jnp.exp(log - top) for log in logs]
        total = sum(scales)
        mean = sum(p * s for p, s in zip(parts, scales)) / total
        result = jnp.where((lane >= head * piece) & (lane < (head + 1) * piece), mean, result)
        for place, part in enumerate(coded_log(top + jnp.log(total))):
            result = jnp.where(lane == own + 3 * head + place, part, result)
    return result


def sum_kernel(count, width, own, last, *refs):
    refs, outs = refs[:count], refs[count:]
    rows = refs[0].shape[0]
    step = min(rows, 16)
    for first in range(0, rows, step):
        at = slice(first, first + step)
        total = sum(ref[at, :width].astype(jnp.float32) for ref in refs)
        mean = merged(own, [ref[at, width:].astype(jnp.float32) for ref in refs])
        if last:
            outs[0][at] = total.astype(jnp.bfloat16)
            outs[1][at] = mean[:, :own].astype(jnp.bfloat16)
            continue
        start = 0
        for out_ref in outs:
            low, high = max(first, start), min(first + step, start + out_ref.shape[0])
            if low < high:
                here, part = slice(low - start, high - start), slice(low - first, high - first)
                out_ref[here, :width] = total[part].astype(jnp.bfloat16)
                out_ref[here, width:] = mean[part].astype(jnp.bfloat16)
            start += out_ref.shape[0]


def summed(parts, sizes, width, own, last=False, flops=1):
    rows, whole = parts[0].shape
    if last:
        shapes = [jax.ShapeDtypeStruct((rows, n), jnp.bfloat16) for n in (width, own)]
    else:
        shapes = [jax.ShapeDtypeStruct((n, whole), jnp.bfloat16) for n in sizes]
    return call(functools.partial(sum_kernel, len(parts), width, own, last), shapes, parts, flops=flops)


def stack_kernel(places, *refs):
    blocks = dict(zip(places, refs))
    stacked = jnp.concatenate([blocks[k][...].astype(jnp.float32) for k in range(len(places))], axis=0)
    refs[-1][...] = stacked.astype(jnp.bfloat16)


def start_order(radix):
    return [2, 3, 1] if radix == 4 else [1]


def gather(block, levels, *ready, flops=1):
    for stride, radix in reversed(levels):
        order = start_order(radix)
        arrived = [exchange(block, stride * k) for k in order]
        if ready:
            arrived = lax.optimization_barrier((*arrived, *ready))[: len(order)]
        rows, width = block.shape
        block = call(
            functools.partial(stack_kernel, [0] + order),
            jax.ShapeDtypeStruct((radix * rows, width), jnp.bfloat16),
            [block, *arrived],
            flops=flops,
        )
    return block


def scatter(pieces, levels, width, own):
    stride, radix = levels[0]
    parts = [pieces[0]] + [exchange(pieces[k], stride * k) for k in start_order(radix)]
    if len(levels) == 1:
        return parts
    rows = parts[0].shape[0] // levels[1][1]
    return scatter(summed(parts, [rows] * levels[1][1], width, own), levels[1:], width, own)


def per_device(
    tokens, norm_gain, routes, gate_scores, w_gate, w_up, w_down, query, k_cache, v_cache, cache_len
):
    rows_dev, width = tokens.shape
    devices = lax.axis_size("ffn")
    experts = devices // 2
    levels = levels_of(devices)
    own = query.shape[1] // devices
    extra = -(-2 * experts // LANES) * LANES
    block = call(
        functools.partial(payload_kernel, experts),
        jax.ShapeDtypeStruct((rows_dev, width + extra), jnp.bfloat16),
        in_hbm(tokens, norm_gain[None], routes, gate_scores),
        in_specs=[HBM] * 4,
        scratch=[pltpu.VMEM(a.shape, a.dtype) for a in (tokens, norm_gain[None], routes, gate_scores)]
        + [fetched(4)],
    )
    (stride, radix), *outer = levels
    corner = 3 * stride
    rows = rows_dev * (devices // (2 * radix))
    cut = [rows // outer[0][1]] * outer[0][1]
    across = [exchange(block, corner)] if radix == 4 else []
    stacked = query.reshape(-1, HEADS, HEAD_DIM).transpose(1, 0, 2).reshape(-1, HEAD_DIM)
    w_gate, stacked, k_cache, v_cache = keep(w_gate, stacked, k_cache, v_cache)
    base = gather(block, outer, w_gate)
    sides = [1, 2] if radix == 4 else [1]
    chunks = [exchange(base, stride * k) for k in sides]
    *sums, w_up = attend(after(stacked, base), k_cache, v_cache, cache_len, levels, w_up)
    weights = (w_gate, w_up, w_down)
    last_chunk = [gather(a, outer, sums[0], flops=25 * 10**8) for a in across]
    count = len(sides)
    chunks = lax.optimization_barrier((*chunks, sums[0]))[:count]
    others = [exchange(c, 1) for c in (*chunks, base, *last_chunk)]
    chunks = lax.optimization_barrier((*chunks, *last_chunk))[:count]
    near, far = apply_expert(chunks, others[:count], sides, sums, weights)
    pieces = summed([near, exchange(far, 1)], [rows] * count, width, own)
    base = after(base, near)
    near, far = apply_expert([base, *last_chunk], others[count:], [0] + [3] * len(across), sums, weights)
    total, *corner_pieces = summed([near, exchange(far, 1)], [rows] + cut * len(across), width, own)
    parts = [total] + [exchange(piece, stride * k) for piece, k in zip(pieces, sides)]
    if across:
        corner_parts = scatter(corner_pieces, outer, width, own)
    pieces = summed(parts, cut, width, own)
    last = scatter(pieces, outer, width, own)
    if across:
        corner_parts = lax.optimization_barrier((*corner_parts, pieces[0]))[:-1]
        (corner_sum,) = summed(corner_parts, [rows_dev], width, own)
        last.append(exchange(corner_sum, corner))
    if across:
        (most,) = summed(last[:-1], [rows_dev], width, own, flops=10**9)
        last = [most, last[-1]]
    return tuple(summed(last, [], width, own, last=True))


def solution(mesh):
    in_specs = (
        P(("groups", "ffn"), None),
        P(),
        P(("groups", "ffn"), None),
        P(("groups", "ffn"), None),
        P(None, "ffn"),
        P(None, "ffn"),
        P("ffn", None),
        P("groups", None),
        P("groups", "ffn", None),
        P("groups", "ffn", None),
        P("groups"),
    )
    out_specs = (P(("groups", "ffn"), None), P("groups", "ffn"))
    return jax.shard_map(
        per_device, mesh=mesh, in_specs=in_specs, out_specs=out_specs, check_vma=False
    )
```

```python
import functools

import jax
import jax.numpy as jnp
from jax import lax
from jax.experimental import pallas as pl
from jax.experimental.pallas import tpu as pltpu
from jax.sharding import PartitionSpec as P

HEADS = 64
KV_HEADS = 4
HEAD_DIM = 128
LANES = 128
STRIPS = 4
VMEM = pl.BlockSpec(memory_space=pltpu.VMEM)
SMEM = pl.BlockSpec(memory_space=pltpu.SMEM)
HBM = pl.BlockSpec(memory_space=pltpu.HBM)


def levels_of(devices):
    levels, stride = [], 2
    while stride < devices:
        radix = 4 if devices // stride >= 4 else 2
        levels.append((stride, radix))
        stride *= radix
    return levels


def offsets_of(levels):
    offsets = [0]
    for stride, radix in reversed(levels):
        offsets = [stride * k ^ low for k in range(radix) for low in offsets]
    return offsets


def exchange(value, distance):
    size = lax.axis_size("ffn")
    return lax.ppermute(value, "ffn", [(i, i ^ distance) for i in range(size)])


def after(value, *others):
    return lax.optimization_barrier((value, *others))[0]


def call(body, out_shape, args, in_specs=None, scratch=(), flops=1, nbytes=1, mib=16):
    return pl.pallas_call(
        body,
        out_shape=out_shape,
        in_specs=in_specs or [VMEM] * len(args),
        out_specs=jax.tree.map(lambda _: VMEM, out_shape),
        scratch_shapes=list(scratch),
        compiler_params=pltpu.CompilerParams(vmem_limit_bytes=mib * 2**20),
        cost_estimate=pl.CostEstimate(flops=flops, bytes_accessed=nbytes, transcendentals=0),
    )(*args)


def in_hbm(*arrays):
    return [pltpu.with_memory_space_constraint(array, pltpu.HBM) for array in arrays]


def fetched(count):
    return pltpu.SemaphoreType.DMA((count,))


def fetch(sources, targets, sems):
    copies = [pltpu.make_async_copy(s, t, sems.at[i]) for i, (s, t) in enumerate(zip(sources, targets))]
    for copy in copies:
        copy.start()
    return copies


def strips(ref, count):
    rows = ref.shape[0] // count
    return [ref.at[pl.ds(first * rows, rows)] for first in range(count)]


def payload_kernel(
    experts, tokens_hbm, gain_hbm, routes_hbm, scores_hbm, out_ref, tokens_ref, gain_ref, routes_ref, scores_ref, sems
):
    copies = fetch(
        [tokens_hbm, gain_hbm, routes_hbm, scores_hbm], [tokens_ref, gain_ref, routes_ref, scores_ref], sems
    )
    for copy in copies:
        copy.wait()
    features = tokens_ref[...].astype(jnp.float32)
    width = features.shape[1]
    mean_square = jnp.mean(features * features, axis=-1, keepdims=True)
    normed = features * lax.rsqrt(mean_square + 1e-06) * gain_ref[...]
    scores = scores_ref[...]
    share = scores / jnp.sum(scores, axis=-1, keepdims=True)
    extra = out_ref.shape[1] - width
    lane = lax.broadcasted_iota(jnp.int32, (features.shape[0], extra), 1)
    routes = routes_ref[...]
    gates = jnp.zeros(lane.shape, jnp.float32)
    for choice in range(routes.shape[1]):
        gates += jnp.where(
            routes[:, choice : choice + 1] == lane % experts, share[:, choice : choice + 1], 0.0
        )
    high = gates.astype(jnp.bfloat16).astype(jnp.float32)
    coded = jnp.where(lane < experts, high, jnp.where(lane < 2 * experts, gates - high, 0.0))
    out_ref[:, :width] = normed.astype(jnp.bfloat16)
    out_ref[:, width:] = coded.astype(jnp.bfloat16)


def coded_log(value):
    high = value.astype(jnp.bfloat16).astype(jnp.float32)
    middle = (value - high).astype(jnp.bfloat16).astype(jnp.float32)
    return [high, middle, value - high - middle]


def keep_kernel(cuts, *refs):
    count = len(cuts)
    sources = sum([strips(ref, cut) for ref, cut in zip(refs, cuts)], [])
    targets = sum([strips(ref, cut) for ref, cut in zip(refs[count:], cuts)], [])
    copies = fetch(sources, targets, refs[2 * count])
    for copy in copies:
        copy.wait()


def keep(*arrays):
    cuts = [STRIPS if a.size >= 2**20 else 1 for a in arrays]
    return call(
        functools.partial(keep_kernel, cuts),
        [pltpu.VMEM(a.shape, a.dtype) for a in arrays],
        in_hbm(*arrays),
        in_specs=[HBM] * len(arrays),
        scratch=[fetched(sum(cuts))],
        flops=4 * 10**9,
    )


def attention_kernel(own, offsets, *refs):
    length_hbm, weight_hbm, query_ref, key_ref, value_ref, near_ref, far_ref, weight_out = refs[:8]
    length_ref, wide_ref, mean_ref, logs_ref, dest_ref, sems = refs[8:]
    sources = [length_hbm, *strips(weight_hbm, STRIPS)]
    copies = fetch(sources, [length_ref, *strips(weight_out, STRIPS)], sems)
    me = lax.axis_index("ffn")
    rows, seg_len, _ = key_ref.shape
    per_group = HEADS // KV_HEADS
    place = lax.broadcasted_iota(jnp.int32, (KV_HEADS * per_group, seg_len), 1) + me * seg_len
    per_dest = max(1, own // HEAD_DIM)
    extra = near_ref.shape[1]
    lane = lax.broadcasted_iota(jnp.int32, (rows, extra), 1)
    wide_ref[...] = query_ref[...].astype(jnp.float32)
    pairs = [(row, group) for row in range(rows) for group in range(KV_HEADS)]
    heads = [pl.ds(group * per_group * rows + row, per_group, rows) for row, group in pairs]
    cols = [slice(group * HEAD_DIM, (group + 1) * HEAD_DIM) for _, group in pairs]
    queries = [wide_ref[at, :].astype(jnp.bfloat16) for at in heads]
    scores = [
        lax.dot_general(q, key_ref[row, :, c], (((1,), (1,)), ((), ())), preferred_element_type=jnp.float32)
        for q, c, (row, _) in zip(queries, cols, pairs)
    ]
    scores = jnp.stack(scores).reshape(rows, KV_HEADS * per_group, seg_len) * HEAD_DIM ** (-0.5)
    copies[0].wait()
    usable = jnp.stack([place < length_ref[row] for row in range(rows)])
    peak = jnp.max(jnp.where(usable, scores, -1e30), axis=-1, keepdims=True)
    weights = jnp.where(usable, jnp.exp(scores - peak), 0.0).astype(jnp.bfloat16)
    total = jnp.sum(weights.astype(jnp.float32), axis=-1, keepdims=True)
    some = total > 0.0
    safe = jnp.where(some, total, 1.0)
    logs = jnp.where(some, peak + jnp.log(safe), -1e30)
    parts = [slice(group * per_group, (group + 1) * per_group) for _, group in pairs]
    accs = [
        jnp.dot(weights[row, part], value_ref[row, :, c], preferred_element_type=jnp.float32)
        for part, c, (row, _) in zip(parts, cols, pairs)
    ]
    for acc, part, at, (row, _) in zip(accs, parts, heads, pairs):
        mean_ref[at, :] = acc / safe[row, part]
        logs_ref[at, :] = jnp.broadcast_to(logs[row, part], acc.shape)
    if own >= HEAD_DIM:
        for dest in range(HEADS // per_dest):
            stats = jnp.zeros((rows, extra - own), jnp.float32)
            for slot in range(per_dest):
                at = slice((dest * per_dest + slot) * rows, (dest * per_dest + slot + 1) * rows)
                dest_ref[dest, :, slot * HEAD_DIM : (slot + 1) * HEAD_DIM] = mean_ref[at, :]
                for number, part in enumerate(coded_log(logs_ref[at, :1])):
                    stats = jnp.where(lane[:, own:] == own + 3 * slot + number, part, stats)
            dest_ref[dest, :, own:] = stats
    else:
        for head in range(HEADS):
            mean, logs = mean_ref[head * rows : (head + 1) * rows, :], logs_ref[head * rows : (head + 1) * rows, :1]
            for half in range(HEAD_DIM // own):
                moved = mean if half == 0 else pltpu.roll(mean, HEAD_DIM - half * own, 1)
                block = jnp.where(lane < own, moved, 0.0)
                for number, part in enumerate(coded_log(logs)):
                    block = jnp.where(lane == own + number, part, block)
                dest_ref[head * (HEAD_DIM // own) + half] = block
    for out_ref, core in ((near_ref, 0), (far_ref, 1)):
        for first in range(0, len(offsets), 2):
            pair = [dest_ref[me ^ (offset ^ core)] for offset in offsets[first : first + 2]]
            out_ref[first * rows : (first + 2) * rows] = jnp.concatenate(pair, axis=0).astype(jnp.bfloat16)
    for copy in copies[1:]:
        copy.wait()


def attend(stacked, k_cache, v_cache, cache_len, levels, weight):
    devices = lax.axis_size("ffn")
    rows, _, _ = k_cache.shape
    own = HEADS * HEAD_DIM // devices
    extra = -(-(own + 3 * max(1, own // HEAD_DIM)) // LANES) * LANES
    offsets = offsets_of(levels)
    out = jax.ShapeDtypeStruct((len(offsets) * rows, extra), jnp.bfloat16)
    return call(
        functools.partial(attention_kernel, own, offsets),
        [out, out, pltpu.VMEM(weight.shape, weight.dtype)],
        [*in_hbm(cache_len, weight), stacked, k_cache, v_cache],
        in_specs=[HBM] * 2 + [VMEM] * 3,
        scratch=[
            pltpu.SMEM(cache_len.shape, cache_len.dtype),
            *[pltpu.VMEM(stacked.shape, jnp.float32)] * 3,
            pltpu.VMEM((devices, rows, extra), jnp.float32),
            fetched(1 + STRIPS),
        ],
        flops=4 * 10**9,
    )


def expert_kernel(experts, chunks, *refs):
    count = len(chunks)
    same_refs, other_refs, refs = refs[:count], refs[count : 2 * count], refs[2 * count :]
    near_ref, far_ref, gate_ref, up_ref, down_ref, own_out, far_out = refs
    width = gate_ref.shape[0]
    rows = same_refs[0].shape[0]
    coded = jnp.concatenate([r[:, width:] for r in same_refs + other_refs], axis=0).astype(jnp.float32)
    lane = lax.broadcasted_iota(jnp.int32, coded.shape, 1)
    mine = (lane < 2 * experts) & (lane % experts == lax.axis_index("ffn") // 2)
    share = jnp.sum(jnp.where(mine, coded, 0.0), axis=-1, keepdims=True)
    for place, chunk in enumerate(chunks):
        at, here = slice(place * rows, (place + 1) * rows), slice(chunk * rows, (chunk + 1) * rows)
        own_out[at, width:] = near_ref[here]
        far_out[at, width:] = far_ref[here]
    stacked = jnp.concatenate([r[:, :width] for r in same_refs + other_refs], axis=0)
    gate_part = jnp.dot(stacked, gate_ref[...], preferred_element_type=jnp.float32)
    up_part = jnp.dot(stacked, up_ref[...], preferred_element_type=jnp.float32)
    hidden = (gate_part / (1.0 + jnp.exp(-gate_part)) * up_part).astype(jnp.bfloat16)
    step = 1024
    for first in range(0, width, step):
        at = slice(first, first + step)
        part = jnp.dot(hidden, down_ref[:, at], preferred_element_type=jnp.float32)
        part = (part * share).astype(jnp.bfloat16)
        own_out[:, at] = part[: count * rows]
        far_out[:, at] = part[count * rows :]


def apply_expert(same, other, chunks, sums, weights):
    rows = same[0].shape[0]
    width, hidden = weights[0].shape
    devices = lax.axis_size("ffn")
    shape = jax.ShapeDtypeStruct((len(same) * rows, width + sums[0].shape[1]), jnp.bfloat16)
    args = [*same, *other, *sums, *weights]
    return call(
        functools.partial(expert_kernel, devices // 2, chunks),
        [shape, shape],
        args,
        flops=4 * 10**9,
        nbytes=2 * 3 * width * hidden,
        mib=8 + sum(2 * a.size for a in args) // 2**20,
    )


def merged(own, parts):
    heads, piece = max(1, own // HEAD_DIM), min(own, HEAD_DIM)
    lane = lax.broadcasted_iota(jnp.int32, parts[0].shape, 1)
    result = jnp.zeros(parts[0].shape, jnp.float32)
    for head in range(heads):
        stat = (lane >= own + 3 * head) & (lane < own + 3 * head + 3)
        logs = [jnp.sum(jnp.where(stat, p, 0.0), axis=-1, keepdims=True) for p in parts]
        top = functools.reduce(jnp.maximum, logs)
        scales = [jnp.exp(log - top) for log in logs]
        total = sum(scales)
        mean = sum(p * s for p, s in zip(parts, scales)) / total
        result = jnp.where((lane >= head * piece) & (lane < (head + 1) * piece), mean, result)
        for place, part in enumerate(coded_log(top + jnp.log(total))):
            result = jnp.where(lane == own + 3 * head + place, part, result)
    return result


def sum_kernel(count, width, own, last, *refs):
    refs, outs = refs[:count], refs[count:]
    rows = refs[0].shape[0]
    step = min(rows, 16)
    for first in range(0, rows, step):
        at = slice(first, first + step)
        total = sum(ref[at, :width].astype(jnp.float32) for ref in refs)
        mean = merged(own, [ref[at, width:].astype(jnp.float32) for ref in refs])
        if last:
            outs[0][at] = total.astype(jnp.bfloat16)
            outs[1][at] = mean[:, :own].astype(jnp.bfloat16)
            continue
        start = 0
        for out_ref in outs:
            low, high = max(first, start), min(first + step, start + out_ref.shape[0])
            if low < high:
                here, part = slice(low - start, high - start), slice(low - first, high - first)
                out_ref[here, :width] = total[part].astype(jnp.bfloat16)
                out_ref[here, width:] = mean[part].astype(jnp.bfloat16)
            start += out_ref.shape[0]


def summed(parts, sizes, width, own, last=False, flops=1):
    rows, whole = parts[0].shape
    if last:
        shapes = [jax.ShapeDtypeStruct((rows, n), jnp.bfloat16) for n in (width, own)]
    else:
        shapes = [jax.ShapeDtypeStruct((n, whole), jnp.bfloat16) for n in sizes]
    return call(functools.partial(sum_kernel, len(parts), width, own, last), shapes, parts, flops=flops)


def stack_kernel(places, *refs):
    blocks = dict(zip(places, refs))
    stacked = jnp.concatenate([blocks[k][...].astype(jnp.float32) for k in range(len(places))], axis=0)
    refs[-1][...] = stacked.astype(jnp.bfloat16)


def start_order(radix, order):
    return order if radix == 4 else [1]


def gather(block, levels, *ready, flops=1, order=[2, 3, 1]):
    for stride, radix in reversed(levels):
        order = start_order(radix, order)
        arrived = [exchange(block, stride * k) for k in order]
        if ready:
            arrived = lax.optimization_barrier((*arrived, *ready))[: len(order)]
        rows, width = block.shape
        block = call(
            functools.partial(stack_kernel, [0] + order),
            jax.ShapeDtypeStruct((radix * rows, width), jnp.bfloat16),
            [block, *arrived],
            flops=flops,
        )
    return block


def scatter(pieces, levels, width, own, order=[2, 3, 1]):
    stride, radix = levels[0]
    parts = [pieces[0]] + [exchange(pieces[k], stride * k) for k in start_order(radix, order)]
    if len(levels) == 1:
        return parts
    rows = parts[0].shape[0] // levels[1][1]
    return scatter(summed(parts, [rows] * levels[1][1], width, own), levels[1:], width, own, order)


def per_device(
    tokens, norm_gain, routes, gate_scores, w_gate, w_up, w_down, query, k_cache, v_cache, cache_len
):
    rows_dev, width = tokens.shape
    devices = lax.axis_size("ffn")
    experts = devices // 2
    levels = levels_of(devices)
    own = query.shape[1] // devices
    extra = -(-2 * experts // LANES) * LANES
    block = call(
        functools.partial(payload_kernel, experts),
        jax.ShapeDtypeStruct((rows_dev, width + extra), jnp.bfloat16),
        in_hbm(tokens, norm_gain[None], routes, gate_scores),
        in_specs=[HBM] * 4,
        scratch=[pltpu.VMEM(a.shape, a.dtype) for a in (tokens, norm_gain[None], routes, gate_scores)]
        + [fetched(4)],
    )
    (stride, radix), *outer = levels
    corner = 3 * stride
    rows = rows_dev * (devices // (2 * radix))
    cut = [rows // outer[0][1]] * outer[0][1]
    across = [exchange(block, corner)] if radix == 4 else []
    stacked = query.reshape(-1, HEADS, HEAD_DIM).transpose(1, 0, 2).reshape(-1, HEAD_DIM)
    w_gate, stacked, k_cache, v_cache = keep(w_gate, stacked, k_cache, v_cache)
    base = gather(block, outer, w_gate, order=[2, 1, 3])
    sides = [2, 1] if radix == 4 else [1]
    chunks = [exchange(base, stride * k) for k in sides]
    *sums, w_up = attend(after(stacked, base), k_cache, v_cache, cache_len, levels, w_up)
    weights = (w_gate, w_up, w_down)
    last_chunk = [gather(a, outer, sums[0], flops=25 * 10**8, order=[2, 3, 1]) for a in across]
    count = len(sides)
    chunks = lax.optimization_barrier((*chunks, sums[0]))[:count]
    others = [exchange(c, 1) for c in (*chunks, base, *last_chunk)]
    chunks = lax.optimization_barrier((*chunks, *last_chunk))[:count]
    near, far = apply_expert(chunks, others[:count], sides, sums, weights)
    pieces = summed([near, exchange(far, 1)], [rows] * count, width, own)
    base = after(base, near)
    near, far = apply_expert([base, *last_chunk], others[count:], [0] + [3] * len(across), sums, weights)
    total, *corner_pieces = summed([near, exchange(far, 1)], [rows] + cut * len(across), width, own)
    parts = [total] + [exchange(piece, stride * k) for piece, k in zip(pieces, sides)]
    if across:
        corner_parts = scatter(corner_pieces, outer, width, own, [2, 3, 1])
    pieces = summed(parts, cut, width, own)
    last = scatter(pieces, outer, width, own, [2, 3, 1])
    if across:
        corner_parts = lax.optimization_barrier((*corner_parts, pieces[0]))[:-1]
        (corner_sum,) = summed(corner_parts, [rows_dev], width, own)
        last.append(exchange(corner_sum, corner))
    if across:
        (most,) = summed(last[:-1], [rows_dev], width, own, flops=10**9)
        last = [most, last[-1]]
    return tuple(summed(last, [], width, own, last=True))


def solution(mesh):
    in_specs = (
        P(("groups", "ffn"), None),
        P(),
        P(("groups", "ffn"), None),
        P(("groups", "ffn"), None),
        P(None, "ffn"),
        P(None, "ffn"),
        P("ffn", None),
        P("groups", None),
        P("groups", "ffn", None),
        P("groups", "ffn", None),
        P("groups"),
    )
    out_specs = (P(("groups", "ffn"), None), P("groups", "ffn"))
    return jax.shard_map(
        per_device, mesh=mesh, in_specs=in_specs, out_specs=out_specs, check_vma=False
    )
```

```python
import functools

import jax
import jax.numpy as jnp
from jax import lax
from jax.experimental import pallas as pl
from jax.experimental.pallas import tpu as pltpu
from jax.sharding import PartitionSpec as P

HEADS = 64
KV_HEADS = 4
HEAD_DIM = 128
LANES = 128
STRIPS = 4
VMEM = pl.BlockSpec(memory_space=pltpu.VMEM)
SMEM = pl.BlockSpec(memory_space=pltpu.SMEM)
HBM = pl.BlockSpec(memory_space=pltpu.HBM)


def levels_of(devices):
    levels, stride = [], 2
    while stride < devices:
        radix = 4 if devices // stride >= 4 else 2
        levels.append((stride, radix))
        stride *= radix
    return levels


def offsets_of(levels):
    offsets = [0]
    for stride, radix in reversed(levels):
        offsets = [stride * k ^ low for k in range(radix) for low in offsets]
    return offsets


def exchange(value, distance):
    size = lax.axis_size("ffn")
    return lax.ppermute(value, "ffn", [(i, i ^ distance) for i in range(size)])


def after(value, *others):
    return lax.optimization_barrier((value, *others))[0]


def call(body, out_shape, args, in_specs=None, scratch=(), flops=1, nbytes=1, mib=16):
    return pl.pallas_call(
        body,
        out_shape=out_shape,
        in_specs=in_specs or [VMEM] * len(args),
        out_specs=jax.tree.map(lambda _: VMEM, out_shape),
        scratch_shapes=list(scratch),
        compiler_params=pltpu.CompilerParams(vmem_limit_bytes=mib * 2**20),
        cost_estimate=pl.CostEstimate(flops=flops, bytes_accessed=nbytes, transcendentals=0),
    )(*args)


def in_hbm(*arrays):
    return [pltpu.with_memory_space_constraint(array, pltpu.HBM) for array in arrays]


def fetched(count):
    return pltpu.SemaphoreType.DMA((count,))


def fetch(sources, targets, sems):
    copies = [pltpu.make_async_copy(s, t, sems.at[i]) for i, (s, t) in enumerate(zip(sources, targets))]
    for copy in copies:
        copy.start()
    return copies


def strips(ref, count):
    rows = ref.shape[0] // count
    return [ref.at[pl.ds(first * rows, rows)] for first in range(count)]


def payload_kernel(
    experts, tokens_hbm, gain_hbm, routes_hbm, scores_hbm, out_ref, tokens_ref, gain_ref, routes_ref, scores_ref, sems
):
    copies = fetch(
        [tokens_hbm, gain_hbm, routes_hbm, scores_hbm], [tokens_ref, gain_ref, routes_ref, scores_ref], sems
    )
    for copy in copies:
        copy.wait()
    features = tokens_ref[...].astype(jnp.float32)
    width = features.shape[1]
    mean_square = jnp.mean(features * features, axis=-1, keepdims=True)
    normed = features * lax.rsqrt(mean_square + 1e-06) * gain_ref[...]
    scores = scores_ref[...]
    share = scores / jnp.sum(scores, axis=-1, keepdims=True)
    extra = out_ref.shape[1] - width
    lane = lax.broadcasted_iota(jnp.int32, (features.shape[0], extra), 1)
    routes = routes_ref[...]
    gates = jnp.zeros(lane.shape, jnp.float32)
    for choice in range(routes.shape[1]):
        gates += jnp.where(
            routes[:, choice : choice + 1] == lane % experts, share[:, choice : choice + 1], 0.0
        )
    high = gates.astype(jnp.bfloat16).astype(jnp.float32)
    coded = jnp.where(lane < experts, high, jnp.where(lane < 2 * experts, gates - high, 0.0))
    out_ref[:, :width] = normed.astype(jnp.bfloat16)
    out_ref[:, width:] = coded.astype(jnp.bfloat16)


def coded_log(value):
    high = value.astype(jnp.bfloat16).astype(jnp.float32)
    middle = (value - high).astype(jnp.bfloat16).astype(jnp.float32)
    return [high, middle, value - high - middle]


def keep_kernel(cuts, *refs):
    count = len(cuts)
    sources = sum([strips(ref, cut) for ref, cut in zip(refs, cuts)], [])
    targets = sum([strips(ref, cut) for ref, cut in zip(refs[count:], cuts)], [])
    copies = fetch(sources, targets, refs[2 * count])
    for copy in copies:
        copy.wait()


def keep(*arrays):
    cuts = [STRIPS if a.size >= 2**20 else 1 for a in arrays]
    return call(
        functools.partial(keep_kernel, cuts),
        [pltpu.VMEM(a.shape, a.dtype) for a in arrays],
        in_hbm(*arrays),
        in_specs=[HBM] * len(arrays),
        scratch=[fetched(sum(cuts))],
        flops=4 * 10**9,
    )


def attention_kernel(own, offsets, *refs):
    length_hbm, weight_hbm, query_ref, key_ref, value_ref, near_ref, far_ref, weight_out = refs[:8]
    length_ref, wide_ref, mean_ref, logs_ref, dest_ref, sems = refs[8:]
    sources = [length_hbm, *strips(weight_hbm, STRIPS)]
    copies = fetch(sources, [length_ref, *strips(weight_out, STRIPS)], sems)
    me = lax.axis_index("ffn")
    rows, seg_len, _ = key_ref.shape
    per_group = HEADS // KV_HEADS
    place = lax.broadcasted_iota(jnp.int32, (KV_HEADS * per_group, seg_len), 1) + me * seg_len
    per_dest = max(1, own // HEAD_DIM)
    extra = near_ref.shape[1]
    lane = lax.broadcasted_iota(jnp.int32, (rows, extra), 1)
    wide_ref[...] = query_ref[...].astype(jnp.float32)
    pairs = [(row, group) for row in range(rows) for group in range(KV_HEADS)]
    heads = [pl.ds(group * per_group * rows + row, per_group, rows) for row, group in pairs]
    cols = [slice(group * HEAD_DIM, (group + 1) * HEAD_DIM) for _, group in pairs]
    queries = [wide_ref[at, :].astype(jnp.bfloat16) for at in heads]
    scores = [
        lax.dot_general(q, key_ref[row, :, c], (((1,), (1,)), ((), ())), preferred_element_type=jnp.float32)
        for q, c, (row, _) in zip(queries, cols, pairs)
    ]
    scores = jnp.stack(scores).reshape(rows, KV_HEADS * per_group, seg_len) * HEAD_DIM ** (-0.5)
    copies[0].wait()
    usable = jnp.stack([place < length_ref[row] for row in range(rows)])
    peak = jnp.max(jnp.where(usable, scores, -1e30), axis=-1, keepdims=True)
    weights = jnp.where(usable, jnp.exp(scores - peak), 0.0).astype(jnp.bfloat16)
    total = jnp.sum(weights.astype(jnp.float32), axis=-1, keepdims=True)
    some = total > 0.0
    safe = jnp.where(some, total, 1.0)
    logs = jnp.where(some, peak + jnp.log(safe), -1e30)
    parts = [slice(group * per_group, (group + 1) * per_group) for _, group in pairs]
    accs = [
        jnp.dot(weights[row, part], value_ref[row, :, c], preferred_element_type=jnp.float32)
        for part, c, (row, _) in zip(parts, cols, pairs)
    ]
    for acc, part, at, (row, _) in zip(accs, parts, heads, pairs):
        mean_ref[at, :] = acc / safe[row, part]
        logs_ref[at, :] = jnp.broadcast_to(logs[row, part], acc.shape)
    if own >= HEAD_DIM:
        for dest in range(HEADS // per_dest):
            stats = jnp.zeros((rows, extra - own), jnp.float32)
            for slot in range(per_dest):
                at = slice((dest * per_dest + slot) * rows, (dest * per_dest + slot + 1) * rows)
                dest_ref[dest, :, slot * HEAD_DIM : (slot + 1) * HEAD_DIM] = mean_ref[at, :]
                for number, part in enumerate(coded_log(logs_ref[at, :1])):
                    stats = jnp.where(lane[:, own:] == own + 3 * slot + number, part, stats)
            dest_ref[dest, :, own:] = stats
    else:
        for head in range(HEADS):
            mean, logs = mean_ref[head * rows : (head + 1) * rows, :], logs_ref[head * rows : (head + 1) * rows, :1]
            for half in range(HEAD_DIM // own):
                moved = mean if half == 0 else pltpu.roll(mean, HEAD_DIM - half * own, 1)
                block = jnp.where(lane < own, moved, 0.0)
                for number, part in enumerate(coded_log(logs)):
                    block = jnp.where(lane == own + number, part, block)
                dest_ref[head * (HEAD_DIM // own) + half] = block
    for out_ref, core in ((near_ref, 0), (far_ref, 1)):
        for first in range(0, len(offsets), 2):
            pair = [dest_ref[me ^ (offset ^ core)] for offset in offsets[first : first + 2]]
            out_ref[first * rows : (first + 2) * rows] = jnp.concatenate(pair, axis=0).astype(jnp.bfloat16)
    for copy in copies[1:]:
        copy.wait()


def attend(stacked, k_cache, v_cache, cache_len, levels, weight):
    devices = lax.axis_size("ffn")
    rows, _, _ = k_cache.shape
    own = HEADS * HEAD_DIM // devices
    extra = -(-(own + 3 * max(1, own // HEAD_DIM)) // LANES) * LANES
    offsets = offsets_of(levels)
    out = jax.ShapeDtypeStruct((len(offsets) * rows, extra), jnp.bfloat16)
    return call(
        functools.partial(attention_kernel, own, offsets),
        [out, out, pltpu.VMEM(weight.shape, weight.dtype)],
        [*in_hbm(cache_len, weight), stacked, k_cache, v_cache],
        in_specs=[HBM] * 2 + [VMEM] * 3,
        scratch=[
            pltpu.SMEM(cache_len.shape, cache_len.dtype),
            *[pltpu.VMEM(stacked.shape, jnp.float32)] * 3,
            pltpu.VMEM((devices, rows, extra), jnp.float32),
            fetched(1 + STRIPS),
        ],
        flops=4 * 10**9,
    )


def expert_kernel(experts, chunks, *refs):
    count = len(chunks)
    same_refs, other_refs, refs = refs[:count], refs[count : 2 * count], refs[2 * count :]
    near_ref, far_ref, gate_ref, up_ref, down_ref, own_out, far_out = refs
    width = gate_ref.shape[0]
    rows = same_refs[0].shape[0]
    coded = jnp.concatenate([r[:, width:] for r in same_refs + other_refs], axis=0).astype(jnp.float32)
    lane = lax.broadcasted_iota(jnp.int32, coded.shape, 1)
    mine = (lane < 2 * experts) & (lane % experts == lax.axis_index("ffn") // 2)
    share = jnp.sum(jnp.where(mine, coded, 0.0), axis=-1, keepdims=True)
    for place, chunk in enumerate(chunks):
        at, here = slice(place * rows, (place + 1) * rows), slice(chunk * rows, (chunk + 1) * rows)
        own_out[at, width:] = near_ref[here]
        far_out[at, width:] = far_ref[here]
    stacked = jnp.concatenate([r[:, :width] for r in same_refs + other_refs], axis=0)
    gate_part = jnp.dot(stacked, gate_ref[...], preferred_element_type=jnp.float32)
    up_part = jnp.dot(stacked, up_ref[...], preferred_element_type=jnp.float32)
    hidden = (gate_part / (1.0 + jnp.exp(-gate_part)) * up_part).astype(jnp.bfloat16)
    step = 1024
    for first in range(0, width, step):
        at = slice(first, first + step)
        part = jnp.dot(hidden, down_ref[:, at], preferred_element_type=jnp.float32)
        part = (part * share).astype(jnp.bfloat16)
        own_out[:, at] = part[: count * rows]
        far_out[:, at] = part[count * rows :]


def apply_expert(same, other, chunks, sums, weights):
    rows = same[0].shape[0]
    width, hidden = weights[0].shape
    devices = lax.axis_size("ffn")
    shape = jax.ShapeDtypeStruct((len(same) * rows, width + sums[0].shape[1]), jnp.bfloat16)
    args = [*same, *other, *sums, *weights]
    return call(
        functools.partial(expert_kernel, devices // 2, chunks),
        [shape, shape],
        args,
        flops=4 * 10**9,
        nbytes=2 * 3 * width * hidden,
        mib=8 + sum(2 * a.size for a in args) // 2**20,
    )


def merged(own, parts):
    heads, piece = max(1, own // HEAD_DIM), min(own, HEAD_DIM)
    lane = lax.broadcasted_iota(jnp.int32, parts[0].shape, 1)
    result = jnp.zeros(parts[0].shape, jnp.float32)
    for head in range(heads):
        stat = (lane >= own + 3 * head) & (lane < own + 3 * head + 3)
        logs = [jnp.sum(jnp.where(stat, p, 0.0), axis=-1, keepdims=True) for p in parts]
        top = functools.reduce(jnp.maximum, logs)
        scales = [jnp.exp(log - top) for log in logs]
        total = sum(scales)
        mean = sum(p * s for p, s in zip(parts, scales)) / total
        result = jnp.where((lane >= head * piece) & (lane < (head + 1) * piece), mean, result)
        for place, part in enumerate(coded_log(top + jnp.log(total))):
            result = jnp.where(lane == own + 3 * head + place, part, result)
    return result


def sum_kernel(count, width, own, last, *refs):
    refs, outs = refs[:count], refs[count:]
    rows = refs[0].shape[0]
    step = min(rows, 16)
    for first in range(0, rows, step):
        at = slice(first, first + step)
        total = sum(ref[at, :width].astype(jnp.float32) for ref in refs)
        mean = merged(own, [ref[at, width:].astype(jnp.float32) for ref in refs])
        if last:
            outs[0][at] = total.astype(jnp.bfloat16)
            outs[1][at] = mean[:, :own].astype(jnp.bfloat16)
            continue
        start = 0
        for out_ref in outs:
            low, high = max(first, start), min(first + step, start + out_ref.shape[0])
            if low < high:
                here, part = slice(low - start, high - start), slice(low - first, high - first)
                out_ref[here, :width] = total[part].astype(jnp.bfloat16)
                out_ref[here, width:] = mean[part].astype(jnp.bfloat16)
            start += out_ref.shape[0]


def summed(parts, sizes, width, own, last=False, flops=1):
    rows, whole = parts[0].shape
    if last:
        shapes = [jax.ShapeDtypeStruct((rows, n), jnp.bfloat16) for n in (width, own)]
    else:
        shapes = [jax.ShapeDtypeStruct((n, whole), jnp.bfloat16) for n in sizes]
    return call(functools.partial(sum_kernel, len(parts), width, own, last), shapes, parts, flops=flops)


def stack_kernel(places, *refs):
    blocks = dict(zip(places, refs))
    stacked = jnp.concatenate([blocks[k][...].astype(jnp.float32) for k in range(len(places))], axis=0)
    refs[-1][...] = stacked.astype(jnp.bfloat16)


def start_order(radix, order):
    return order if radix == 4 else [1]


def gather(block, levels, *ready, flops=1, order=[2, 3, 1]):
    for stride, radix in reversed(levels):
        order = start_order(radix, order)
        arrived = [exchange(block, stride * k) for k in order]
        if ready:
            arrived = lax.optimization_barrier((*arrived, *ready))[: len(order)]
        rows, width = block.shape
        block = call(
            functools.partial(stack_kernel, [0] + order),
            jax.ShapeDtypeStruct((radix * rows, width), jnp.bfloat16),
            [block, *arrived],
            flops=flops,
        )
    return block


def scatter(pieces, levels, width, own, order=[2, 3, 1]):
    stride, radix = levels[0]
    parts = [pieces[0]] + [exchange(pieces[k], stride * k) for k in start_order(radix, order)]
    if len(levels) == 1:
        return parts
    rows = parts[0].shape[0] // levels[1][1]
    return scatter(summed(parts, [rows] * levels[1][1], width, own), levels[1:], width, own, order)


def per_device(
    tokens, norm_gain, routes, gate_scores, w_gate, w_up, w_down, query, k_cache, v_cache, cache_len
):
    rows_dev, width = tokens.shape
    devices = lax.axis_size("ffn")
    experts = devices // 2
    levels = levels_of(devices)
    own = query.shape[1] // devices
    extra = -(-2 * experts // LANES) * LANES
    block = call(
        functools.partial(payload_kernel, experts),
        jax.ShapeDtypeStruct((rows_dev, width + extra), jnp.bfloat16),
        in_hbm(tokens, norm_gain[None], routes, gate_scores),
        in_specs=[HBM] * 4,
        scratch=[pltpu.VMEM(a.shape, a.dtype) for a in (tokens, norm_gain[None], routes, gate_scores)]
        + [fetched(4)],
    )
    (stride, radix), *outer = levels
    corner = 3 * stride
    rows = rows_dev * (devices // (2 * radix))
    cut = [rows // outer[0][1]] * outer[0][1]
    across = [exchange(block, corner)] if radix == 4 else []
    stacked = query.reshape(-1, HEADS, HEAD_DIM).transpose(1, 0, 2).reshape(-1, HEAD_DIM)
    w_gate, stacked, k_cache, v_cache = keep(w_gate, stacked, k_cache, v_cache)
    base = gather(block, outer, w_gate, order=[2, 1, 3])
    sides = [2, 1] if radix == 4 else [1]
    chunks = [exchange(base, stride * k) for k in sides]
    *sums, w_up = attend(after(stacked, base), k_cache, v_cache, cache_len, levels, w_up)
    weights = (w_gate, w_up, w_down)
    last_chunk = [gather(a, outer, sums[0], flops=25 * 10**8, order=[2, 3, 1]) for a in across]
    count = len(sides)
    chunks = lax.optimization_barrier((*chunks, sums[0]))[:count]
    others = [exchange(c, 1) for c in (*chunks, base, *last_chunk)]
    chunks = lax.optimization_barrier((*chunks, *last_chunk))[:count]
    near, far = apply_expert(chunks, others[:count], sides, sums, weights)
    pieces = summed([near, exchange(far, 1)], [rows] * count, width, own)
    base = after(base, near)
    near, far = apply_expert([base, *last_chunk], others[count:], [0] + [3] * len(across), sums, weights)
    total, *corner_pieces = summed([near, exchange(far, 1)], [rows] + cut * len(across), width, own)
    parts = [total] + [exchange(piece, stride * k) for piece, k in list(zip(pieces, sides))[::-1]]
    if across:
        corner_parts = scatter(corner_pieces, outer, width, own, [2, 3, 1])
    pieces = summed(parts, cut, width, own)
    last = scatter(pieces, outer, width, own, [2, 3, 1])
    if across:
        corner_parts = lax.optimization_barrier((*corner_parts, pieces[0]))[:-1]
        (corner_sum,) = summed(corner_parts, [rows_dev], width, own)
        last.append(exchange(corner_sum, corner))
    if across:
        (most,) = summed(last[:-1], [rows_dev], width, own, flops=10**9)
        last = [most, last[-1]]
    return tuple(summed(last, [], width, own, last=True))


def solution(mesh):
    in_specs = (
        P(("groups", "ffn"), None),
        P(),
        P(("groups", "ffn"), None),
        P(("groups", "ffn"), None),
        P(None, "ffn"),
        P(None, "ffn"),
        P("ffn", None),
        P("groups", None),
        P("groups", "ffn", None),
        P("groups", "ffn", None),
        P("groups"),
    )
    out_specs = (P(("groups", "ffn"), None), P("groups", "ffn"))
    return jax.shard_map(
        per_device, mesh=mesh, in_specs=in_specs, out_specs=out_specs, check_vma=False
    )
```
